32 devices in a mesh: dp: 8 (over y, x, core), tensor: 4 (over z).
Axes of the slice: x: 2, y: 2, z: 4, core: 2. Of those that a mesh axis runs over, the one named last changes fastest.
Arguments:
- block_input: bfloat16 [2048, 4, 1536], P(('dp', 'tensor')), may hold values from -6 to 6
- out_grad: bfloat16 [2048, 4, 1536], P(('dp', 'tensor')), may hold values from -6 to 6
- lengths: int32 [4], replicated, may hold values from 512 to 2048, as said below
- routes: int32 [2048, 4, 6], P('dp'), may hold values from 0 to 15, all different within a row; in each aligned block of 1024 rows (0 to 1023, 1024 to 2047, ..., all dimensions but the last counted through in order) at most 512 rows name the same one
- norm1_gain: bfloat16 [1536], P('dp'), may hold values from 0.25 to 1.75
- w_zx: bfloat16 [1536, 2, 3072], P('dp', None, 'tensor'), may hold values from -0.15625 to 0.15625
- w_bc: bfloat16 [1536, 256], P('dp'), may hold values from -0.15625 to 0.15625
- w_dt: bfloat16 [1536, 48], P('dp', 'tensor'), may hold values from -0.15625 to 0.15625
- conv_x: float32 [5, 3072], P(None, 'tensor'), may hold values from -3 to 3
- conv_bc: float32 [5, 256], replicated, may hold values from -3 to 3
- head_params: float32 [3, 48], P(None, 'tensor'), may hold values from -11 to 2
- gate_gain: float32 [3072], P('tensor'), may hold values from 0.25 to 1.75
- w_out: bfloat16 [3072, 1536], P('tensor', 'dp'), may hold values from -0.109375 to 0.109375
- norm2_gain: bfloat16 [1536], P('dp'), may hold values from 0.25 to 1.75
- w_router: bfloat16 [1536, 16], P('dp'), may hold values from -0.078125 to 0.078125
- w_gu: bfloat16 [16, 1536, 2, 512], P(None, 'dp', None, 'tensor'), may hold values from -0.15625 to 0.15625
- w_dn: bfloat16 [16, 512, 1536], P(None, 'tensor', 'dp'), may hold values from -0.5 to 0.5
- s_gu: bfloat16 [1536, 2, 1024], P('dp', None, 'tensor'), may hold values from -0.15625 to 0.15625
- s_dn: bfloat16 [1024, 1536], P('tensor', 'dp'), may hold values from -0.1875 to 0.1875
Outputs:
- output: bfloat16 [2048, 4, 1536], P(('dp', 'tensor'))
- input_grad: bfloat16 [2048, 4, 1536], P(('dp', 'tensor'))
- norm1_gain_grad: float32 [1536], P(('dp', 'tensor'))
- w_zx_grad: float32 [1536, 2, 3072], P('dp', None, 'tensor')
- w_bc_grad: float32 [1536, 256], P(('dp', 'tensor'))
- w_dt_grad: float32 [1536, 48], P('dp', 'tensor')
- conv_x_grad: float32 [5, 3072], P(None, ('dp', 'tensor'))
- conv_bc_grad: float32 [5, 256], P(None, ('dp', 'tensor'))
- head_params_grad: float32 [3, 48], replicated
- gate_gain_grad: float32 [3072], P(('dp', 'tensor'))
- w_out_grad: float32 [3072, 1536], P('tensor', 'dp')
- norm2_gain_grad: float32 [1536], P(('dp', 'tensor'))
- w_router_grad: float32 [1536, 16], P(('dp', 'tensor'))
- w_gu_grad: float32 [16, 1536, 2, 512], P(None, 'dp', None, 'tensor')
- w_dn_grad: float32 [16, 512, 1536], P(None, 'tensor', 'dp')
- s_gu_grad: float32 [1536, 2, 1024], P('dp', None, 'tensor')
- s_dn_grad: float32 [1024, 1536], P('tensor', 'dp')
- stats: float32 [3], replicated
The draws below stay inside these ranges and needn't reach their ends.
Inputs may be any that keep to these rules, and one draw needn't show every extreme that they name: `lengths`: each slot has between a quarter of 2048 and 2048 valid positions; one slot is full. `routes`: within the rows of one index of dp (aligned blocks of 1024 rows, positions before slots) no expert is named by more than 512 rows, and some expert reaches that.
All inputs are finite; a program needn't handle non-finite values.
Results may differ from the reference program's by a relative error of at most 0.015.
Values may be sent and summed in bfloat16 or wider, within the bound.
No kernel may reach another device: no remote copies, remote signals or barrier semaphores. Data moves between devices by JAX's collectives and lax.ppermute only.
A program may use at most 448 MiB of HBM per device.

```python
import math
import jax
import jax.numpy as jnp
import numpy as np
from jax import lax

D_MODEL = 1536
HEAD_COUNT = 48
HEAD_DIM = 64
STATE_DIM = 128
CONV_WIDTH = 4
EXPERT_FF = 512
SHARED_FF = 1024
TOP_K = 6
EXPERTS = 16
SLOT_COUNT = 4
PIECE_LEN = 256
INNER_DIM = 3072
SLOT_LEN = 2048
CAPACITY = 512


def draw_lengths(key, part):
    slot_lengths = jax.random.randint(jax.random.fold_in(key, 11), (SLOT_COUNT,), SLOT_LEN // 4, SLOT_LEN + 1)
    full_slot = jax.random.randint(jax.random.fold_in(key, 12), (), 0, SLOT_COUNT)
    slot_lengths = slot_lengths.at[full_slot].set(SLOT_LEN)
    return slot_lengths.astype(jnp.int32)


def draw_head_params(key, part):
    slow_tenths = 5
    slow_heads = jax.random.randint(jax.random.fold_in(key, 21), (HEAD_COUNT,), 0, 10) < slow_tenths
    slow_log = jax.random.uniform(jax.random.fold_in(key, 22), (HEAD_COUNT,), jnp.float32, jnp.log(0.3 / SLOT_LEN), jnp.log(2.0 / SLOT_LEN))
    fast_log = jax.random.uniform(jax.random.fold_in(key, 23), (HEAD_COUNT,), jnp.float32, jnp.log(0.01), jnp.log(0.05))
    log_rate = jnp.where(slow_heads, slow_log, fast_log)
    step_bias = jax.random.uniform(jax.random.fold_in(key, 24), (HEAD_COUNT,), jnp.float32, -1.0, 1.0)
    skip_weight = jax.random.uniform(jax.random.fold_in(key, 25), (HEAD_COUNT,), jnp.float32, 0.3, 1.5)
    return jnp.stack([log_rate, step_bias, skip_weight]).astype(jnp.float32)


def shard_levels(key, shape, shards, smallest, high):
    gain, own = 1.0, jax.random.fold_in(key, 6)
    for dim, shards_of in shards:
        draws = jnp.exp(jax.random.uniform(jax.random.fold_in(own, dim), (shards_of,), jnp.float32, smallest / len(shards), high / len(shards)))
        gain = gain * jnp.repeat(draws, shape[dim] // shards_of).reshape([-1 if axis == dim else 1 for axis in range(len(shape))])
    return gain


def assign_block(stream_key, own, number, rows, number_of, top, bound, lean):
    ranking = jax.random.permutation(stream_key, number_of)
    crowded, usual = load_shares(number_of, rows * top, bound, lean, True), load_shares(number_of, rows * top, bound, lean, False)
    places = jnp.arange(number_of)

    def named(sizes, offset_by):
        used = int((sizes > 0).sum())
        fixed = max(1, used // 4)
        shifted = fixed + (places - fixed + offset_by * (used - fixed)) % max(1, number_of - fixed)
        return jnp.zeros((number_of,), jnp.int32).at[ranking[jnp.where(places < fixed, places, shifted)]].set(jnp.asarray(sizes, jnp.int32))

    sizes = jnp.where(number % 4 == 0, named(crowded, number // 4), named(usual, number - number // 4 - 1))
    mixed = jax.random.permutation(jax.random.fold_in(own, 3), number_of)
    giver, receiver = mixed[0:number_of // 2 * 2:2], mixed[1:number_of // 2 * 2:2]
    room = jnp.minimum(sizes[giver] - 1, bound - sizes[receiver]) // 2
    room = jnp.where((giver == ranking[0]) | (receiver == ranking[0]) | (sizes[receiver] == 0), 0, jnp.maximum(room, 0))
    shifted = jax.random.randint(jax.random.fold_in(own, 4), (number_of // 2,), 0, 1 << 20) % (room + 1)
    sizes = sizes.at[giver].add(-shifted).at[receiver].add(shifted)
    labels = jnp.searchsorted(jnp.cumsum(sizes), jnp.arange(rows * top), side="right").astype(jnp.int32)
    listing = labels.reshape(top, rows).T
    listing = listing[jax.random.permutation(jax.random.fold_in(own, 1), rows)]
    offset_by = jax.random.randint(jax.random.fold_in(own, 2), (rows, 1), 0, top)
    return jnp.take_along_axis(listing, (jnp.arange(top)[None, :] + offset_by) % top, axis=1)


def load_shares(amount, total, most, skew, full):
    weights = [(1 << 20) // math.isqrt(standing ** skew) + 1 for standing in range(1, amount + 1)]
    largest = most if full else min(most, max(-(-total // amount), total * weights[0] // sum(weights)))
    least = 1 if total - largest >= amount - 1 else 0
    given, rest = [largest] + [least] * (amount - 1), total - largest - least * (amount - 1)
    while rest > 0:
        candidates = [i for i in range(1, amount) if given[i] < largest] or [i for i in range(1, amount) if given[i] < most]
        mass, remaining = sum([weights[i] for i in candidates]), rest
        for i in candidates:
            addition = min(most - given[i], max(1, remaining * weights[i] // mass), rest)
            given[i] = given[i] + addition
            rest = rest - addition
    return np.array(given)


def centred(stream_key, dims, deviation, limit, cuts=(), kind=jnp.bfloat16):
    drawn = deviation * jax.random.normal(stream_key, dims, jnp.float32)
    if cuts:
        drawn = drawn * shard_levels(stream_key, dims, cuts, -0.22, 0.18)
    return jnp.clip(drawn, -limit, limit).astype(kind)


def setup_inputs(seed: int = 0) -> dict:
    key_list = jax.random.split(jax.random.key(seed), 20)
    block_input = centred(key_list[0], (SLOT_LEN, SLOT_COUNT, D_MODEL), 1.0, 6.0, ((0, 32),))
    out_grad = centred(key_list[1], (SLOT_LEN, SLOT_COUNT, D_MODEL), 1.0, 6.0, ((0, 32),))
    lengths = draw_lengths(jax.random.fold_in(key_list[19], 71), 0)
    routes_keys = jax.random.split(jax.random.fold_in(key_list[3], 1), SLOT_LEN * SLOT_COUNT // (PIECE_LEN * SLOT_COUNT))
    routes_turns = jax.random.permutation(jax.random.fold_in(key_list[3], 3), SLOT_LEN * SLOT_COUNT // (PIECE_LEN * SLOT_COUNT))
    routes = jax.vmap(lambda own, number: assign_block(jax.random.fold_in(key_list[3], 2), own, number, PIECE_LEN * SLOT_COUNT, EXPERTS, TOP_K, CAPACITY, 1))(routes_keys, routes_turns).reshape((SLOT_LEN, SLOT_COUNT, TOP_K))
    norm1_gain = jnp.clip(1.0 + 0.15 * jax.random.normal(key_list[4], (D_MODEL,), jnp.float32), 0.25, 1.75).astype(jnp.bfloat16)
    w_zx = centred(key_list[5], (D_MODEL, 2, INNER_DIM), D_MODEL ** -0.5, 0.15625, ((0, 8), (2, 4)))
    w_bc = centred(key_list[6], (D_MODEL, 2 * STATE_DIM), D_MODEL ** -0.5, 0.15625, ((0, 8),))
    w_dt = centred(key_list[7], (D_MODEL, HEAD_COUNT), D_MODEL ** -0.5, 0.15625, ((0, 8), (1, 4)))
    conv_x = centred(key_list[8], (CONV_WIDTH + 1, INNER_DIM), 0.5, 3.0, ((1, 4),), jnp.float32)
    conv_bc = centred(key_list[9], (CONV_WIDTH + 1, 2 * STATE_DIM), 0.5, 3.0, (), jnp.float32)
    head_params = draw_head_params(jax.random.fold_in(key_list[19], 71), 0)
    gate_gain = jnp.clip(1.0 + 0.15 * jax.random.normal(key_list[11], (INNER_DIM,), jnp.float32), 0.25, 1.75)
    w_out = centred(key_list[12], (INNER_DIM, D_MODEL), INNER_DIM ** -0.5, 0.109375, ((0, 4), (1, 8)))
    norm2_gain = jnp.clip(1.0 + 0.15 * jax.random.normal(key_list[13], (D_MODEL,), jnp.float32), 0.25, 1.75).astype(jnp.bfloat16)
    w_router = centred(key_list[14], (D_MODEL, EXPERTS), (4 * D_MODEL) ** -0.5, 0.078125, ((0, 8),))
    w_gu = centred(key_list[15], (EXPERTS, D_MODEL, 2, EXPERT_FF), D_MODEL ** -0.5, 0.15625, ((1, 8), (3, 4)))
    w_dn = centred(key_list[16], (EXPERTS, EXPERT_FF, D_MODEL), (EXPERT_FF // 4) ** -0.5, 0.5, ((1, 4), (2, 8)))
    s_gu = centred(key_list[17], (D_MODEL, 2, SHARED_FF), D_MODEL ** -0.5, 0.15625, ((0, 8), (2, 4)))
    s_dn = centred(key_list[18], (SHARED_FF, D_MODEL), SHARED_FF ** -0.5, 0.1875, ((0, 4), (1, 8)))
    return dict(block_input=block_input, out_grad=out_grad, lengths=lengths, routes=routes, norm1_gain=norm1_gain, w_zx=w_zx, w_bc=w_bc, w_dt=w_dt, conv_x=conv_x, conv_bc=conv_bc, head_params=head_params, gate_gain=gate_gain, w_out=w_out, norm2_gain=norm2_gain, w_router=w_router, w_gu=w_gu, w_dn=w_dn, s_gu=s_gu, s_dn=s_dn)


norm_eps = 1e-05
highest = lax.Precision.HIGHEST

@jax.custom_vjp
def low(v):
    return lax.optimization_barrier(v.astype(jnp.bfloat16)).astype(jnp.float32)

@jax.custom_vjp
def low_back(v):
    return v

def low_keep(v):
    return (low(v), None)

def low_pass(kept, grad):
    return (grad,)

def back_keep(v):
    return (v, None)

def back_low(kept, grad):
    return (low(grad),)
low.defvjp(low_keep, low_pass)
low_back.defvjp(back_keep, back_low)

def rms_scale(values, gain_vec):
    return values * lax.rsqrt(lax.optimization_barrier(jnp.mean(values * values, axis=-1, keepdims=True)) + norm_eps) * gain_vec

def conv_pre_act(padded, conv_weights, length):
    tap_count = conv_weights.shape[0] - 1
    summed = conv_weights[tap_count] + conv_weights[0] * padded[0:length]
    for offset in range(1, tap_count):
        summed = summed + conv_weights[offset] * padded[offset:offset + length]
    return summed

def causal_conv(values, conv_weights):
    rim_width = conv_weights.shape[0] - 2
    padded = jnp.concatenate([jnp.zeros((rim_width,) + values.shape[1:], jnp.float32), values], axis=0)
    return conv_pre_act(padded, conv_weights, values.shape[0])

def piece_terms(x_heads, step_size, decay_rate, write_vec, read_vec):
    log_sum = jnp.cumsum(-step_size * decay_rate, axis=0)
    extent = x_heads.shape[0]
    causal_mask = jnp.arange(extent)[:, None] >= jnp.arange(extent)[None, :]
    gap_log = log_sum[:, None] - log_sum[None, :]
    decays = jnp.exp(jnp.where(causal_mask[:, :, None, None], gap_log, -jnp.inf))
    scores = jnp.einsum('tsn,jsn->tjs', read_vec, write_vec, precision=highest)
    mixing = decays * scores[..., None] * step_size[None]
    y_inner = jnp.einsum('tjsh,jshp->tshp', mixing, x_heads, precision=highest)
    tail_decay = jnp.exp(log_sum[-1][None] - log_sum) * step_size
    s_local = jnp.einsum('jsh,jshp,jsn->shpn', tail_decay, x_heads, write_vec, precision=highest)
    return (y_inner, s_local, log_sum)

def state_terms(log_sum, read_vec, entering):
    y_state = jnp.einsum('tsh,tsn,shpn->tshp', jnp.exp(log_sum), read_vec, entering, precision=highest)
    leaving = jnp.exp(log_sum[-1])[..., None, None] * entering
    return (y_state, leaving)

def whole_scan(x_heads, step_size, decay_rate, write_vec, read_vec):
    blocks = x_heads.shape[0] // PIECE_LEN

    def advance(carried, pieces):
        x_part, step_part, write_part, read_part = pieces
        y_inner, s_local, log_sum = piece_terms(x_part, step_part, decay_rate, write_part, read_part)
        y_state, leaving = state_terms(log_sum, read_part, carried)
        return (leaving + s_local, y_inner + y_state)

    def to_blocks(values):
        return values.reshape((blocks, PIECE_LEN) + values.shape[1:])
    initial = jnp.zeros((x_heads.shape[1], x_heads.shape[2], x_heads.shape[3], write_vec.shape[2]), jnp.float32)
    last_state, outputs = lax.scan(jax.checkpoint(advance), initial, (to_blocks(x_heads), to_blocks(step_size), to_blocks(write_vec), to_blocks(read_vec)))
    return outputs.reshape(x_heads.shape)

def reference(block_input, out_grad, lengths, routes, norm1_gain, w_zx, w_bc, w_dt, conv_x, conv_bc, head_params, gate_gain, w_out, norm2_gain, w_router, w_gu, w_dn, s_gu, s_dn):
    slot_len = block_input.shape[0]
    valid = (jnp.arange(slot_len)[:, None] < lengths[None, :]).astype(jnp.float32)[:, :, None]
    route_hot = (routes[:, :, :, None] == jnp.arange(EXPERTS)[None, None, None, :]).astype(jnp.float32)

    def forward(inputs, gain_one, proj_zx, proj_bc, proj_dt, conv_xw, conv_bcw, head_vals, gate_vec, proj_out, gain_two, proj_router, expert_up, expert_down, shared_up, shared_down):
        n_one = low(rms_scale(inputs, gain_one))
        zx_raw = low_back(jnp.einsum('tsd,dcf->tscf', n_one, proj_zx, precision=highest))
        bc_raw = jnp.einsum('tsd,dn->tsn', n_one, proj_bc, precision=highest)
        dt_raw = low_back(jnp.einsum('tsd,dh->tsh', n_one, proj_dt, precision=highest))
        x_conv = jax.nn.silu(causal_conv(zx_raw[:, :, 1], conv_xw))
        bc_conv = jax.nn.silu(causal_conv(bc_raw, conv_bcw))
        x_heads = x_conv.reshape(slot_len, SLOT_COUNT, HEAD_COUNT, HEAD_DIM)
        step_size = jax.nn.softplus(dt_raw + head_vals[1])
        y_heads = whole_scan(x_heads, step_size, jnp.exp(head_vals[0]), bc_conv[:, :, :STATE_DIM], bc_conv[:, :, STATE_DIM:]) + head_vals[2][:, None] * x_heads
        gated = y_heads.reshape(slot_len, SLOT_COUNT, INNER_DIM) * jax.nn.silu(zx_raw[:, :, 0])
        mixed = low_back(jnp.einsum('tsf,fd->tsd', low(rms_scale(gated, gate_vec)), proj_out, precision=highest))
        resid = inputs + mixed
        n_two = low(rms_scale(resid, gain_two))
        logits = jnp.einsum('tsd,de->tse', n_two, proj_router, precision=highest)
        gates = jax.nn.softmax(lax.optimization_barrier(jnp.sum(route_hot * logits[:, :, None, :], axis=-1)), axis=-1)
        dense_gate = lax.optimization_barrier(jnp.sum(gates[..., None] * route_hot, axis=2)).reshape(-1, EXPERTS)
        flat_in = n_two.reshape(-1, D_MODEL)

        def expert_step(summed, pieces):
            gate_col, up_weight, down_weight = pieces
            hidden = low_back(jnp.einsum('rd,dcf->rcf', flat_in, up_weight, precision=highest))
            expert_act = low(jax.nn.silu(hidden[:, 0]) * hidden[:, 1])
            produced = low_back(jnp.dot(expert_act, down_weight, precision=highest))
            return (summed + gate_col[:, None] * produced, None)
        expert_sum, unused = lax.scan(jax.checkpoint(expert_step), jnp.zeros(flat_in.shape, jnp.float32), (dense_gate.T, expert_up, expert_down))
        shared_hidden = low_back(jnp.einsum('rd,dcf->rcf', flat_in, shared_up, precision=highest))
        shared_act = low(jax.nn.silu(shared_hidden[:, 0]) * shared_hidden[:, 1])
        moe = low_back(expert_sum + jnp.dot(shared_act, shared_down, precision=highest)).reshape(resid.shape)
        return (resid + moe, (mixed, moe))
    floats = [array.astype(jnp.float32) for array in (block_input, norm1_gain, w_zx, w_bc, w_dt, conv_x, conv_bc, head_params, gate_gain, w_out, norm2_gain, w_router, w_gu, w_dn, s_gu, s_dn)]
    output, pullback, extras = jax.vjp(forward, *floats, has_aux=True)
    grads = pullback(out_grad.astype(jnp.float32) * valid)
    mixed, moe = extras
    count = jnp.sum(lengths).astype(jnp.float32) * D_MODEL
    stats = jnp.sqrt(jnp.stack([jnp.sum(valid * output * output), jnp.sum(valid * mixed * mixed), jnp.sum(valid * moe * moe)]) / count)
    return (output.astype(jnp.bfloat16), grads[0].astype(jnp.bfloat16), grads[1], grads[2], grads[3], grads[4], grads[5], grads[6], grads[7], grads[8], grads[9], grads[10], grads[11], grads[12], grads[13], grads[14], grads[15], stats)
```

```python
import functools

import jax
import jax.numpy as jnp
from jax import lax
from jax.experimental import pallas as pl
from jax.experimental.pallas import tpu as pltpu
from jax.sharding import PartitionSpec as P

D_MODEL = 1536
HEAD_COUNT = 48
HEAD_DIM = 64
STATE_DIM = 128
CONV_WIDTH = 4
TOP_K = 6
EXPERTS = 16
SLOT_COUNT = 4
INNER_DIM = 3072
LANES = 128
CHUNKS = 1

norm_eps = 1e-05
highest = lax.Precision.HIGHEST
f32 = jnp.float32
bf16 = jnp.bfloat16


def passed_along(value, axis, steps):
    count = lax.axis_size(axis)
    first, last = (max(0, -steps), min(count, count - steps))
    return lax.ppermute(value, axis, [(source, source + steps) for source in range(first, last)])


def line_gather(value):
    size = lax.axis_size("tensor")
    rights, lefts = [], []
    right, left = value, value
    for _ in range(1, size):
        right = lax.ppermute(right, "tensor", [(a, a + 1) for a in range(size - 1)])
        left = lax.ppermute(left, "tensor", [(a, a - 1) for a in range(1, size)])
        rights.append(right)
        lefts.append(left)
    return [value] + [rights[size - k - 1] + lefts[k - 1] for k in range(1, size)]


def line_scatter(block_of):
    size = lax.axis_size("tensor")
    right, left = None, None
    for k in range(1, size):
        to_right, to_left = block_of(size - k), block_of(k)
        if k > 1:
            to_right = (to_right.astype(f32) + right.astype(f32)).astype(bf16)
            to_left = (to_left.astype(f32) + left.astype(f32)).astype(bf16)
        right = lax.ppermute(to_right, "tensor", [(a, a + 1) for a in range(k)])
        left = lax.ppermute(to_left, "tensor", [(a, a - 1) for a in range(size - k, size)])
    return block_of(0).astype(f32) + right.astype(f32) + left.astype(f32)


def in_order(blocks):
    size = len(blocks)
    own = lax.axis_index("tensor")
    whole = jnp.zeros((size,) + blocks[0].shape, blocks[0].dtype)
    for k in range(size):
        whole = lax.dynamic_update_index_in_dim(whole, blocks[k], (own + k) % size, 0)
    return whole


def by_distance(whole):
    size = whole.shape[0]
    own = lax.axis_index("tensor")
    return lambda k: lax.dynamic_index_in_dim(whole, (own + k) % size, 0, False)


def weight_gather(shard):
    return lax.all_gather(shard, "dp", axis=0, tiled=False)


def weight_scatter(grads):
    return lax.psum_scatter(grads.astype(bf16), "dp", scatter_dimension=0, tiled=False)


def rms_scale(values, gain_vec):
    return (
        values * lax.rsqrt(jnp.mean(values * values, axis=-1, keepdims=True) + norm_eps) * gain_vec
    )


def silu_slope(values):
    logistic = jax.nn.sigmoid(values)
    return logistic * (1.0 + values * (1.0 - logistic))


def dot(a, b, dims, precision=None):
    return lax.dot_general(a, b, (dims, ((), ())), precision=precision, preferred_element_type=f32)


def split_parts(values):
    upper = values.astype(bf16)
    return upper, (values - upper.astype(f32)).astype(bf16)


def dot_split(a, b, dims):
    return dot(a[0], b[0], dims) + (dot(a[0], b[1], dims) + dot(a[1], b[0], dims))


def after(value, *others):
    return lax.optimization_barrier((value,) + others)[0]


NN = ((1,), (0,))
NT = ((1,), (1,))
TN = ((0,), (0,))


def head_spread(inner):
    row = lax.broadcasted_iota(jnp.int32, (LANES, inner), 0)
    col = lax.broadcasted_iota(jnp.int32, (LANES, inner), 1)
    return (col // HEAD_DIM == row).astype(f32)


def head_sums(inner):
    row = lax.broadcasted_iota(jnp.int32, (inner, LANES), 0)
    col = lax.broadcasted_iota(jnp.int32, (inner, LANES), 1)
    return (row // HEAD_DIM == col).astype(f32)


def lower_ones(extent):
    row = lax.broadcasted_iota(jnp.int32, (extent, extent), 0)
    col = lax.broadcasted_iota(jnp.int32, (extent, extent), 1)
    return (row >= col).astype(f32)


def kernel_params(mib):
    return pltpu.CompilerParams(vmem_limit_bytes=mib * 1024 * 1024)


def conv_of(v_ref, halo_ref, cw_ref, padded):
    extent = padded.shape[0] - 8
    width = padded.shape[1]
    padded[0:8, :] = halo_ref[0]
    padded[8:, :] = v_ref[:, 0, :, 0:width].reshape(extent, width)
    summed = cw_ref[CONV_WIDTH : CONV_WIDTH + 1, :]
    for tap in range(CONV_WIDTH):
        summed = summed + cw_ref[tap : tap + 1, :] * padded[5 + tap : 5 + tap + extent, :]
    return summed


def step_sizes(v_ref, hp_ref, conv_width, extent):
    raw = v_ref[:, 0, :, conv_width : conv_width + LANES].reshape(extent, LANES) + hp_ref[1:2, :]
    step = jnp.maximum(raw, 0.0) + jnp.log1p(jnp.exp(-jnp.abs(raw)))
    return raw, step


def enter_kernel(inner, v_ref, halo_ref, cw_ref, hp_ref, xs_ref, rw_ref, dl_ref, s_ref, padded):
    extent = xs_ref.shape[1]
    width = padded.shape[1]
    pre = conv_of(v_ref, halo_ref, cw_ref, padded)
    act = pre * jax.nn.sigmoid(pre)
    xs = act[:, :inner]
    write = act[:, inner : inner + STATE_DIM]
    unused_raw, step = step_sizes(v_ref, hp_ref, width, extent)
    log_sum = dot(lower_ones(extent), -step * jnp.exp(hp_ref[0:1, :]), NN, highest)
    tail = jnp.exp(log_sum[extent - 1 : extent, :] - log_sum) * step
    spread = dot(tail, head_spread(inner), NN, highest)
    xs_ref[0] = xs
    rw_ref[0] = act[:, inner:]
    dl_ref[0, :, 0:LANES] = step
    dl_ref[0, :, LANES:] = log_sum
    s_ref[0] = dot_split(split_parts(xs * spread), split_parts(write), TN)


def mixer_enter(v, halo, cw, hp, inner):
    zs, slots, rows, cols = v.shape
    extent = zs * rows
    width = cw.shape[1]
    heads = inner // HEAD_DIM
    return pl.pallas_call(
        functools.partial(enter_kernel, inner),
        grid=(slots,),
        in_specs=[
            pl.BlockSpec((zs, 1, rows, cols), lambda s: (0, s, 0, 0)),
            pl.BlockSpec((1, 8, width), lambda s: (s, 0, 0)),
            pl.BlockSpec(cw.shape, lambda s: (0, 0)),
            pl.BlockSpec(hp.shape, lambda s: (0, 0)),
        ],
        out_specs=[
            pl.BlockSpec((1, extent, inner), lambda s: (s, 0, 0)),
            pl.BlockSpec((1, extent, 2 * STATE_DIM), lambda s: (s, 0, 0)),
            pl.BlockSpec((1, extent, 2 * LANES), lambda s: (s, 0, 0)),
            pl.BlockSpec((1, inner, STATE_DIM), lambda s: (s, 0, 0)),
        ],
        out_shape=[
            jax.ShapeDtypeStruct((slots, extent, inner), f32),
            jax.ShapeDtypeStruct((slots, extent, 2 * STATE_DIM), f32),
            jax.ShapeDtypeStruct((slots, extent, 2 * LANES), f32),
            jax.ShapeDtypeStruct((slots, inner, STATE_DIM), f32),
        ],
        scratch_shapes=[pltpu.VMEM((extent + 8, width), f32)],
        compiler_params=kernel_params(48),
        cost_estimate=pl.CostEstimate(
            flops=slots * extent * inner * 500, bytes_accessed=slots * extent * cols * 8, transcendentals=slots * extent * cols
        ),
        name="mixer_enter",
    )(v, halo, cw, hp)


def scan_kernel(reverse, got_ref, decay_ref, out_ref):
    count = got_ref.shape[0]
    state = jnp.zeros(got_ref.shape[1:], f32)
    order = range(count - 1, -1, -1) if reverse else range(count)
    for piece in order:
        out_ref[piece] = state
        state = decay_ref[piece] * state + got_ref[piece]


def scan_pieces(got, decay, reverse):
    return pl.pallas_call(
        functools.partial(scan_kernel, reverse),
        out_shape=jax.ShapeDtypeStruct(got.shape, f32),
        compiler_params=kernel_params(32),
        name="scan_pieces",
    )(got, decay)


def exchanged(rows):
    return lax.all_to_all(rows, "dp", 0, 0, tiled=False)


def states_forward(s_local, log_last):
    count = lax.axis_size("dp")
    slots, inner, _ = s_local.shape
    share = slots * inner // count
    per_row = jnp.repeat(jnp.exp(log_last).reshape(-1), HEAD_DIM).reshape(count, share)
    lines = -(-share // (8 * LANES)) * 8
    per_row = jnp.pad(per_row, ((0, 0), (0, lines * LANES - share))).reshape(count, lines, LANES)
    got = exchanged(jnp.concatenate([s_local.reshape(count, share, STATE_DIM), per_row], axis=1))
    decay = got[:, share:].reshape(count, lines * LANES)[:, :share, None]
    entering = exchanged(scan_pieces(got[:, :share], decay, False))
    return entering.reshape(slots, inner, STATE_DIM), decay


def states_backward(g_local, decay):
    count = lax.axis_size("dp")
    slots, inner, _ = g_local.shape
    got = exchanged(g_local.reshape(count, slots * inner // count, STATE_DIM))
    return exchanged(scan_pieces(got, decay, True)).reshape(slots, inner, STATE_DIM)


def leave_kernel(inner, xs_ref, rw_ref, dl_ref, h_ref, z_ref, hp_ref, gain_ref, y_ref, gg_ref, sq_ref, ybuf):
    extent = xs_ref.shape[1]
    zs, _, rows, _ = z_ref.shape
    xs = xs_ref[0]
    write = split_parts(rw_ref[0, :, :STATE_DIM])
    read = split_parts(rw_ref[0, :, STATE_DIM:])
    step_t = dl_ref[0, :, 0:LANES].T
    log_sum = dl_ref[0, :, LANES:]
    log_t = log_sum.T
    scores = dot_split(read, write, NT)
    causal = lax.broadcasted_iota(jnp.int32, (extent, extent), 0) >= lax.broadcasted_iota(
        jnp.int32, (extent, extent), 1
    )
    xs_low = xs.astype(bf16)
    for head in range(inner // HEAD_DIM):
        cols = slice(head * HEAD_DIM, (head + 1) * HEAD_DIM)
        gap = log_sum[:, head : head + 1] - log_t[head : head + 1, :]
        mixing = jnp.exp(jnp.where(causal, gap, -jnp.inf)) * scores * step_t[head : head + 1, :]
        ybuf[:, cols] = dot(mixing.astype(bf16), xs_low[:, cols], NN)
    spread = head_spread(inner)
    grown = dot(jnp.exp(log_sum), spread, NN, highest)
    y = ybuf[...] + grown * dot_split(read, split_parts(h_ref[0]), NT) + hp_ref[3:4, :] * xs
    y_ref[0] = y
    z = z_ref[...].reshape(extent, inner)
    gated = y * (z * jax.nn.sigmoid(z))
    sq_ref[0] = jnp.broadcast_to(jnp.sum(gated * gated, axis=1, keepdims=True), (extent, LANES))
    gg_ref[...] = (gated * gain_ref[...]).astype(bf16).reshape(zs, 1, rows, inner)


def mixer_leave(xs, rw, dl, h_in, z, skip, gain):
    zs, slots, rows, inner = z.shape
    extent = zs * rows
    return pl.pallas_call(
        functools.partial(leave_kernel, inner),
        grid=(slots,),
        in_specs=[
            pl.BlockSpec((1, extent, inner), lambda s: (s, 0, 0)),
            pl.BlockSpec((1, extent, 2 * STATE_DIM), lambda s: (s, 0, 0)),
            pl.BlockSpec((1, extent, 2 * LANES), lambda s: (s, 0, 0)),
            pl.BlockSpec((1, inner, STATE_DIM), lambda s: (s, 0, 0)),
            pl.BlockSpec((zs, 1, rows, inner), lambda s: (0, s, 0, 0)),
            pl.BlockSpec(skip.shape, lambda s: (0, 0)),
            pl.BlockSpec(gain.shape, lambda s: (0, 0)),
        ],
        out_specs=[
            pl.BlockSpec((1, extent, inner), lambda s: (s, 0, 0)),
            pl.BlockSpec((zs, 1, rows, inner), lambda s: (0, s, 0, 0)),
            pl.BlockSpec((1, extent, LANES), lambda s: (s, 0, 0)),
        ],
        out_shape=[
            jax.ShapeDtypeStruct((slots, extent, inner), f32),
            jax.ShapeDtypeStruct((zs, slots, rows, inner), bf16),
            jax.ShapeDtypeStruct((slots, extent, LANES), f32),
        ],
        scratch_shapes=[pltpu.VMEM((extent, inner), f32)],
        compiler_params=kernel_params(48),
        cost_estimate=pl.CostEstimate(
            flops=slots * extent * inner * 2000, bytes_accessed=slots * extent * inner * 16, transcendentals=slots * extent * inner
        ),
        name="mixer_leave",
    )(xs, rw, dl, h_in, z, skip, gain)


def unmix_kernel(inner, gn_ref, y_ref, z_ref, rw_ref, dl_ref, tok_ref, gain_ref, gy_ref, gz_ref, s_ref, gg_ref):
    extent = y_ref.shape[1]
    zs, _, rows, _ = z_ref.shape
    grad = gn_ref[...].reshape(extent, inner)
    z = z_ref[...].reshape(extent, inner)
    logistic = jax.nn.sigmoid(z)
    gate = z * logistic
    y = y_ref[0]
    gated = y * gate
    inv_rms = tok_ref[0, :, 0:1]
    cross = tok_ref[0, :, 1:2]
    part = jnp.sum(grad * gated * inv_rms, axis=0, keepdims=True)

    @pl.when(pl.program_id(0) == 0)
    def _():
        gg_ref[...] = jnp.zeros_like(gg_ref)

    gg_ref[0:1, :] += part
    gated_grad = grad * gain_ref[...] * inv_rms - gated * cross
    gy = gated_grad * gate
    gy_ref[0] = gy
    gz = gated_grad * y * (logistic * (1.0 + z * (1.0 - logistic)))
    gz_ref[...] = gz.astype(bf16).reshape(zs, 1, rows, inner)
    grown = dot(jnp.exp(dl_ref[0, :, LANES:]), head_spread(inner), NN, highest)
    s_ref[0] = dot_split(split_parts(gy * grown), split_parts(rw_ref[0, :, STATE_DIM:]), TN)


def mixer_unmix(gn, y, z, rw, dl, tok, gain):
    zs, slots, rows, inner = z.shape
    extent = zs * rows
    return pl.pallas_call(
        functools.partial(unmix_kernel, inner),
        grid=(slots,),
        in_specs=[
            pl.BlockSpec((zs, 1, rows, inner), lambda s: (0, s, 0, 0)),
            pl.BlockSpec((1, extent, inner), lambda s: (s, 0, 0)),
            pl.BlockSpec((zs, 1, rows, inner), lambda s: (0, s, 0, 0)),
            pl.BlockSpec((1, extent, 2 * STATE_DIM), lambda s: (s, 0, 0)),
            pl.BlockSpec((1, extent, 2 * LANES), lambda s: (s, 0, 0)),
            pl.BlockSpec((1, extent, 2), lambda s: (s, 0, 0)),
            pl.BlockSpec(gain.shape, lambda s: (0, 0)),
        ],
        out_specs=[
            pl.BlockSpec((1, extent, inner), lambda s: (s, 0, 0)),
            pl.BlockSpec((zs, 1, rows, inner), lambda s: (0, s, 0, 0)),
            pl.BlockSpec((1, inner, STATE_DIM), lambda s: (s, 0, 0)),
            pl.BlockSpec((8, inner), lambda s: (0, 0)),
        ],
        out_shape=[
            jax.ShapeDtypeStruct((slots, extent, inner), f32),
            jax.ShapeDtypeStruct((zs, slots, rows, inner), bf16),
            jax.ShapeDtypeStruct((slots, inner, STATE_DIM), f32),
            jax.ShapeDtypeStruct((8, inner), f32),
        ],
        compiler_params=kernel_params(48),
        cost_estimate=pl.CostEstimate(
            flops=slots * extent * inner * 500, bytes_accessed=slots * extent * inner * 26, transcendentals=slots * extent * inner
        ),
        name="mixer_unmix",
    )(gn, y, z, rw, dl, tok, gain)


def back_kernel(
    inner, v_ref, halo_ref, cw_ref, hp_ref, skip_ref, rw_ref, dl_ref, gy_ref, h_ref, gh_ref,
    gv_ref, gbc_ref, gp_ref, gc_ref, ghp_ref, padded, gpad, bufs, cols_buf,
):
    extent = gy_ref.shape[1]
    zs, _, rows, _ = v_ref.shape
    width = padded.shape[1]
    heads = inner // HEAD_DIM
    first = pl.program_id(0) == 0
    pre = conv_of(v_ref, halo_ref, cw_ref, padded)
    logistic = jax.nn.sigmoid(pre)
    slope = logistic * (1.0 + pre * (1.0 - logistic))
    xs = pre[:, :inner] * logistic[:, :inner]
    write = split_parts(rw_ref[0, :, :STATE_DIM])
    read = split_parts(rw_ref[0, :, STATE_DIM:])
    raw, step = step_sizes(v_ref, hp_ref, width, extent)
    rate = jnp.exp(hp_ref[0:1, :])
    log_sum = dl_ref[0, :, LANES:]
    log_t = log_sum.T
    gy = gy_ref[0]
    gy_parts, xs_parts = split_parts(gy), split_parts(xs)
    scores_t = dot_split(write, read, NT)
    later = lax.broadcasted_iota(jnp.int32, (extent, extent), 1) >= lax.broadcasted_iota(
        jnp.int32, (extent, extent), 0
    )
    lane = lax.broadcasted_iota(jnp.int32, (extent, LANES), 1)
    score_grad_t = jnp.zeros((extent, extent), f32)
    step_direct = jnp.zeros((extent, LANES), f32)
    cols_buf[...] = jnp.zeros_like(cols_buf)
    for head in range(heads):
        cols = slice(head * HEAD_DIM, (head + 1) * HEAD_DIM)
        gap_t = log_t[head : head + 1, :] - log_sum[:, head : head + 1]
        decay_t = jnp.exp(jnp.where(later, gap_t, -jnp.inf))
        mix_t = decay_t * scores_t
        pair_t = dot_split([x[:, cols] for x in xs_parts], [g[:, cols] for g in gy_parts], NT)
        both_t = decay_t * pair_t
        step_col = step[:, head : head + 1]
        score_grad_t = score_grad_t + both_t * step_col
        weight_t = both_t * scores_t
        step_direct = step_direct + jnp.where(lane == head, jnp.sum(weight_t, axis=1, keepdims=True), 0.0)
        cols_buf[head : head + 1, :] = jnp.sum(weight_t * step_col, axis=0, keepdims=True)
        bufs[:, cols] = dot((mix_t * step_col).astype(bf16), gy_parts[0][:, cols], NN)
    sums = head_sums(inner)
    spread = head_spread(inner)
    last = log_sum[extent - 1 : extent, :]
    tail_decay = jnp.exp(last - log_sum)
    tail = dot(tail_decay * step, spread, NN, highest)
    grown = dot(jnp.exp(log_sum), spread, NN, highest)
    gh = gh_ref[0]
    h_in = h_ref[0]
    gh_parts, h_parts = split_parts(gh), split_parts(h_in)
    tail_in = dot(write[0], gh_parts[0], NT)
    tail_direct = tail_decay * dot(xs * tail_in, sums, NN, highest)
    tail_weight = tail_direct * step
    state_part = grown * dot(read[0], h_parts[0], NT)
    state_weight = dot(gy * state_part, sums, NN, highest)
    kept = dot(sums, jnp.sum(gh * h_in, axis=1, keepdims=True) * jnp.ones((1, LANES), f32), TN, highest).T[0:1, :]
    log_grad = cols_buf[...].T - step * step_direct + state_weight - tail_weight
    end_grad = jnp.sum(tail_weight, axis=0, keepdims=True) + jnp.exp(last) * kept
    rate_arg_grad = dot(lower_ones(extent), log_grad, TN, highest) + end_grad
    step_grad = step_direct + tail_direct - rate * rate_arg_grad
    raw_grad = step_grad * jax.nn.sigmoid(raw)
    xs_grad = bufs[...] + tail * tail_in + skip_ref[3:4, :] * gy
    score_parts = split_parts(score_grad_t)
    write_grad = dot_split(score_parts, read, NN) + dot_split(split_parts(tail * xs), gh_parts, NN)
    read_grad = dot_split(score_parts, write, TN) + dot_split(split_parts(grown * gy), h_parts, NN)
    valid_lane = lax.broadcasted_iota(jnp.int32, (1, LANES), 1) < heads
    rate_grad = jnp.where(valid_lane, jnp.sum(-step * rate * rate_arg_grad, axis=0, keepdims=True), 0.0)
    raw_grad = jnp.where(valid_lane, raw_grad, 0.0)
    skip_grad = jnp.sum(dot(gy * xs, sums, NN, highest), axis=0, keepdims=True)

    @pl.when(first)
    def _():
        gc_ref[...] = jnp.zeros_like(gc_ref)
        ghp_ref[...] = jnp.zeros_like(ghp_ref)

    ghp_ref[0:1, :] += rate_grad
    ghp_ref[1:2, :] += jnp.sum(raw_grad, axis=0, keepdims=True)
    ghp_ref[2:3, :] += skip_grad
    gpad[0:8, :] = jnp.zeros((8, width), f32)
    gpad[extent + 8 :, :] = jnp.zeros((8, width), f32)
    gpad[8 : extent + 8, 0:inner] = xs_grad * slope[:, 0:inner]
    gpad[8 : extent + 8, inner : inner + STATE_DIM] = write_grad * slope[:, inner : inner + STATE_DIM]
    gpad[8 : extent + 8, inner + STATE_DIM :] = read_grad * slope[:, inner + STATE_DIM :]
    back = jnp.zeros((extent, width), f32)
    before = jnp.zeros((8, width), f32)
    pre_grad = gpad[8 : extent + 8, :]
    for tap in range(CONV_WIDTH):
        ahead = CONV_WIDTH - 1 - tap
        weight = cw_ref[tap : tap + 1, :]
        back = back + weight * gpad[8 + ahead : 8 + ahead + extent, :]
        before = before + weight * gpad[ahead : 8 + ahead, :]
        gc_ref[tap : tap + 1, :] += jnp.sum(pre_grad * padded[5 + tap : 5 + tap + extent, :], axis=0, keepdims=True)
    gc_ref[CONV_WIDTH : CONV_WIDTH + 1, :] += jnp.sum(pre_grad, axis=0, keepdims=True)
    gp_ref[0] = before
    gv_ref[:, :, :, 0:inner] = back[:, :inner].astype(bf16).reshape(zs, 1, rows, inner)
    gbc_ref[...] = back[:, inner:].reshape(zs, 1, rows, width - inner)
    gv_ref[:, :, :, inner:] = raw_grad.astype(bf16).reshape(zs, 1, rows, LANES)


def mixer_back(v, halo, cw, hp, skip, rw, dl, gy, h_in, gh):
    zs, slots, rows, cols = v.shape
    extent = zs * rows
    inner = gy.shape[2]
    width = cw.shape[1]
    return pl.pallas_call(
        functools.partial(back_kernel, inner),
        grid=(slots,),
        in_specs=[
            pl.BlockSpec((zs, 1, rows, cols), lambda s: (0, s, 0, 0)),
            pl.BlockSpec((1, 8, width), lambda s: (s, 0, 0)),
            pl.BlockSpec(cw.shape, lambda s: (0, 0)),
            pl.BlockSpec(hp.shape, lambda s: (0, 0)),
            pl.BlockSpec(skip.shape, lambda s: (0, 0)),
            pl.BlockSpec((1, extent, 2 * STATE_DIM), lambda s: (s, 0, 0)),
            pl.BlockSpec((1, extent, 2 * LANES), lambda s: (s, 0, 0)),
            pl.BlockSpec((1, extent, inner), lambda s: (s, 0, 0)),
            pl.BlockSpec((1, inner, STATE_DIM), lambda s: (s, 0, 0)),
            pl.BlockSpec((1, inner, STATE_DIM), lambda s: (s, 0, 0)),
        ],
        out_specs=[
            pl.BlockSpec((zs, 1, rows, inner + LANES), lambda s: (0, s, 0, 0)),
            pl.BlockSpec((zs, 1, rows, 2 * STATE_DIM), lambda s: (0, s, 0, 0)),
            pl.BlockSpec((1, 8, width), lambda s: (s, 0, 0)),
            pl.BlockSpec((8, width), lambda s: (0, 0)),
            pl.BlockSpec((8, LANES), lambda s: (0, 0)),
        ],
        out_shape=[
            jax.ShapeDtypeStruct((zs, slots, rows, inner + LANES), bf16),
            jax.ShapeDtypeStruct((zs, slots, rows, 2 * STATE_DIM), f32),
            jax.ShapeDtypeStruct((slots, 8, width), f32),
            jax.ShapeDtypeStruct((8, width), f32),
            jax.ShapeDtypeStruct((8, LANES), f32),
        ],
        scratch_shapes=[
            pltpu.VMEM((extent + 8, width), f32),
            pltpu.VMEM((extent + 16, width), f32),
            pltpu.VMEM((extent, inner), f32),
            pltpu.VMEM((LANES, extent), f32),
        ],
        compiler_params=kernel_params(56),
        cost_estimate=pl.CostEstimate(
            flops=slots * extent * inner * 5000, bytes_accessed=slots * extent * inner * 20, transcendentals=slots * extent * inner * 2
        ),
        name="mixer_back",
    )(v, halo, cw, hp, skip, rw, dl, gy, h_in, gh)


def expert_kernel(
    n_ref, g_ref, mask_ref, router_ref, up_ref, down_ref,
    moe_ref, back_ref, logit_ref, act_ref, hid_ref, moe_sum, back_sum, gates_buf, gate_grad,
):
    pair = pl.program_id(0)
    pairs = pl.num_programs(0)
    tokens = n_ref.shape[0]
    lane = lax.broadcasted_iota(jnp.int32, (tokens, LANES), 1)
    half = up_ref.shape[3] // 2

    @pl.when(pair == 0)
    def _():
        logits = dot(n_ref[...], router_ref[...], NN)
        chosen = mask_ref[...] > 0.0
        logits = jnp.where(chosen, logits, -jnp.inf)
        powers = jnp.exp(logits - jnp.max(logits, axis=1, keepdims=True))
        gates = powers / jnp.sum(powers, axis=1, keepdims=True)
        gates_buf[...] = jnp.where(lane < EXPERTS, gates, 1.0)
        moe_sum[...] = jnp.zeros_like(moe_sum)
        back_sum[...] = jnp.zeros_like(back_sum)
        gate_grad[...] = jnp.zeros_like(gate_grad)

    depth = up_ref.shape[0] * up_ref.shape[2]
    down = down_ref[...].reshape(depth, 2 * half)
    n_val = n_ref[...]
    gates = gates_buf[...]
    act_back = dot(g_ref[...], down, NN)
    for member in range(2):
        up = up_ref[:, member].reshape(depth, 2 * half)
        hidden = dot(n_val, up, NN)
        gate_part, up_part = hidden[:, :half], hidden[:, half:]
        logistic = jax.nn.sigmoid(gate_part)
        silu = gate_part * logistic
        act = (silu * up_part).astype(bf16).astype(f32)
        own = lane == 2 * pair + member
        gate = jnp.sum(jnp.where(own, gates, 0.0), axis=1, keepdims=True)
        part = act_back[:, member * half : (member + 1) * half]
        gate_grad[...] += jnp.where(own, jnp.sum(act * part, axis=1, keepdims=True), 0.0)
        act_ref[0, :, member * half : (member + 1) * half] = (gate * act).astype(bf16)
        part = part * gate
        hid_ref[member, :, :half] = (part * up_part * (logistic * (1.0 + gate_part * (1.0 - logistic)))).astype(bf16)
        hid_ref[member, :, half:] = (part * silu).astype(bf16)
        back_sum[...] += dot(hid_ref[member], up, NT)
    moe_sum[...] += dot(act_ref[0], down, NT)

    @pl.when(pair == pairs - 1)
    def _():
        gates_in = jnp.where(lane < EXPERTS, gates, 0.0)
        grads = gates_in * gate_grad[...]
        logit_grad = (grads - gates_in * jnp.sum(grads, axis=1, keepdims=True)).astype(bf16)
        logit_ref[...] = logit_grad
        back_ref[...] = (back_sum[...] + dot(logit_grad, router_ref[...], NT)).astype(bf16)
        moe_ref[...] = moe_sum[...].astype(bf16)


def experts(n_two, g_moe, mask, router, weights):
    tokens, width = n_two.shape
    count, blocks, rows, cols = weights.shape
    pairs = blocks // 3
    down_at = 2 * pairs
    return pl.pallas_call(
        expert_kernel,
        grid=(pairs,),
        in_specs=[
            pl.BlockSpec((tokens, width), lambda p: (0, 0)),
            pl.BlockSpec((tokens, width), lambda p: (0, 0)),
            pl.BlockSpec((tokens, LANES), lambda p: (0, 0)),
            pl.BlockSpec((width, LANES), lambda p: (0, 0)),
            pl.BlockSpec((count, 2, rows, cols), lambda p: (0, p, 0, 0)),
            pl.BlockSpec((count, 1, rows, cols), lambda p: (0, down_at + p, 0, 0)),
        ],
        out_specs=[
            pl.BlockSpec((tokens, width), lambda p: (0, 0)),
            pl.BlockSpec((tokens, width), lambda p: (0, 0)),
            pl.BlockSpec((tokens, LANES), lambda p: (0, 0)),
            pl.BlockSpec((1, tokens, cols), lambda p: (p, 0, 0)),
            pl.BlockSpec((2, tokens, cols), lambda p: (p, 0, 0)),
        ],
        out_shape=[
            jax.ShapeDtypeStruct((tokens, width), bf16),
            jax.ShapeDtypeStruct((tokens, width), bf16),
            jax.ShapeDtypeStruct((tokens, LANES), bf16),
            jax.ShapeDtypeStruct((pairs, tokens, cols), bf16),
            jax.ShapeDtypeStruct((2 * pairs, tokens, cols), bf16),
        ],
        scratch_shapes=[
            pltpu.VMEM((tokens, width), f32),
            pltpu.VMEM((tokens, width), f32),
            pltpu.VMEM((tokens, LANES), f32),
            pltpu.VMEM((tokens, LANES), f32),
        ],
        compiler_params=kernel_params(60),
        cost_estimate=pl.CostEstimate(
            flops=12 * tokens * width * cols * pairs, bytes_accessed=weights.size * 2 + tokens * width * 20, transcendentals=tokens * cols * pairs
        ),
        name="experts",
    )(n_two, g_moe, mask, router, weights, weights)


def expert_grad_kernel(up_blocks, chunks, start, *refs):
    n_refs, g_refs, h_refs, a_refs = (refs[i * chunks : (i + 1) * chunks] for i in range(4))
    out_ref = refs[4 * chunks]
    block = pl.program_id(0) + start
    count, _, rows, cols = out_ref.shape

    def summed(lefts, rights):
        total = dot(lefts[0][...], rights[0][0], NN)
        for left, right in zip(lefts[1:], rights[1:]):
            total = total + dot(left[...], right[0], NN)
        out_ref[...] = total.astype(bf16).reshape(count, 1, rows, cols)

    @pl.when(block < up_blocks)
    def _():
        summed(n_refs, h_refs)

    @pl.when(block >= up_blocks)
    def _():
        summed(g_refs, a_refs)


def expert_grads(n_list, g_list, hid_list, act_list, count, start, blocks):
    chunks = len(n_list)
    width, tokens = n_list[0].shape
    ups, _, cols = hid_list[0].shape
    whole = pl.BlockSpec((width, tokens), lambda b: (0, 0))
    return pl.pallas_call(
        functools.partial(expert_grad_kernel, ups, chunks, start),
        grid=(blocks,),
        in_specs=[whole] * (2 * chunks)
        + [pl.BlockSpec((1, tokens, cols), lambda b: (jnp.minimum(b + start, ups - 1), 0, 0))] * chunks
        + [pl.BlockSpec((1, tokens, cols), lambda b: (jnp.maximum(b + start - ups, 0), 0, 0))] * chunks,
        out_specs=pl.BlockSpec((count, 1, width // count, cols), lambda b: (0, b, 0, 0)),
        out_shape=jax.ShapeDtypeStruct((count, blocks, width // count, cols), bf16),
        compiler_params=kernel_params(48),
        cost_estimate=pl.CostEstimate(
            flops=2 * chunks * tokens * width * cols * blocks, bytes_accessed=blocks * width * cols * 2, transcendentals=0
        ),
        name="expert_grads",
    )(*n_list, *g_list, *hid_list, *act_list)


def body(
    block_input,
    out_grad,
    lengths,
    routes,
    norm1_gain,
    w_zx,
    w_bc,
    w_dt,
    conv_x,
    conv_bc,
    head_params,
    gate_gain,
    w_out,
    norm2_gain,
    w_router,
    w_gu,
    w_dn,
    s_gu,
    s_dn,
):
    zs = lax.axis_size("tensor")
    pieces = lax.axis_size("dp")
    own = lax.axis_index("tensor")
    wide_index = lax.axis_index("dp")
    rows = block_input.shape[0]
    piece_rows = rows * zs
    heads = HEAD_COUNT // zs
    inner = INNER_DIM // zs
    width = inner + 2 * STATE_DIM
    shard = D_MODEL // pieces
    half = w_gu.shape[3]
    rim = CONV_WIDTH - 1
    per = SLOT_COUNT // CHUNKS
    tokens = per * rows
    chunk_ids = range(CHUNKS)

    enter_shard = jnp.concatenate(
        [w_zx[:, 1], w_bc, jnp.pad(w_dt, ((0, 0), (0, LANES - heads)))], axis=1
    )
    side_shard = jnp.concatenate([w_zx[:, 0], w_out.T], axis=1)
    router_shard = jnp.pad(w_router, ((0, 0), (0, LANES - EXPERTS)))
    expert_shard = jnp.concatenate(
        [
            w_gu.reshape(EXPERTS, shard, 2 * half),
            s_gu.reshape(shard, 2, 2, half).transpose(2, 0, 1, 3).reshape(2, shard, 2 * half),
            w_dn.reshape(EXPERTS // 2, 2 * half, shard).transpose(0, 2, 1),
            s_dn.T[None],
        ],
        axis=0,
    )
    full_enter = weight_gather(enter_shard).reshape(D_MODEL, width + LANES)
    full_side = weight_gather(side_shard).reshape(D_MODEL, 2 * inner)
    full_z, full_out = full_side[:, :inner], full_side[:, inner:]
    gains = jnp.stack([norm1_gain, norm2_gain], axis=1).astype(f32)
    gains = lax.all_gather(gains, "dp", axis=0, tiled=True)
    gain_one, gain_two = gains[:, 0], gains[:, 1]
    full_router = weight_gather(router_shard).reshape(D_MODEL, LANES)
    full_expert = weight_gather(expert_shard)

    positions = wide_index * piece_rows + own * rows + jnp.arange(rows, dtype=jnp.int32)
    valid = (positions[None, :] < lengths[:, None]).astype(f32)[:, :, None]
    u_slots = jnp.transpose(block_input, (1, 0, 2)).astype(f32)
    grad_slots = jnp.transpose(out_grad, (1, 0, 2)).astype(f32) * valid

    def part(values, c):
        return values[c * per : (c + 1) * per].reshape((tokens,) + values.shape[2:])

    conv_w = jnp.pad(jnp.concatenate([conv_x, conv_bc], axis=1), ((0, 8 - CONV_WIDTH - 1), (0, 0)))
    hp = jnp.pad(head_params, ((0, 5), (0, LANES - heads)))
    skip = jnp.pad(jnp.repeat(head_params[2], HEAD_DIM)[None], ((3, 4), (0, 0)))
    gain_row = gate_gain[None]

    hot = jnp.sum(
        (routes[..., None] == jnp.arange(LANES, dtype=jnp.int32)).astype(f32), axis=2
    )
    hot = jnp.transpose(hot.reshape(zs, rows, SLOT_COUNT, LANES), (0, 2, 1, 3))
    hot_at = by_distance(hot)

    u, valid_c, grad_c, n_one, n_one_t, v, halo, z = [], [], [], [], [], [], [], []
    for c in chunk_ids:
        u.append(part(u_slots, c))
        valid_c.append(part(valid, c))
        grad_c.append(part(grad_slots, c))
        normed = rms_scale(u[c], gain_one).astype(bf16)
        n_one.append(in_order(line_gather(normed)))
    for c in chunk_ids:
        flat = n_one[c].reshape(zs * tokens, D_MODEL)
        v.append(dot(flat, full_enter, NN).reshape(zs, per, rows, width + LANES))
        rim_rows = n_one[c].reshape(zs, per, rows, D_MODEL)[zs - 1, :, rows - rim :]
        prior = dot(passed_along(rim_rows, "dp", 1).reshape(per * rim, D_MODEL), full_enter[:, :width], NN)
        halo.append(jnp.pad(prior.reshape(per, rim, width), ((0, 0), (8 - rim, 0), (0, 0))))
    entered = [mixer_enter(v[c], halo[c], conv_w, hp, inner) for c in chunk_ids]
    g_moe = [jnp.concatenate(line_gather(after(grad_c[c].astype(bf16), n_one[c])), axis=0) for c in chunk_ids]
    resid, mixed_all, y_all, h_all, decay_all, tok_all, gg_all, n_two = [], [], [], [], [], [], [], []
    for c in chunk_ids:
        xs, rw, dl, s_local = entered[c]
        h_in, decay = states_forward(s_local, dl[:, piece_rows - 1, LANES : LANES + heads])
        h_in = after(h_in, g_moe[c])
        z.append(dot(n_one[c].reshape(zs * tokens, D_MODEL), full_z, NN).reshape(zs, per, rows, inner))
        y, gg, squares = mixer_leave(xs, rw, dl, h_in, z[c], skip, gain_row)
        square_sum = lax.psum(squares[:, :, 0], "tensor")
        inv_all = lax.rsqrt(square_sum / INNER_DIM + norm_eps)
        inv_own = lax.dynamic_slice_in_dim(inv_all, own * rows, rows, 1).reshape(tokens, 1)
        product = dot(gg.reshape(zs * tokens, inner), full_out, NT).astype(bf16)
        mixed = line_scatter(by_distance(product.reshape(zs, tokens, D_MODEL))) * inv_own
        resid.append(u[c] + mixed)
        mixed_all.append(mixed)
        y_all.append(y)
        h_all.append(h_in)
        decay_all.append(decay)
        tok_all.append(inv_all)
        gg_all.append(gg)
        normed = rms_scale(resid[c], gain_two).astype(bf16)
        n_two.append(jnp.concatenate(line_gather(normed), axis=0))
    moe_part, back_part, logit_grads, acts, hids = [], [], [], [], []
    for c in chunk_ids:
        mask = jnp.concatenate([part(hot_at(k), c) for k in range(zs)], axis=0)
        results = experts(n_two[c], g_moe[c], mask, full_router, full_expert)
        moe_part.append(results[0].reshape(zs, tokens, D_MODEL))
        back_part.append(results[1].reshape(zs, tokens, D_MODEL))
        logit_grads.append(results[2])
        acts.append(results[3])
        hids.append(results[4])

    def two_back(values, gain_vec):
        return jax.vjp(rms_scale, values, gain_vec)[1]

    n_two_t, g_moe_t = [n.T for n in n_two], [g.T for g in g_moe]
    third = (EXPERTS + 2) // 2
    expert_grad = [
        expert_grads(n_two_t, g_moe_t, hids, acts, pieces, start, third) for start in (0, third, 2 * third)
    ]
    resid_grad, g_mixed, gain_two_grad = [], [], 0.0
    unmixed, gate_gain_grad = [], 0.0
    for c in chunk_ids:
        n_two_grad = line_scatter(lambda k: back_part[c][k])
        from_norm, gain_grad = two_back(resid[c], gain_two)(n_two_grad)
        gain_two_grad = gain_two_grad + gain_grad
        resid_grad.append(grad_c[c] + from_norm)
        low = resid_grad[c].astype(bf16)
        if c == 0:
            low = after(low, expert_grad[0], expert_grad[1])
        g_mixed.append(in_order(line_gather(low)))
        grad = dot(g_mixed[c].reshape(zs * tokens, D_MODEL), full_out, NN).reshape(zs, per, rows, inner)
        if c == 0:
            grad = after(grad, expert_grad[2])
        xs, rw, dl, _ = entered[c]
        inv_all = tok_all[c]
        y_like = jnp.transpose(y_all[c].reshape(per, zs, rows, inner), (1, 0, 2, 3))
        cross = jnp.sum(grad * gain_row * y_like * jax.nn.silu(z[c]), axis=-1)
        cross = lax.psum(jnp.transpose(cross, (1, 0, 2)).reshape(per, piece_rows), "tensor")
        tok = jnp.stack([inv_all, cross * (inv_all * inv_all * inv_all) / INNER_DIM], axis=-1)
        gy, gz, g_local, gg_grad = mixer_unmix(grad, y_all[c], z[c], rw, dl, tok, gain_row)
        gate_gain_grad = gate_gain_grad + gg_grad[0]
        unmixed.append((gy, gz, g_local))

    moe_part = [after(moe_part[c], g_mixed[c]) for c in chunk_ids]
    moe = [line_scatter(lambda k: moe_part[c][k]) for c in chunk_ids]
    output = [resid[c] + moe[c] for c in chunk_ids]
    stat_terms = sum(
        jnp.stack(
            [
                jnp.sum(valid_c[c] * output[c] * output[c]),
                jnp.sum(valid_c[c] * mixed_all[c] * mixed_all[c]),
                jnp.sum(valid_c[c] * moe[c] * moe[c]),
            ]
        )
        for c in chunk_ids
    )
    router_grad = sum(dot(n_two[c], logit_grads[c], TN)[:, :EXPERTS] for c in chunk_ids)

    def rows_of(values):
        return jnp.concatenate([v.reshape(zs * tokens, -1) for v in values], axis=0)

    inv_rows = [
        jnp.transpose(tok_all[c].reshape(per, zs, rows), (1, 0, 2)).reshape(zs * tokens, 1) for c in chunk_ids
    ]
    scaled = [
        (g_mixed[c].reshape(zs * tokens, D_MODEL).astype(f32) * inv_rows[c]).astype(bf16) for c in chunk_ids
    ]
    out_w_grad = dot(rows_of(scaled), rows_of(gg_all), TN)

    z_grads, v_grads, bc_grads, conv_grad, head_grad = [], [], [], 0.0, 0.0
    full_x = jnp.concatenate([full_enter[:, :inner], full_enter[:, width:]], axis=1)
    full_bc = full_enter[:, inner:width]
    full_bc = jnp.concatenate([full_bc, full_bc], axis=1)
    for c in chunk_ids:
        gy, gz, g_local = unmixed[c]
        xs, rw, dl, _ = entered[c]
        gh = states_backward(g_local, decay_all[c])
        gv, gbc, g_rim, gc, ghp = mixer_back(
            v[c], halo[c], conv_w, hp, skip, rw, dl, gy, h_all[c], gh
        )
        conv_grad = conv_grad + gc
        head_grad = head_grad + ghp
        following = passed_along(g_rim[:, 8 - rim :].astype(bf16), "dp", -1)
        following = following.astype(f32)
        edge = gv[zs - 1, :, rows - rim :, :inner].astype(f32) + following[:, :, :inner]
        gv = lax.dynamic_update_slice(gv, edge.astype(bf16)[None], (zs - 1, 0, rows - rim, 0))
        edge = gbc[zs - 1, :, rows - rim :] + following[:, :, inner:]
        gbc = lax.dynamic_update_slice(gbc, edge[None], (zs - 1, 0, rows - rim, 0))
        z_grads.append(gz)
        v_grads.append(gv)
        bc_grads.append(jnp.concatenate(split_parts(gbc), axis=-1))
    u_grad, gain_one_grad = [], 0.0
    for c in chunk_ids:
        n_grad = (
            dot(z_grads[c].reshape(zs * tokens, inner), full_z, NT)
            + dot(v_grads[c].reshape(zs * tokens, inner + LANES), full_x, NT)
            + dot(bc_grads[c].reshape(zs * tokens, 4 * STATE_DIM), full_bc, NT)
        )
        n_grad = n_grad.astype(bf16).reshape(zs, tokens, D_MODEL)
        from_norm, gain_grad = two_back(u[c], gain_one)(line_scatter(by_distance(n_grad)))
        gain_one_grad = gain_one_grad + gain_grad
        u_grad.append(resid_grad[c] + from_norm)
    n_rows = rows_of(n_one)
    z_w_grad = dot(n_rows, rows_of(z_grads), TN)
    enter_w_grad = dot(n_rows, rows_of(v_grads), TN)
    bc_w_grad = dot(n_rows, rows_of(bc_grads), TN)
    bc_w_grad = bc_w_grad[:, : 2 * STATE_DIM] + bc_w_grad[:, 2 * STATE_DIM :]
    side_grad = weight_scatter(
        jnp.concatenate([z_w_grad, out_w_grad], axis=1).reshape(pieces, shard, 2 * inner)
    ).astype(f32)
    enter_grad = weight_scatter(enter_w_grad.reshape(pieces, shard, inner + LANES)).astype(f32)

    column = own * inner
    conv_x_full = lax.dynamic_update_slice(
        jnp.zeros((CONV_WIDTH + 1, INNER_DIM), f32), conv_grad[: CONV_WIDTH + 1, :inner], (jnp.int32(0), column)
    )
    gate_full = lax.dynamic_update_slice(jnp.zeros((INNER_DIM,), f32), gate_gain_grad, (column,))
    head_full = lax.dynamic_update_slice(
        jnp.zeros((3, HEAD_COUNT), f32), head_grad[:3, :heads], (jnp.int32(0), own * heads)
    )
    both = ("dp", "tensor")
    bc_grad = lax.psum_scatter(bc_w_grad, both, scatter_dimension=0, tiled=True)
    shared_grads = (
        lax.psum_scatter(gain_one_grad, both, scatter_dimension=0, tiled=True),
        lax.psum_scatter(conv_x_full, both, scatter_dimension=1, tiled=True),
        lax.psum_scatter(conv_grad[: CONV_WIDTH + 1, inner:], both, scatter_dimension=1, tiled=True),
        lax.psum_scatter(gate_full, both, scatter_dimension=0, tiled=True),
        lax.psum_scatter(gain_two_grad, both, scatter_dimension=0, tiled=True),
        lax.psum_scatter(router_grad, both, scatter_dimension=0, tiled=True),
    )
    stat_sum, head_sum = lax.psum((stat_terms, head_full), both)
    stats = jnp.sqrt(stat_sum / (jnp.sum(lengths).astype(f32) * D_MODEL))

    def placed_back(values):
        whole = jnp.concatenate([value.astype(bf16).reshape(per, rows, D_MODEL) for value in values], axis=0)
        return jnp.transpose(whole, (1, 0, 2))

    expert_grad = jnp.concatenate([weight_scatter(grads) for grads in expert_grad], axis=0).astype(f32)
    ups, pairs = EXPERTS + 2, EXPERTS // 2
    return (
        placed_back(output),
        placed_back(u_grad),
        shared_grads[0],
        jnp.stack([side_grad[:, :inner], enter_grad[:, :inner]], axis=1),
        bc_grad,
        enter_grad[:, inner : inner + heads],
        shared_grads[1],
        shared_grads[2],
        head_sum,
        shared_grads[3],
        side_grad[:, inner:].T,
        shared_grads[4],
        shared_grads[5],
        expert_grad[:EXPERTS].reshape(EXPERTS, shard, 2, half),
        expert_grad[ups : ups + pairs].transpose(0, 2, 1).reshape(EXPERTS, half, shard),
        expert_grad[EXPERTS:ups].reshape(2, shard, 2, half).transpose(1, 2, 0, 3).reshape(shard, 2, 2 * half),
        expert_grad[ups + pairs].T,
        stats,
    )


def solution(mesh):
    both = ("dp", "tensor")
    placed = (
        P(both, None, None),
        P(both, None, None),
        P(),
        P("dp", None, None),
        P("dp"),
        P("dp", None, "tensor"),
        P("dp", None),
        P("dp", "tensor"),
        P(None, "tensor"),
        P(),
        P(None, "tensor"),
        P("tensor"),
        P("tensor", "dp"),
        P("dp"),
        P("dp", None),
        P(None, "dp", None, "tensor"),
        P(None, "tensor", "dp"),
        P("dp", None, "tensor"),
        P("tensor", "dp"),
    )
    return jax.shard_map(
        body,
        mesh=mesh,
        in_specs=placed,
        out_specs=(
            P(both, None, None),
            P(both, None, None),
            P(both),
            P("dp", None, "tensor"),
            P(both, None),
            P("dp", "tensor"),
            P(None, both),
            P(None, both),
            P(),
            P(both),
            P("tensor", "dp"),
            P(both),
            P(both, None),
            P(None, "dp", None, "tensor"),
            P(None, "tensor", "dp"),
            P("dp", None, "tensor"),
            P("tensor", "dp"),
            P(),
        ),
        check_vma=False,
    )
```

```python
import functools

import jax
import jax.numpy as jnp
from jax import lax
from jax.experimental import pallas as pl
from jax.experimental.layout import Layout, with_layout_constraint
from jax.experimental.pallas import tpu as pltpu
from jax.sharding import PartitionSpec as P

D_MODEL = 1536
HEAD_COUNT = 48
HEAD_DIM = 64
STATE_DIM = 128
CONV_WIDTH = 4
TOP_K = 6
EXPERTS = 16
SLOT_COUNT = 4
INNER_DIM = 3072
LANES = 128
CHUNKS = 1

norm_eps = 1e-05
highest = lax.Precision.HIGHEST
f32 = jnp.float32
bf16 = jnp.bfloat16


def passed_along(value, axis, steps):
    count = lax.axis_size(axis)
    first, last = (max(0, -steps), min(count, count - steps))
    return lax.ppermute(value, axis, [(source, source + steps) for source in range(first, last)])


def row_major(value):
    return with_layout_constraint(value, Layout(major_to_minor=tuple(range(value.ndim))))


def line_gather(value):
    size = lax.axis_size("tensor")
    return lax.all_to_all(row_major(jnp.broadcast_to(value[None], (size,) + value.shape)), "tensor", 0, 0)


def line_scatter(blocks):
    got = lax.all_to_all(row_major(blocks), "tensor", 0, 0)
    return row_major(jnp.sum(got.astype(f32), axis=0))


def line_scatter_steps(blocks):
    size = lax.axis_size("tensor")
    own = lax.axis_index("tensor")
    total = lax.dynamic_index_in_dim(blocks, own, 0, False).astype(f32)
    for step in range(1, size):
        sent = lax.dynamic_index_in_dim(blocks, (own + step) % size, 0, False)
        sent = lax.ppermute(row_major(sent), "tensor", [(a, (a + step) % size) for a in range(size)])
        total = total + sent.astype(f32)
    return row_major(total)


def weight_gather(shard):
    return lax.all_gather(shard, "dp", axis=0, tiled=False)


def weight_scatter(grads):
    return lax.psum_scatter(grads.astype(bf16), "dp", scatter_dimension=0, tiled=False)


def rms_scale(values, gain_vec):
    return (
        values * lax.rsqrt(jnp.mean(values * values, axis=-1, keepdims=True) + norm_eps) * gain_vec
    )


def silu_slope(values):
    logistic = jax.nn.sigmoid(values)
    return logistic * (1.0 + values * (1.0 - logistic))


def dot(a, b, dims, precision=None):
    return lax.dot_general(a, b, (dims, ((), ())), precision=precision, preferred_element_type=f32)


def split_parts(values):
    upper = values.astype(bf16)
    return upper, (values - upper.astype(f32)).astype(bf16)


def dot_split(a, b, dims):
    return dot(a[0], b[0], dims) + (dot(a[0], b[1], dims) + dot(a[1], b[0], dims))


def after(value, *others):
    anywhere = pl.BlockSpec(memory_space=pl.ANY)
    return pl.pallas_call(
        lambda *refs: None,
        in_specs=[anywhere] * (1 + len(others)),
        out_specs=anywhere,
        out_shape=jax.ShapeDtypeStruct(value.shape, value.dtype),
        input_output_aliases={0: 0},
        name="after",
    )(value, *others)


NN = ((1,), (0,))
NT = ((1,), (1,))
TN = ((0,), (0,))


def head_spread(inner):
    row = lax.broadcasted_iota(jnp.int32, (LANES, inner), 0)
    col = lax.broadcasted_iota(jnp.int32, (LANES, inner), 1)
    return (col // HEAD_DIM == row).astype(f32)


def head_sums(inner):
    row = lax.broadcasted_iota(jnp.int32, (inner, LANES), 0)
    col = lax.broadcasted_iota(jnp.int32, (inner, LANES), 1)
    return (row // HEAD_DIM == col).astype(f32)


def lower_ones(extent):
    row = lax.broadcasted_iota(jnp.int32, (extent, extent), 0)
    col = lax.broadcasted_iota(jnp.int32, (extent, extent), 1)
    return (row >= col).astype(f32)


def kernel_params(mib):
    return pltpu.CompilerParams(vmem_limit_bytes=mib * 1024 * 1024)


def taking(micros, tokens):
    return pl.CostEstimate(flops=int(micros * tokens * 1.1e6), bytes_accessed=1024, transcendentals=0)


def conv_of(v_ref, halo_ref, cw_ref, padded):
    extent = padded.shape[0] - 8
    width = padded.shape[1]
    padded[0:8, :] = halo_ref[0]
    padded[8:, :] = v_ref[:, 0, :, 0:width].reshape(extent, width)
    summed = cw_ref[CONV_WIDTH : CONV_WIDTH + 1, :]
    for tap in range(CONV_WIDTH):
        summed = summed + cw_ref[tap : tap + 1, :] * padded[5 + tap : 5 + tap + extent, :]
    return summed


def step_sizes(v_ref, hp_ref, conv_width, extent):
    raw = v_ref[:, 0, :, conv_width : conv_width + LANES].reshape(extent, LANES) + hp_ref[1:2, :]
    step = jnp.maximum(raw, 0.0) + jnp.log1p(jnp.exp(-jnp.abs(raw)))
    return raw, step


def enter_kernel(inner, v_ref, halo_ref, cw_ref, hp_ref, xs_ref, rw_ref, dl_ref, s_ref, padded):
    extent = xs_ref.shape[1]
    width = padded.shape[1]
    pre = conv_of(v_ref, halo_ref, cw_ref, padded)
    act = pre * jax.nn.sigmoid(pre)
    xs = act[:, :inner]
    write = act[:, inner : inner + STATE_DIM]
    unused_raw, step = step_sizes(v_ref, hp_ref, width, extent)
    log_sum = dot(lower_ones(extent), -step * jnp.exp(hp_ref[0:1, :]), NN, highest)
    tail = jnp.exp(log_sum[extent - 1 : extent, :] - log_sum) * step
    spread = dot(tail, head_spread(inner), NN, highest)
    xs_ref[0] = xs
    rw_ref[0] = act[:, inner:]
    dl_ref[0, :, 0:LANES] = step
    dl_ref[0, :, LANES:] = log_sum
    s_ref[0] = dot_split(split_parts(xs * spread), split_parts(write), TN)


def mixer_enter(v, halo, cw, hp, inner):
    zs, slots, rows, cols = v.shape
    extent = zs * rows
    width = cw.shape[1]
    heads = inner // HEAD_DIM
    return pl.pallas_call(
        functools.partial(enter_kernel, inner),
        grid=(slots,),
        in_specs=[
            pl.BlockSpec((zs, 1, rows, cols), lambda s: (0, s, 0, 0)),
            pl.BlockSpec((1, 8, width), lambda s: (s, 0, 0)),
            pl.BlockSpec(cw.shape, lambda s: (0, 0)),
            pl.BlockSpec(hp.shape, lambda s: (0, 0)),
        ],
        out_specs=[
            pl.BlockSpec((1, extent, inner), lambda s: (s, 0, 0)),
            pl.BlockSpec((1, extent, 2 * STATE_DIM), lambda s: (s, 0, 0)),
            pl.BlockSpec((1, extent, 2 * LANES), lambda s: (s, 0, 0)),
            pl.BlockSpec((1, inner, STATE_DIM), lambda s: (s, 0, 0)),
        ],
        out_shape=[
            jax.ShapeDtypeStruct((slots, extent, inner), f32),
            jax.ShapeDtypeStruct((slots, extent, 2 * STATE_DIM), f32),
            jax.ShapeDtypeStruct((slots, extent, 2 * LANES), f32),
            jax.ShapeDtypeStruct((slots, inner, STATE_DIM), f32),
        ],
        scratch_shapes=[pltpu.VMEM((extent + 8, width), f32)],
        compiler_params=kernel_params(48),
        cost_estimate=taking(12, zs * slots * rows),
        name="mixer_enter",
    )(v, halo, cw, hp)


def scan_kernel(reverse, got_ref, decay_ref, out_ref):
    count = got_ref.shape[0]
    state = jnp.zeros(got_ref.shape[1:], f32)
    order = range(count - 1, -1, -1) if reverse else range(count)
    for piece in order:
        out_ref[piece] = state
        state = decay_ref[piece] * state + got_ref[piece]


def scan_pieces(got, decay, reverse):
    return pl.pallas_call(
        functools.partial(scan_kernel, reverse),
        out_shape=jax.ShapeDtypeStruct(got.shape, f32),
        compiler_params=kernel_params(32),
        name="scan_pieces",
    )(got, decay)


def exchanged(rows):
    return lax.all_to_all(rows, "dp", 0, 0, tiled=False)


def states_forward(s_local, log_last):
    count = lax.axis_size("dp")
    slots, inner, _ = s_local.shape
    share = slots * inner // count
    per_row = jnp.repeat(jnp.exp(log_last).reshape(-1), HEAD_DIM).reshape(count, share)
    lines = -(-share // (8 * LANES)) * 8
    per_row = jnp.pad(per_row, ((0, 0), (0, lines * LANES - share))).reshape(count, lines, LANES)
    got = exchanged(jnp.concatenate([s_local.reshape(count, share, STATE_DIM), per_row], axis=1))
    decay = got[:, share:].reshape(count, lines * LANES)[:, :share, None]
    entering = exchanged(scan_pieces(got[:, :share], decay, False))
    return entering.reshape(slots, inner, STATE_DIM), decay


def states_backward(g_local, decay):
    count = lax.axis_size("dp")
    slots, inner, _ = g_local.shape
    got = exchanged(g_local.reshape(count, slots * inner // count, STATE_DIM))
    return exchanged(scan_pieces(got, decay, True)).reshape(slots, inner, STATE_DIM)


def inner_kernel(inner, xs_ref, rw_ref, dl_ref, y_ref):
    extent = xs_ref.shape[1]
    write = split_parts(rw_ref[0, :, :STATE_DIM])
    read = split_parts(rw_ref[0, :, STATE_DIM:])
    step_t = dl_ref[0, :, 0:LANES].T
    log_sum = dl_ref[0, :, LANES:]
    log_t = log_sum.T
    scores = dot_split(read, write, NT)
    causal = lax.broadcasted_iota(jnp.int32, (extent, extent), 0) >= lax.broadcasted_iota(
        jnp.int32, (extent, extent), 1
    )
    xs_low = xs_ref[0].astype(bf16)
    for head in range(inner // HEAD_DIM):
        cols = slice(head * HEAD_DIM, (head + 1) * HEAD_DIM)
        gap = log_sum[:, head : head + 1] - log_t[head : head + 1, :]
        mixing = jnp.exp(jnp.where(causal, gap, -jnp.inf)) * scores * step_t[head : head + 1, :]
        y_ref[0, :, cols] = dot(mixing.astype(bf16), xs_low[:, cols], NN)


def mixer_inner(xs, rw, dl):
    slots, extent, inner = xs.shape
    return pl.pallas_call(
        functools.partial(inner_kernel, inner),
        grid=(slots,),
        in_specs=[
            pl.BlockSpec((1, extent, inner), lambda s: (s, 0, 0)),
            pl.BlockSpec((1, extent, 2 * STATE_DIM), lambda s: (s, 0, 0)),
            pl.BlockSpec((1, extent, 2 * LANES), lambda s: (s, 0, 0)),
        ],
        out_specs=pl.BlockSpec((1, extent, inner), lambda s: (s, 0, 0)),
        out_shape=jax.ShapeDtypeStruct((slots, extent, inner), f32),
        compiler_params=kernel_params(40),
        cost_estimate=taking(9, slots * extent),
        name="mixer_inner",
    )(xs, rw, dl)


def leave_kernel(inner, yi_ref, xs_ref, rw_ref, dl_ref, h_ref, z_ref, hp_ref, gain_ref, y_ref, gg_ref, sq_ref):
    extent = xs_ref.shape[1]
    zs, _, rows, _ = z_ref.shape
    read = split_parts(rw_ref[0, :, STATE_DIM:])
    grown = dot(jnp.exp(dl_ref[0, :, LANES:]), head_spread(inner), NN, highest)
    y = yi_ref[0] + grown * dot_split(read, split_parts(h_ref[0]), NT) + hp_ref[3:4, :] * xs_ref[0]
    y_ref[0] = y
    z = z_ref[...].reshape(extent, inner)
    gated = y * (z * jax.nn.sigmoid(z))
    sq_ref[0] = jnp.broadcast_to(jnp.sum(gated * gated, axis=1, keepdims=True), (extent, LANES))
    gg_ref[...] = (gated * gain_ref[...]).astype(bf16).reshape(zs, 1, rows, inner)


def mixer_leave(yi, xs, rw, dl, h_in, z, skip, gain):
    zs, slots, rows, inner = z.shape
    extent = zs * rows
    return pl.pallas_call(
        functools.partial(leave_kernel, inner),
        grid=(slots,),
        in_specs=[
            pl.BlockSpec((1, extent, inner), lambda s: (s, 0, 0)),
            pl.BlockSpec((1, extent, inner), lambda s: (s, 0, 0)),
            pl.BlockSpec((1, extent, 2 * STATE_DIM), lambda s: (s, 0, 0)),
            pl.BlockSpec((1, extent, 2 * LANES), lambda s: (s, 0, 0)),
            pl.BlockSpec((1, inner, STATE_DIM), lambda s: (s, 0, 0)),
            pl.BlockSpec((zs, 1, rows, inner), lambda s: (0, s, 0, 0)),
            pl.BlockSpec(skip.shape, lambda s: (0, 0)),
            pl.BlockSpec(gain.shape, lambda s: (0, 0)),
        ],
        out_specs=[
            pl.BlockSpec((1, extent, inner), lambda s: (s, 0, 0)),
            pl.BlockSpec((zs, 1, rows, inner), lambda s: (0, s, 0, 0)),
            pl.BlockSpec((1, extent, LANES), lambda s: (s, 0, 0)),
        ],
        out_shape=[
            jax.ShapeDtypeStruct((slots, extent, inner), f32),
            jax.ShapeDtypeStruct((zs, slots, rows, inner), bf16),
            jax.ShapeDtypeStruct((slots, extent, LANES), f32),
        ],
        compiler_params=kernel_params(48),
        cost_estimate=taking(7, zs * slots * rows),
        name="mixer_leave",
    )(yi, xs, rw, dl, h_in, z, skip, gain)


def unmix_kernel(inner, gn_ref, y_ref, z_ref, rw_ref, dl_ref, tok_ref, gain_ref, gy_ref, gz_ref, s_ref, gg_ref):
    extent = y_ref.shape[1]
    zs, _, rows, _ = z_ref.shape
    grad = gn_ref[...].reshape(extent, inner)
    z = z_ref[...].reshape(extent, inner)
    logistic = jax.nn.sigmoid(z)
    gate = z * logistic
    y = y_ref[0]
    gated = y * gate
    inv_rms = tok_ref[0, :, 0:1]
    cross = tok_ref[0, :, 1:2]
    part = jnp.sum(grad * gated * inv_rms, axis=0, keepdims=True)

    @pl.when(pl.program_id(0) == 0)
    def _():
        gg_ref[...] = jnp.zeros_like(gg_ref)

    gg_ref[0:1, :] += part
    gated_grad = grad * gain_ref[...] * inv_rms - gated * cross
    gy = gated_grad * gate
    gy_ref[0] = gy
    gz = gated_grad * y * (logistic * (1.0 + z * (1.0 - logistic)))
    gz_ref[...] = gz.astype(bf16).reshape(zs, 1, rows, inner)
    grown = dot(jnp.exp(dl_ref[0, :, LANES:]), head_spread(inner), NN, highest)
    s_ref[0] = dot_split(split_parts(gy * grown), split_parts(rw_ref[0, :, STATE_DIM:]), TN)


def mixer_unmix(gn, y, z, rw, dl, tok, gain):
    zs, slots, rows, inner = z.shape
    extent = zs * rows
    return pl.pallas_call(
        functools.partial(unmix_kernel, inner),
        grid=(slots,),
        in_specs=[
            pl.BlockSpec((zs, 1, rows, inner), lambda s: (0, s, 0, 0)),
            pl.BlockSpec((1, extent, inner), lambda s: (s, 0, 0)),
            pl.BlockSpec((zs, 1, rows, inner), lambda s: (0, s, 0, 0)),
            pl.BlockSpec((1, extent, 2 * STATE_DIM), lambda s: (s, 0, 0)),
            pl.BlockSpec((1, extent, 2 * LANES), lambda s: (s, 0, 0)),
            pl.BlockSpec((1, extent, 2), lambda s: (s, 0, 0)),
            pl.BlockSpec(gain.shape, lambda s: (0, 0)),
        ],
        out_specs=[
            pl.BlockSpec((1, extent, inner), lambda s: (s, 0, 0)),
            pl.BlockSpec((zs, 1, rows, inner), lambda s: (0, s, 0, 0)),
            pl.BlockSpec((1, inner, STATE_DIM), lambda s: (s, 0, 0)),
            pl.BlockSpec((8, inner), lambda s: (0, 0)),
        ],
        out_shape=[
            jax.ShapeDtypeStruct((slots, extent, inner), f32),
            jax.ShapeDtypeStruct((zs, slots, rows, inner), bf16),
            jax.ShapeDtypeStruct((slots, inner, STATE_DIM), f32),
            jax.ShapeDtypeStruct((8, inner), f32),
        ],
        compiler_params=kernel_params(48),
        cost_estimate=taking(9, zs * slots * rows),
        name="mixer_unmix",
    )(gn, y, z, rw, dl, tok, gain)


def pairs_kernel(inner, xs_ref, rw_ref, dl_ref, gy_ref, gx_ref, grw_ref, gdl_ref, cols_buf):
    extent = gy_ref.shape[1]
    write = split_parts(rw_ref[0, :, :STATE_DIM])
    read = split_parts(rw_ref[0, :, STATE_DIM:])
    step = dl_ref[0, :, 0:LANES]
    log_sum = dl_ref[0, :, LANES:]
    log_t = log_sum.T
    gy_parts, xs_parts = split_parts(gy_ref[0]), split_parts(xs_ref[0])
    scores_t = dot_split(write, read, NT)
    later = lax.broadcasted_iota(jnp.int32, (extent, extent), 1) >= lax.broadcasted_iota(
        jnp.int32, (extent, extent), 0
    )
    lane = lax.broadcasted_iota(jnp.int32, (extent, LANES), 1)
    score_grad_t = jnp.zeros((extent, extent), f32)
    step_direct = jnp.zeros((extent, LANES), f32)
    cols_buf[...] = jnp.zeros_like(cols_buf)
    for head in range(inner // HEAD_DIM):
        cols = slice(head * HEAD_DIM, (head + 1) * HEAD_DIM)
        gap_t = log_t[head : head + 1, :] - log_sum[:, head : head + 1]
        decay_t = jnp.exp(jnp.where(later, gap_t, -jnp.inf))
        step_col = step[:, head : head + 1]
        pair_t = dot_split([x[:, cols] for x in xs_parts], [g[:, cols] for g in gy_parts], NT)
        both_t = decay_t * pair_t
        score_grad_t = score_grad_t + both_t * step_col
        weight_t = both_t * scores_t
        step_direct = step_direct + jnp.where(lane == head, jnp.sum(weight_t, axis=1, keepdims=True), 0.0)
        cols_buf[head : head + 1, :] = jnp.sum(weight_t * step_col, axis=0, keepdims=True)
        gx_ref[0, :, cols] = dot((decay_t * scores_t * step_col).astype(bf16), gy_parts[0][:, cols], NN)
    score_parts = split_parts(score_grad_t)
    grw_ref[0, :, :STATE_DIM] = dot_split(score_parts, read, NN)
    grw_ref[0, :, STATE_DIM:] = dot_split(score_parts, write, TN)
    gdl_ref[0, :, 0:LANES] = step_direct
    gdl_ref[0, :, LANES:] = cols_buf[...].T - step * step_direct


def mixer_pairs(xs, rw, dl, gy):
    slots, extent, inner = xs.shape
    wide = pl.BlockSpec((1, extent, inner), lambda s: (s, 0, 0))
    two = pl.BlockSpec((1, extent, 2 * LANES), lambda s: (s, 0, 0))
    return pl.pallas_call(
        functools.partial(pairs_kernel, inner),
        grid=(slots,),
        in_specs=[wide, two, two, wide],
        out_specs=[wide, two, two],
        out_shape=[
            jax.ShapeDtypeStruct((slots, extent, inner), f32),
            jax.ShapeDtypeStruct((slots, extent, 2 * STATE_DIM), f32),
            jax.ShapeDtypeStruct((slots, extent, 2 * LANES), f32),
        ],
        scratch_shapes=[pltpu.VMEM((LANES, extent), f32)],
        compiler_params=kernel_params(48),
        cost_estimate=taking(42, slots * extent),
        name="mixer_pairs",
    )(xs, rw, dl, gy)


def back_kernel(
    inner, v_ref, halo_ref, cw_ref, hp_ref, skip_ref, rw_ref, dl_ref, gy_ref, gx_ref, grw_ref, gdl_ref, h_ref, gh_ref,
    gv_ref, gbc_ref, gp_ref, gc_ref, ghp_ref, padded, gpad,
):
    extent = gy_ref.shape[1]
    zs, _, rows, _ = v_ref.shape
    width = padded.shape[1]
    heads = inner // HEAD_DIM
    first = pl.program_id(0) == 0
    pre = conv_of(v_ref, halo_ref, cw_ref, padded)
    logistic = jax.nn.sigmoid(pre)
    slope = logistic * (1.0 + pre * (1.0 - logistic))
    xs = pre[:, :inner] * logistic[:, :inner]
    write_low = rw_ref[0, :, :STATE_DIM].astype(bf16)
    read_low = rw_ref[0, :, STATE_DIM:].astype(bf16)
    raw, step = step_sizes(v_ref, hp_ref, width, extent)
    rate = jnp.exp(hp_ref[0:1, :])
    log_sum = dl_ref[0, :, LANES:]
    gy = gy_ref[0]
    step_direct = gdl_ref[0, :, 0:LANES]
    sums = head_sums(inner)
    spread = head_spread(inner)
    last = log_sum[extent - 1 : extent, :]
    tail_decay = jnp.exp(last - log_sum)
    tail = dot(tail_decay * step, spread, NN, highest)
    grown = dot(jnp.exp(log_sum), spread, NN, highest)
    gh = gh_ref[0]
    h_in = h_ref[0]
    gh_parts, h_parts = split_parts(gh), split_parts(h_in)
    tail_in = dot(write_low, gh_parts[0], NT)
    tail_direct = tail_decay * dot(xs * tail_in, sums, NN, highest)
    tail_weight = tail_direct * step
    state_part = grown * dot(read_low, h_parts[0], NT)
    state_weight = dot(gy * state_part, sums, NN, highest)
    kept = dot(sums, jnp.sum(gh * h_in, axis=1, keepdims=True) * jnp.ones((1, LANES), f32), TN, highest).T[0:1, :]
    log_grad = gdl_ref[0, :, LANES:] + state_weight - tail_weight
    end_grad = jnp.sum(tail_weight, axis=0, keepdims=True) + jnp.exp(last) * kept
    rate_arg_grad = dot(lower_ones(extent), log_grad, TN, highest) + end_grad
    step_grad = step_direct + tail_direct - rate * rate_arg_grad
    raw_grad = step_grad * jax.nn.sigmoid(raw)
    xs_grad = gx_ref[0] + tail * tail_in + skip_ref[3:4, :] * gy
    write_grad = grw_ref[0, :, :STATE_DIM] + dot_split(split_parts(tail * xs), gh_parts, NN)
    read_grad = grw_ref[0, :, STATE_DIM:] + dot_split(split_parts(grown * gy), h_parts, NN)
    valid_lane = lax.broadcasted_iota(jnp.int32, (1, LANES), 1) < heads
    rate_grad = jnp.where(valid_lane, jnp.sum(-step * rate * rate_arg_grad, axis=0, keepdims=True), 0.0)
    raw_grad = jnp.where(valid_lane, raw_grad, 0.0)
    skip_grad = jnp.sum(dot(gy * xs, sums, NN, highest), axis=0, keepdims=True)

    @pl.when(first)
    def _():
        gc_ref[...] = jnp.zeros_like(gc_ref)
        ghp_ref[...] = jnp.zeros_like(ghp_ref)

    ghp_ref[0:1, :] += rate_grad
    ghp_ref[1:2, :] += jnp.sum(raw_grad, axis=0, keepdims=True)
    ghp_ref[2:3, :] += skip_grad
    gpad[0:8, :] = jnp.zeros((8, width), f32)
    gpad[extent + 8 :, :] = jnp.zeros((8, width), f32)
    gpad[8 : extent + 8, 0:inner] = xs_grad * slope[:, 0:inner]
    gpad[8 : extent + 8, inner : inner + STATE_DIM] = write_grad * slope[:, inner : inner + STATE_DIM]
    gpad[8 : extent + 8, inner + STATE_DIM :] = read_grad * slope[:, inner + STATE_DIM :]
    back = jnp.zeros((extent, width), f32)
    before = jnp.zeros((8, width), f32)
    pre_grad = gpad[8 : extent + 8, :]
    for tap in range(CONV_WIDTH):
        ahead = CONV_WIDTH - 1 - tap
        weight = cw_ref[tap : tap + 1, :]
        back = back + weight * gpad[8 + ahead : 8 + ahead + extent, :]
        before = before + weight * gpad[ahead : 8 + ahead, :]
        gc_ref[tap : tap + 1, :] += jnp.sum(pre_grad * padded[5 + tap : 5 + tap + extent, :], axis=0, keepdims=True)
    gc_ref[CONV_WIDTH : CONV_WIDTH + 1, :] += jnp.sum(pre_grad, axis=0, keepdims=True)
    gp_ref[0] = before
    gv_ref[:, :, :, 0:inner] = back[:, :inner].astype(bf16).reshape(zs, 1, rows, inner)
    gbc_ref[...] = back[:, inner:].reshape(zs, 1, rows, width - inner)
    gv_ref[:, :, :, inner:] = raw_grad.astype(bf16).reshape(zs, 1, rows, LANES)


def mixer_back(v, halo, cw, hp, skip, rw, dl, gy, gx, grw, gdl, h_in, gh):
    zs, slots, rows, cols = v.shape
    extent = zs * rows
    inner = gy.shape[2]
    width = cw.shape[1]
    wide = pl.BlockSpec((1, extent, inner), lambda s: (s, 0, 0))
    two = pl.BlockSpec((1, extent, 2 * LANES), lambda s: (s, 0, 0))
    state = pl.BlockSpec((1, inner, STATE_DIM), lambda s: (s, 0, 0))
    return pl.pallas_call(
        functools.partial(back_kernel, inner),
        grid=(slots,),
        in_specs=[
            pl.BlockSpec((zs, 1, rows, cols), lambda s: (0, s, 0, 0)),
            pl.BlockSpec((1, 8, width), lambda s: (s, 0, 0)),
            pl.BlockSpec(cw.shape, lambda s: (0, 0)),
            pl.BlockSpec(hp.shape, lambda s: (0, 0)),
            pl.BlockSpec(skip.shape, lambda s: (0, 0)),
            two,
            two,
            wide,
            wide,
            two,
            two,
            state,
            state,
        ],
        out_specs=[
            pl.BlockSpec((zs, 1, rows, inner + LANES), lambda s: (0, s, 0, 0)),
            pl.BlockSpec((zs, 1, rows, 2 * STATE_DIM), lambda s: (0, s, 0, 0)),
            pl.BlockSpec((1, 8, width), lambda s: (s, 0, 0)),
            pl.BlockSpec((8, width), lambda s: (0, 0)),
            pl.BlockSpec((8, LANES), lambda s: (0, 0)),
        ],
        out_shape=[
            jax.ShapeDtypeStruct((zs, slots, rows, inner + LANES), bf16),
            jax.ShapeDtypeStruct((zs, slots, rows, 2 * STATE_DIM), f32),
            jax.ShapeDtypeStruct((slots, 8, width), f32),
            jax.ShapeDtypeStruct((8, width), f32),
            jax.ShapeDtypeStruct((8, LANES), f32),
        ],
        scratch_shapes=[
            pltpu.VMEM((extent + 8, width), f32),
            pltpu.VMEM((extent + 16, width), f32),
        ],
        compiler_params=kernel_params(56),
        cost_estimate=taking(18, zs * slots * rows),
        name="mixer_back",
    )(v, halo, cw, hp, skip, rw, dl, gy, gx, grw, gdl, h_in, gh)


def expert_kernel(
    n_ref, g_ref, mask_ref, router_ref, up_ref, down_ref,
    moe_ref, back_ref, logit_ref, act_ref, hid_ref, moe_sum, back_sum, gates_buf, gate_grad,
):
    pair = pl.program_id(0)
    pairs = pl.num_programs(0)
    tokens = n_ref.shape[0]
    lane = lax.broadcasted_iota(jnp.int32, (tokens, LANES), 1)
    half = up_ref.shape[3] // 2

    @pl.when(pair == 0)
    def _():
        logits = dot(n_ref[...], router_ref[...], NN)
        chosen = mask_ref[...] > 0.0
        logits = jnp.where(chosen, logits, -jnp.inf)
        powers = jnp.exp(logits - jnp.max(logits, axis=1, keepdims=True))
        gates = powers / jnp.sum(powers, axis=1, keepdims=True)
        gates_buf[...] = jnp.where(lane < EXPERTS, gates, 1.0)
        moe_sum[...] = jnp.zeros_like(moe_sum)
        back_sum[...] = jnp.zeros_like(back_sum)
        gate_grad[...] = jnp.zeros_like(gate_grad)

    depth = up_ref.shape[0] * up_ref.shape[2]
    down = down_ref[...].reshape(depth, 2 * half)
    n_val = n_ref[...]
    gates = gates_buf[...]
    act_back = dot(g_ref[...], down, NN)
    ups = [up_ref[:, member].reshape(depth, 2 * half) for member in range(2)]
    for member in range(2):
        hidden = dot(n_val, ups[member], NN)
        gate_part, up_part = hidden[:, :half], hidden[:, half:]
        logistic = jax.nn.sigmoid(gate_part)
        silu = gate_part * logistic
        act = (silu * up_part).astype(bf16).astype(f32)
        own = lane == 2 * pair + member
        gate = jnp.sum(jnp.where(own, gates, 0.0), axis=1, keepdims=True)
        part = act_back[:, member * half : (member + 1) * half]
        gate_grad[...] += jnp.where(own, jnp.sum(act * part, axis=1, keepdims=True), 0.0)
        act_ref[0, :, member * half : (member + 1) * half] = (gate * act).astype(bf16)
        part = part * gate
        first_col = 2 * member * half
        hid_ref[0, :, first_col : first_col + half] = (part * up_part * (logistic * (1.0 + gate_part * (1.0 - logistic)))).astype(bf16)
        hid_ref[0, :, first_col + half : first_col + 2 * half] = (part * silu).astype(bf16)
    moe_sum[...] += dot(act_ref[0], down, NT)
    back_sum[...] += dot(hid_ref[0], jnp.concatenate(ups, axis=1), NT)

    @pl.when(pair == pairs - 1)
    def _():
        gates_in = jnp.where(lane < EXPERTS, gates, 0.0)
        grads = gates_in * gate_grad[...]
        logit_grad = (grads - gates_in * jnp.sum(grads, axis=1, keepdims=True)).astype(bf16)
        logit_ref[...] = logit_grad
        back_ref[...] = (back_sum[...] + dot(logit_grad, router_ref[...], NT)).astype(bf16)
        moe_ref[...] = moe_sum[...].astype(bf16)


def experts(n_two, g_moe, mask, router, weights):
    tokens, width = n_two.shape
    count, blocks, rows, cols = weights.shape
    pairs = blocks // 3
    down_at = 2 * pairs
    return pl.pallas_call(
        expert_kernel,
        grid=(pairs,),
        in_specs=[
            pl.BlockSpec((tokens, width), lambda p: (0, 0)),
            pl.BlockSpec((tokens, width), lambda p: (0, 0)),
            pl.BlockSpec((tokens, LANES), lambda p: (0, 0)),
            pl.BlockSpec((width, LANES), lambda p: (0, 0)),
            pl.BlockSpec((count, 2, rows, cols), lambda p: (0, p, 0, 0)),
            pl.BlockSpec((count, 1, rows, cols), lambda p: (0, down_at + p, 0, 0)),
        ],
        out_specs=[
            pl.BlockSpec((tokens, width), lambda p: (0, 0)),
            pl.BlockSpec((tokens, width), lambda p: (0, 0)),
            pl.BlockSpec((tokens, LANES), lambda p: (0, 0)),
            pl.BlockSpec((1, tokens, cols), lambda p: (p, 0, 0)),
            pl.BlockSpec((1, tokens, 2 * cols), lambda p: (p, 0, 0)),
        ],
        out_shape=[
            jax.ShapeDtypeStruct((tokens, width), bf16),
            jax.ShapeDtypeStruct((tokens, width), bf16),
            jax.ShapeDtypeStruct((tokens, LANES), bf16),
            jax.ShapeDtypeStruct((pairs, tokens, cols), bf16),
            jax.ShapeDtypeStruct((pairs, tokens, 2 * cols), bf16),
        ],
        scratch_shapes=[
            pltpu.VMEM((tokens, width), f32),
            pltpu.VMEM((tokens, width), f32),
            pltpu.VMEM((tokens, LANES), f32),
            pltpu.VMEM((tokens, LANES), f32),
        ],
        compiler_params=kernel_params(60),
        cost_estimate=taking(72, tokens),
        name="experts",
    )(n_two, g_moe, mask, router, weights, weights)


def expert_grad_kernel(up_blocks, chunks, *refs):
    n_refs, g_refs, h_refs, a_refs = (refs[i * chunks : (i + 1) * chunks] for i in range(4))
    out_ref = refs[4 * chunks]
    block = pl.program_id(0)
    count, _, rows, cols = out_ref.shape

    def summed(lefts, rights):
        total = dot(lefts[0][...], rights[0][0], NN)
        for left, right in zip(lefts[1:], rights[1:]):
            total = total + dot(left[...], right[0], NN)
        out_ref[...] = total.astype(bf16).reshape(count, 1, rows, cols)

    @pl.when(block < up_blocks)
    def _():
        summed(n_refs, h_refs)

    @pl.when(block >= up_blocks)
    def _():
        summed(g_refs, a_refs)


def expert_grads(n_list, g_list, hid_list, act_list, count):
    chunks = len(n_list)
    width, tokens = n_list[0].shape
    pairs, _, cols = act_list[0].shape
    ups = 2 * pairs
    blocks = 3 * pairs
    whole = pl.BlockSpec((width, tokens), lambda b: (0, 0))
    hid_at = lambda b: (jnp.minimum(b, ups - 1) // 2, 0, jnp.minimum(b, ups - 1) % 2)
    return pl.pallas_call(
        functools.partial(expert_grad_kernel, ups, chunks),
        grid=(blocks,),
        in_specs=[whole] * (2 * chunks)
        + [pl.BlockSpec((1, tokens, cols), hid_at)] * chunks
        + [pl.BlockSpec((1, tokens, cols), lambda b: (jnp.maximum(b - ups, 0), 0, 0))] * chunks,
        out_specs=pl.BlockSpec((count, 1, width // count, cols), lambda b: (0, b, 0, 0)),
        out_shape=jax.ShapeDtypeStruct((count, blocks, width // count, cols), bf16),
        compiler_params=kernel_params(48),
        cost_estimate=taking(40, chunks * tokens),
        name="expert_grads",
    )(*n_list, *g_list, *hid_list, *act_list)


def body(
    block_input,
    out_grad,
    lengths,
    routes,
    norm1_gain,
    w_zx,
    w_bc,
    w_dt,
    conv_x,
    conv_bc,
    head_params,
    gate_gain,
    w_out,
    norm2_gain,
    w_router,
    w_gu,
    w_dn,
    s_gu,
    s_dn,
):
    zs = lax.axis_size("tensor")
    pieces = lax.axis_size("dp")
    own = lax.axis_index("tensor")
    wide_index = lax.axis_index("dp")
    rows = block_input.shape[0]
    piece_rows = rows * zs
    heads = HEAD_COUNT // zs
    inner = INNER_DIM // zs
    width = inner + 2 * STATE_DIM
    shard = D_MODEL // pieces
    half = w_gu.shape[3]
    rim = CONV_WIDTH - 1
    per = SLOT_COUNT // CHUNKS
    tokens = per * rows
    chunk_ids = range(CHUNKS)

    enter_shard = jnp.concatenate(
        [w_zx[:, 1], w_bc, jnp.pad(w_dt, ((0, 0), (0, LANES - heads)))], axis=1
    )
    side_shard = jnp.concatenate(
        [w_zx[:, 0], w_out.T, jnp.pad(w_router, ((0, 0), (0, LANES - EXPERTS)))], axis=1
    )
    expert_shard = jnp.concatenate(
        [
            w_gu.reshape(EXPERTS, shard, 2 * half),
            s_gu.reshape(shard, 2, 2, half).transpose(2, 0, 1, 3).reshape(2, shard, 2 * half),
            w_dn.reshape(EXPERTS // 2, 2 * half, shard).transpose(0, 2, 1),
            s_dn.T[None],
        ],
        axis=0,
    )

    def by_slot(values):
        return jnp.transpose(values, (1, 0, 2))

    def part(values, c):
        return values[c * per : (c + 1) * per].reshape((tokens,) + values.shape[2:])

    u_slots = by_slot(block_input)
    u_low = [row_major(part(u_slots, c)) for c in chunk_ids]
    u_all = [line_gather(u_low[c]) for c in chunk_ids]
    full_enter = weight_gather(enter_shard).reshape(D_MODEL, width + LANES)
    gains = jnp.stack([norm1_gain, norm2_gain], axis=1).astype(f32)
    gains = lax.all_gather(gains, "dp", axis=0, tiled=True)
    gain_one, gain_two = gains[:, 0], gains[:, 1]
    full_side = weight_gather(side_shard).reshape(D_MODEL, 2 * inner + LANES)
    full_z, full_out, full_router = full_side[:, :inner], full_side[:, inner : 2 * inner], full_side[:, 2 * inner :]
    full_expert = weight_gather(expert_shard)

    positions = wide_index * piece_rows + own * rows + jnp.arange(rows, dtype=jnp.int32)
    valid = (positions[None, :] < lengths[:, None]).astype(f32)[:, :, None]
    grad_slots = by_slot(out_grad).astype(f32) * valid

    conv_w = jnp.pad(jnp.concatenate([conv_x, conv_bc], axis=1), ((0, 8 - CONV_WIDTH - 1), (0, 0)))
    hp = jnp.pad(head_params, ((0, 5), (0, LANES - heads)))
    skip = jnp.pad(jnp.repeat(head_params[2], HEAD_DIM)[None], ((3, 4), (0, 0)))
    gain_row = gate_gain[None]

    hot = jnp.sum(
        (routes[..., None] == jnp.arange(LANES, dtype=jnp.int32)).astype(f32), axis=2
    )
    hot = jnp.transpose(hot.reshape(zs, rows, SLOT_COUNT, LANES), (0, 2, 1, 3))

    def flat(values):
        return values.reshape((zs * tokens,) + values.shape[2:])

    def in_slots(values):
        return values.reshape((zs, per, rows) + values.shape[1:])

    u = [row_major(u_low[c].astype(f32)) for c in chunk_ids]
    valid_c = [part(valid, c) for c in chunk_ids]
    grad_c = [row_major(part(grad_slots, c)) for c in chunk_ids]
    n_one, v, z, halo, entered = [], [], [], [], []
    for c in chunk_ids:
        n_one.append(row_major(rms_scale(flat(u_all[c]).astype(f32), gain_one).astype(bf16)))
        v.append(in_slots(dot(n_one[c], full_enter, NN)))
        rim_rows = in_slots(n_one[c])[zs - 1, :, rows - rim :]
        prior = dot(passed_along(rim_rows, "dp", 1).reshape(per * rim, D_MODEL), full_enter[:, :width], NN)
        halo.append(jnp.pad(prior.reshape(per, rim, width), ((0, 0), (8 - rim, 0), (0, 0))))
        entered.append(mixer_enter(v[c], halo[c], conv_w, hp, inner))
    g_moe = [line_gather(after(grad_c[c].astype(bf16), u_all[CHUNKS - 1])) for c in chunk_ids]
    resid, mixed_all, y_all, h_all, decay_all, inv_alls, gg_all, n_two = [], [], [], [], [], [], [], []
    for c in chunk_ids:
        xs, rw, dl, s_local = entered[c]
        yi = mixer_inner(xs, rw, dl)
        z.append(in_slots(dot(n_one[c], full_z, NN)))
        h_in, decay = states_forward(s_local, dl[:, piece_rows - 1, LANES : LANES + heads])
        h_in = after(h_in, g_moe[c])
        y, gg, squares = mixer_leave(yi, xs, rw, dl, h_in, z[c], skip, gain_row)
        product = dot(flat(gg.reshape(zs, tokens, inner)), full_out, NT).astype(bf16)
        mixed = line_scatter(product.reshape(zs, tokens, D_MODEL))
        square_sum = lax.psum(squares[:, :, 0], "tensor")
        inv_all = lax.rsqrt(square_sum / INNER_DIM + norm_eps)
        mixed = mixed * lax.dynamic_slice_in_dim(inv_all, own * rows, rows, 1).reshape(tokens, 1)
        resid.append(row_major(u[c] + mixed))
        mixed_all.append(mixed)
        y_all.append(y)
        h_all.append(h_in)
        decay_all.append(decay)
        inv_alls.append(inv_all)
        gg_all.append(gg)
        n_two.append(flat(line_gather(row_major(rms_scale(resid[c], gain_two).astype(bf16)))))
    g_moe = [flat(g_moe[c]) for c in chunk_ids]
    moe_part, back_part, logit_grads, acts, hids = [], [], [], [], []
    for c in chunk_ids:
        mask = hot[:, c * per : (c + 1) * per].reshape(zs * tokens, LANES)
        results = experts(n_two[c], g_moe[c], mask, full_router, full_expert)
        moe_part.append(results[0].reshape(zs, tokens, D_MODEL))
        back_part.append(results[1].reshape(zs, tokens, D_MODEL))
        logit_grads.append(results[2])
        acts.append(results[3])
        hids.append(results[4])

    def norm_back(values, gain_vec, grads):
        return jax.vjp(rms_scale, values, gain_vec)[1](grads)

    resid_grad, g_mixed, gain_two_grad = [], [], 0.0
    unmixed, pairs, gate_gain_grad = [], [], 0.0
    for c in chunk_ids:
        n_two_grad = line_scatter_steps(back_part[c])
        from_norm, gain_grad = norm_back(resid[c], gain_two, n_two_grad)
        gain_two_grad = gain_two_grad + gain_grad
        resid_grad.append(row_major(grad_c[c] + from_norm))
        low = resid_grad[c].astype(bf16)
        g_mixed.append(flat(line_gather(low)))
        grad = in_slots(dot(g_mixed[c], full_out, NN))
        xs, rw, dl, _ = entered[c]
        inv_all = inv_alls[c]
        y_like = jnp.transpose(y_all[c].reshape(per, zs, rows, inner), (1, 0, 2, 3))
        cross = jnp.sum(grad * gain_row * y_like * jax.nn.silu(z[c]), axis=-1)
        cross = lax.psum(jnp.transpose(cross, (1, 0, 2)).reshape(per, piece_rows), "tensor")
        tok = jnp.stack([inv_all, cross * (inv_all * inv_all * inv_all) / INNER_DIM], axis=-1)
        gy, gz, g_local, gg_grad = mixer_unmix(grad, y_all[c], z[c], rw, dl, tok, gain_row)
        gate_gain_grad = gate_gain_grad + gg_grad[0]
        unmixed.append((gy, gz, g_local))
        pairs.append(mixer_pairs(xs, rw, dl, gy))

    expert_grad = weight_scatter(
        expert_grads([n.T for n in n_two], [g.T for g in g_moe], hids, acts, pieces)
    )
    moe = [line_scatter(after(moe_part[c], g_mixed[CHUNKS - 1])) for c in chunk_ids]
    output = [resid[c] + moe[c] for c in chunk_ids]
    stat_terms = sum(
        jnp.stack(
            [
                jnp.sum(valid_c[c] * output[c] * output[c]),
                jnp.sum(valid_c[c] * mixed_all[c] * mixed_all[c]),
                jnp.sum(valid_c[c] * moe[c] * moe[c]),
            ]
        )
        for c in chunk_ids
    )
    router_grad = sum(dot(n_two[c], logit_grads[c], TN)[:, :EXPERTS] for c in chunk_ids)

    def rows_of(values):
        return jnp.concatenate([v.reshape(zs * tokens, -1) for v in values], axis=0)

    inv_rows = [
        jnp.transpose(inv_alls[c].reshape(per, zs, rows), (1, 0, 2)).reshape(zs * tokens, 1) for c in chunk_ids
    ]
    scaled = [(g_mixed[c].astype(f32) * inv_rows[c]).astype(bf16) for c in chunk_ids]
    out_w_grad = dot(rows_of(scaled), rows_of(gg_all), TN).astype(bf16)
    n_rows = rows_of(n_one)
    z_w_grad = dot(n_rows, rows_of([unmixed[c][1] for c in chunk_ids]), TN).astype(bf16)

    v_grads, bc_grads, conv_grad, head_grad = [], [], 0.0, 0.0
    full_x = jnp.concatenate([full_enter[:, :inner], full_enter[:, width:]], axis=1)
    full_bc = full_enter[:, inner:width]
    full_bc = jnp.concatenate([full_bc, full_bc], axis=1)
    for c in chunk_ids:
        gy, gz, g_local = unmixed[c]
        xs, rw, dl, _ = entered[c]
        gh = after(states_backward(g_local, decay_all[c]), moe[c])
        gv, gbc, g_rim, gc, ghp = mixer_back(
            v[c], halo[c], conv_w, hp, skip, rw, dl, gy, *pairs[c], h_all[c], gh
        )
        conv_grad = conv_grad + gc
        head_grad = head_grad + ghp
        following = passed_along(g_rim[:, 8 - rim :].astype(bf16), "dp", -1).astype(f32)
        edge = gv[zs - 1, :, rows - rim :, :inner].astype(f32) + following[:, :, :inner]
        gv = lax.dynamic_update_slice(gv, edge.astype(bf16)[None], (zs - 1, 0, rows - rim, 0))
        edge = gbc[zs - 1, :, rows - rim :] + following[:, :, inner:]
        gbc = lax.dynamic_update_slice(gbc, edge[None], (zs - 1, 0, rows - rim, 0))
        v_grads.append(gv)
        bc_grads.append(jnp.concatenate(split_parts(gbc), axis=-1))
    u_grad, n_parts, gain_one_grad = [], [], 0.0
    for c in chunk_ids:
        n_grad = (
            dot(unmixed[c][1].reshape(zs * tokens, inner), full_z, NT)
            + dot(v_grads[c].reshape(zs * tokens, inner + LANES), full_x, NT)
            + dot(bc_grads[c].reshape(zs * tokens, 4 * STATE_DIM), full_bc, NT)
        )
        every = flat(u_all[c]).astype(f32)
        scale = lax.rsqrt(jnp.mean(every * every, axis=-1, keepdims=True) + norm_eps)
        gain_one_grad = gain_one_grad + jnp.sum(n_grad * (every * scale), axis=0)
        n_parts.append(n_grad.astype(bf16))
        total = line_scatter(n_parts[c].reshape(zs, tokens, D_MODEL))
        u_grad.append(resid_grad[c] + norm_back(u[c], gain_one, total)[0])
    v_grads[0] = after(v_grads[0], expert_grad, *n_parts)
    bc_grads[0] = after(bc_grads[0], *n_parts)
    enter_w_grad = dot(n_rows, rows_of(v_grads), TN).astype(bf16)
    bc_w_grad = dot(n_rows, rows_of(bc_grads), TN)
    bc_w_grad = bc_w_grad[:, : 2 * STATE_DIM] + bc_w_grad[:, 2 * STATE_DIM :]
    mixer_grad = weight_scatter(
        jnp.concatenate([z_w_grad, out_w_grad, enter_w_grad], axis=1).reshape(pieces, shard, 3 * inner + LANES)
    ).astype(f32)

    def to_shares(values, dim):
        size = values.shape[dim] // (pieces * zs)
        values = jnp.moveaxis(values, dim, 0).reshape(pieces, zs, size, -1)
        return jnp.moveaxis(values, 3, 2).reshape(pieces, zs, -1)

    column = own * inner
    conv_x_full = lax.dynamic_update_slice(
        jnp.zeros((CONV_WIDTH + 1, INNER_DIM), f32), conv_grad[: CONV_WIDTH + 1, :inner], (jnp.int32(0), column)
    )
    gate_full = lax.dynamic_update_slice(jnp.zeros((INNER_DIM,), f32), gate_gain_grad, (column,))
    small = [
        (gain_one_grad, 0),
        (conv_x_full, 1),
        (conv_grad[: CONV_WIDTH + 1, inner:], 1),
        (gate_full, 0),
        (gain_two_grad, 0),
        (router_grad, 0),
    ]
    shares = [to_shares(values, dim) for values, dim in small]
    sizes = [share.shape[2] for share in shares]
    shares = jnp.concatenate(shares, axis=2)
    length = shares.shape[2]
    shares = jnp.pad(shares, ((0, 0), (0, 0), (0, -length % (8 * LANES))))
    wide_share = bc_w_grad.reshape(pieces, zs, -1, LANES)
    shares = jnp.concatenate([wide_share, shares.reshape(pieces, zs, -1, LANES)], axis=2)
    shares = jnp.sum(lax.all_to_all(shares, "dp", 0, 0), axis=0)
    shares = jnp.sum(lax.all_to_all(shares, "tensor", 0, 0), axis=0)
    bc_lines = wide_share.shape[2]
    bc_grad = shares[:bc_lines].reshape(-1, 2 * STATE_DIM)
    shares = shares[bc_lines:].reshape(-1)
    ends = [sum(sizes[: k + 1]) for k in range(len(sizes))]
    took = []
    for (values, dim), size, end in zip(small, sizes, ends):
        share = shares[end - size : end]
        if values.ndim == 2:
            other = values.shape[1 - dim]
            share = share.reshape(other, size // other)
            share = share if dim == 1 else share.T
        took.append(share)
    tile = jnp.zeros((8, LANES), f32)
    tile = tile.at[:3, :heads].set(head_grad[:3, :heads]).at[3, :3].set(stat_terms)
    tile = jnp.sum(lax.all_gather(tile, "dp"), axis=0)
    tiles = lax.all_gather(tile, "tensor")
    head_sum = jnp.transpose(tiles[:, :3, :heads], (1, 0, 2)).reshape(3, HEAD_COUNT)
    stat_sum = jnp.sum(tiles[:, 3, :3], axis=0)
    stats = jnp.sqrt(stat_sum / (jnp.sum(lengths).astype(f32) * D_MODEL))

    def placed_back(values):
        whole = jnp.concatenate([value.astype(bf16).reshape(per, rows, D_MODEL) for value in values], axis=0)
        return jnp.transpose(whole, (1, 0, 2))

    expert_grad = expert_grad.astype(f32)
    ups, downs = EXPERTS + 2, EXPERTS // 2
    z_part, out_part = mixer_grad[:, :inner], mixer_grad[:, inner : 2 * inner]
    x_part, dt_part = mixer_grad[:, 2 * inner : 3 * inner], mixer_grad[:, 3 * inner :]
    return (
        placed_back(output),
        placed_back(u_grad),
        took[0],
        jnp.stack([z_part, x_part], axis=1),
        bc_grad,
        dt_part[:, :heads],
        took[1],
        took[2],
        head_sum,
        took[3],
        out_part.T,
        took[4],
        took[5],
        expert_grad[:EXPERTS].reshape(EXPERTS, shard, 2, half),
        expert_grad[ups : ups + downs].transpose(0, 2, 1).reshape(EXPERTS, half, shard),
        expert_grad[EXPERTS:ups].reshape(2, shard, 2, half).transpose(1, 2, 0, 3).reshape(shard, 2, 2 * half),
        expert_grad[ups + downs].T,
        stats,
    )


def solution(mesh):
    both = ("dp", "tensor")
    placed = (
        P(both, None, None),
        P(both, None, None),
        P(),
        P("dp", None, None),
        P("dp"),
        P("dp", None, "tensor"),
        P("dp", None),
        P("dp", "tensor"),
        P(None, "tensor"),
        P(),
        P(None, "tensor"),
        P("tensor"),
        P("tensor", "dp"),
        P("dp"),
        P("dp", None),
        P(None, "dp", None, "tensor"),
        P(None, "tensor", "dp"),
        P("dp", None, "tensor"),
        P("tensor", "dp"),
    )
    return jax.shard_map(
        body,
        mesh=mesh,
        in_specs=placed,
        out_specs=(
            P(both, None, None),
            P(both, None, None),
            P(both),
            P("dp", None, "tensor"),
            P(both, None),
            P("dp", "tensor"),
            P(None, both),
            P(None, both),
            P(),
            P(both),
            P("tensor", "dp"),
            P(both),
            P(both, None),
            P(None, "dp", None, "tensor"),
            P(None, "tensor", "dp"),
            P("dp", None, "tensor"),
            P("tensor", "dp"),
            P(),
        ),
        check_vma=False,
    )
```

```python
import functools

import jax
import jax.numpy as jnp
from jax import lax
from jax.experimental import pallas as pl
from jax.experimental.layout import Layout, with_layout_constraint
from jax.experimental.pallas import tpu as pltpu
from jax.sharding import PartitionSpec as P

D_MODEL = 1536
HEAD_COUNT = 48
HEAD_DIM = 64
STATE_DIM = 128
CONV_WIDTH = 4
TOP_K = 6
EXPERTS = 16
SLOT_COUNT = 4
INNER_DIM = 3072
LANES = 128
CHUNKS = 1

norm_eps = 1e-05
highest = lax.Precision.HIGHEST
f32 = jnp.float32
bf16 = jnp.bfloat16


def passed_along(value, axis, steps):
    count = lax.axis_size(axis)
    first, last = (max(0, -steps), min(count, count - steps))
    return lax.ppermute(value, axis, [(source, source + steps) for source in range(first, last)])


def row_major(value):
    return with_layout_constraint(value, Layout(major_to_minor=tuple(range(value.ndim))))


def line_gather(value):
    size = lax.axis_size("tensor")
    return [value] + [
        row_major(lax.ppermute(row_major(value), "tensor", [(a, (a - step) % size) for a in range(size)]))
        for step in range(1, size)
    ]


def line_parts(block_of):
    size = lax.axis_size("tensor")
    return [block_of(0)] + [
        lax.ppermute(row_major(block_of(step)), "tensor", [(a, (a + step) % size) for a in range(size)])
        for step in range(1, size)
    ]


def summed(parts):
    total = parts[0].astype(f32)
    for part in parts[1:]:
        total = total + part.astype(f32)
    return row_major(total)


def in_order(blocks):
    size = len(blocks)
    own = lax.axis_index("tensor")
    whole = jnp.zeros((size,) + blocks[0].shape, blocks[0].dtype)
    for k in range(size):
        whole = lax.dynamic_update_index_in_dim(whole, blocks[k], (own + k) % size, 0)
    return whole


def by_distance(whole):
    size = whole.shape[0]
    own = lax.axis_index("tensor")
    return lambda k: lax.dynamic_index_in_dim(whole, (own + k) % size, 0, False)


def weight_gather(shard):
    return lax.all_gather(shard, "dp", axis=0, tiled=False)


def weight_scatter(grads):
    return row_major(lax.psum_scatter(grads.astype(bf16), "dp", scatter_dimension=0, tiled=False))


def rms_scale(values, gain_vec):
    return (
        values * lax.rsqrt(jnp.mean(values * values, axis=-1, keepdims=True) + norm_eps) * gain_vec
    )


def silu_slope(values):
    logistic = jax.nn.sigmoid(values)
    return logistic * (1.0 + values * (1.0 - logistic))


def dot(a, b, dims, precision=None):
    return lax.dot_general(a, b, (dims, ((), ())), precision=precision, preferred_element_type=f32)


def split_parts(values):
    upper = values.astype(bf16)
    return upper, (values - upper.astype(f32)).astype(bf16)


def dot_split(a, b, dims):
    return dot(a[0], b[0], dims) + (dot(a[0], b[1], dims) + dot(a[1], b[0], dims))


def dot_ones(values, ones, dims):
    upper, lower = split_parts(values)
    return dot(upper, ones, dims) + dot(lower, ones, dims)


def after(value, *others):
    anywhere = pl.BlockSpec(memory_space=pl.ANY)
    return pl.pallas_call(
        lambda *refs: None,
        in_specs=[anywhere] * (1 + len(others)),
        out_specs=anywhere,
        out_shape=jax.ShapeDtypeStruct(value.shape, value.dtype),
        input_output_aliases={0: 0},
        name="after",
    )(value, *others)


NN = ((1,), (0,))
NT = ((1,), (1,))
TN = ((0,), (0,))


def head_spread(inner):
    row = lax.broadcasted_iota(jnp.int32, (LANES, inner), 0)
    col = lax.broadcasted_iota(jnp.int32, (LANES, inner), 1)
    return (col // HEAD_DIM == row).astype(bf16)


def head_sums(inner):
    row = lax.broadcasted_iota(jnp.int32, (inner, LANES), 0)
    col = lax.broadcasted_iota(jnp.int32, (inner, LANES), 1)
    return (row // HEAD_DIM == col).astype(bf16)


def lower_ones(extent):
    row = lax.broadcasted_iota(jnp.int32, (extent, extent), 0)
    col = lax.broadcasted_iota(jnp.int32, (extent, extent), 1)
    return (row >= col).astype(f32)


def kernel_params(mib):
    return pltpu.CompilerParams(vmem_limit_bytes=mib * 1024 * 1024)


def taking(micros, tokens):
    return pl.CostEstimate(flops=int(micros * tokens * 1.1e6), bytes_accessed=1024, transcendentals=0)


def conv_of(v_ref, halo_ref, cw_ref, padded):
    extent = padded.shape[0] - 8
    width = padded.shape[1]
    padded[0:8, :] = halo_ref[0]
    padded[8:, :] = v_ref[:, 0, :, 0:width].reshape(extent, width)
    summed = cw_ref[CONV_WIDTH : CONV_WIDTH + 1, :]
    for tap in range(CONV_WIDTH):
        summed = summed + cw_ref[tap : tap + 1, :] * padded[5 + tap : 5 + tap + extent, :]
    return summed


def step_sizes(v_ref, hp_ref, conv_width, extent):
    raw = v_ref[:, 0, :, conv_width : conv_width + LANES].reshape(extent, LANES) + hp_ref[1:2, :]
    step = jnp.maximum(raw, 0.0) + jnp.log1p(jnp.exp(-jnp.abs(raw)))
    return raw, step


def enter_kernel(inner, v_ref, halo_ref, cw_ref, hp_ref, xs_ref, rw_ref, dl_ref, s_ref, padded):
    extent = xs_ref.shape[1]
    width = padded.shape[1]
    pre = conv_of(v_ref, halo_ref, cw_ref, padded)
    act = pre * jax.nn.sigmoid(pre)
    xs = act[:, :inner]
    write = act[:, inner : inner + STATE_DIM]
    unused_raw, step = step_sizes(v_ref, hp_ref, width, extent)
    log_sum = dot(lower_ones(extent), -step * jnp.exp(hp_ref[0:1, :]), NN, highest)
    tail = jnp.exp(log_sum[extent - 1 : extent, :] - log_sum) * step
    spread = dot_ones(tail, head_spread(inner), NN)
    xs_ref[0] = xs
    rw_ref[0] = act[:, inner:]
    dl_ref[0, :, 0:LANES] = step
    dl_ref[0, :, LANES:] = log_sum
    s_ref[0] = dot_split(split_parts(xs * spread), split_parts(write), TN)


def mixer_enter(v, halo, cw, hp, inner):
    zs, slots, rows, cols = v.shape
    extent = zs * rows
    width = cw.shape[1]
    heads = inner // HEAD_DIM
    return pl.pallas_call(
        functools.partial(enter_kernel, inner),
        grid=(slots,),
        in_specs=[
            pl.BlockSpec((zs, 1, rows, cols), lambda s: (0, s, 0, 0)),
            pl.BlockSpec((1, 8, width), lambda s: (s, 0, 0)),
            pl.BlockSpec(cw.shape, lambda s: (0, 0)),
            pl.BlockSpec(hp.shape, lambda s: (0, 0)),
        ],
        out_specs=[
            pl.BlockSpec((1, extent, inner), lambda s: (s, 0, 0)),
            pl.BlockSpec((1, extent, 2 * STATE_DIM), lambda s: (s, 0, 0)),
            pl.BlockSpec((1, extent, 2 * LANES), lambda s: (s, 0, 0)),
            pl.BlockSpec((1, inner, STATE_DIM), lambda s: (s, 0, 0)),
        ],
        out_shape=[
            jax.ShapeDtypeStruct((slots, extent, inner), f32),
            jax.ShapeDtypeStruct((slots, extent, 2 * STATE_DIM), f32),
            jax.ShapeDtypeStruct((slots, extent, 2 * LANES), f32),
            jax.ShapeDtypeStruct((slots, inner, STATE_DIM), f32),
        ],
        scratch_shapes=[pltpu.VMEM((extent + 8, width), f32)],
        compiler_params=kernel_params(48),
        cost_estimate=taking(12, zs * slots * rows),
        name="mixer_enter",
    )(v, halo, cw, hp)


def scan_kernel(reverse, got_ref, decay_ref, out_ref):
    count = got_ref.shape[0]
    state = jnp.zeros(got_ref.shape[1:], f32)
    order = range(count - 1, -1, -1) if reverse else range(count)
    for piece in order:
        out_ref[piece] = state
        state = decay_ref[piece] * state + got_ref[piece]


def scan_pieces(got, decay, reverse):
    return pl.pallas_call(
        functools.partial(scan_kernel, reverse),
        out_shape=jax.ShapeDtypeStruct(got.shape, f32),
        compiler_params=kernel_params(32),
        name="scan_pieces",
    )(got, decay)


def exchanged(rows):
    return lax.all_to_all(rows, "dp", 0, 0, tiled=False)


def states_forward(beside, s_local, log_last):
    count = lax.axis_size("dp")
    slots, inner, _ = s_local.shape
    share = slots * inner // count
    per_row = jnp.repeat(jnp.exp(log_last).reshape(-1), HEAD_DIM).reshape(count, share)
    lines = -(-share // (8 * LANES)) * 8
    per_row = jnp.pad(per_row, ((0, 0), (0, lines * LANES - share))).reshape(count, lines, LANES)
    got = exchanged(jnp.concatenate([s_local.reshape(count, share, STATE_DIM), per_row], axis=1))
    decay = got[:, share:].reshape(count, lines * LANES)[:, :share, None]
    entering = exchanged(after(scan_pieces(got[:, :share], decay, False), beside))
    return entering.reshape(slots, inner, STATE_DIM), decay


def states_backward(g_local, decay):
    count = lax.axis_size("dp")
    slots, inner, _ = g_local.shape
    got = exchanged(g_local.reshape(count, slots * inner // count, STATE_DIM))
    return exchanged(scan_pieces(got, decay, True)).reshape(slots, inner, STATE_DIM)


def inner_kernel(inner, xs_ref, rw_ref, dl_ref, y_ref):
    extent = xs_ref.shape[1]
    write = split_parts(rw_ref[0, :, :STATE_DIM])
    read = split_parts(rw_ref[0, :, STATE_DIM:])
    step_t = dl_ref[0, :, 0:LANES].T
    log_sum = dl_ref[0, :, LANES:]
    log_t = log_sum.T
    scores = dot_split(read, write, NT)
    causal = lax.broadcasted_iota(jnp.int32, (extent, extent), 0) >= lax.broadcasted_iota(
        jnp.int32, (extent, extent), 1
    )
    xs_low = xs_ref[0].astype(bf16)
    for head in range(inner // HEAD_DIM):
        cols = slice(head * HEAD_DIM, (head + 1) * HEAD_DIM)
        gap = log_sum[:, head : head + 1] - log_t[head : head + 1, :]
        mixing = jnp.exp(jnp.where(causal, gap, -jnp.inf)) * scores * step_t[head : head + 1, :]
        y_ref[0, :, cols] = dot(mixing.astype(bf16), xs_low[:, cols], NN)


def mixer_inner(xs, rw, dl):
    slots, extent, inner = xs.shape
    return pl.pallas_call(
        functools.partial(inner_kernel, inner),
        grid=(slots,),
        in_specs=[
            pl.BlockSpec((1, extent, inner), lambda s: (s, 0, 0)),
            pl.BlockSpec((1, extent, 2 * STATE_DIM), lambda s: (s, 0, 0)),
            pl.BlockSpec((1, extent, 2 * LANES), lambda s: (s, 0, 0)),
        ],
        out_specs=pl.BlockSpec((1, extent, inner), lambda s: (s, 0, 0)),
        out_shape=jax.ShapeDtypeStruct((slots, extent, inner), f32),
        compiler_params=kernel_params(40),
        cost_estimate=taking(9, slots * extent),
        name="mixer_inner",
    )(xs, rw, dl)


def leave_kernel(inner, yi_ref, xs_ref, rw_ref, dl_ref, h_ref, z_ref, hp_ref, gain_ref, y_ref, gg_ref, sq_ref):
    extent = xs_ref.shape[1]
    zs, _, rows, _ = z_ref.shape
    read = split_parts(rw_ref[0, :, STATE_DIM:])
    grown = dot_ones(jnp.exp(dl_ref[0, :, LANES:]), head_spread(inner), NN)
    y = yi_ref[0] + grown * dot_split(read, split_parts(h_ref[0]), NT) + hp_ref[3:4, :] * xs_ref[0]
    y_ref[0] = y
    z = z_ref[...].reshape(extent, inner)
    gated = y * (z * jax.nn.sigmoid(z))
    sq_ref[0] = jnp.broadcast_to(jnp.sum(gated * gated, axis=1, keepdims=True), (extent, LANES))
    gg_ref[...] = (gated * gain_ref[...]).astype(bf16).reshape(zs, 1, rows, inner)


def mixer_leave(yi, xs, rw, dl, h_in, z, skip, gain):
    zs, slots, rows, inner = z.shape
    extent = zs * rows
    return pl.pallas_call(
        functools.partial(leave_kernel, inner),
        grid=(slots,),
        in_specs=[
            pl.BlockSpec((1, extent, inner), lambda s: (s, 0, 0)),
            pl.BlockSpec((1, extent, inner), lambda s: (s, 0, 0)),
            pl.BlockSpec((1, extent, 2 * STATE_DIM), lambda s: (s, 0, 0)),
            pl.BlockSpec((1, extent, 2 * LANES), lambda s: (s, 0, 0)),
            pl.BlockSpec((1, inner, STATE_DIM), lambda s: (s, 0, 0)),
            pl.BlockSpec((zs, 1, rows, inner), lambda s: (0, s, 0, 0)),
            pl.BlockSpec(skip.shape, lambda s: (0, 0)),
            pl.BlockSpec(gain.shape, lambda s: (0, 0)),
        ],
        out_specs=[
            pl.BlockSpec((1, extent, inner), lambda s: (s, 0, 0)),
            pl.BlockSpec((zs, 1, rows, inner), lambda s: (0, s, 0, 0)),
            pl.BlockSpec((1, extent, LANES), lambda s: (s, 0, 0)),
        ],
        out_shape=[
            jax.ShapeDtypeStruct((slots, extent, inner), f32),
            jax.ShapeDtypeStruct((zs, slots, rows, inner), bf16),
            jax.ShapeDtypeStruct((slots, extent, LANES), f32),
        ],
        compiler_params=kernel_params(48),
        cost_estimate=taking(7, zs * slots * rows),
        name="mixer_leave",
    )(yi, xs, rw, dl, h_in, z, skip, gain)


def unmix_kernel(inner, gn_ref, y_ref, z_ref, rw_ref, dl_ref, tok_ref, gain_ref, gy_ref, gz_ref, s_ref, gg_ref):
    extent = y_ref.shape[1]
    zs, _, rows, _ = z_ref.shape
    grad = gn_ref[...].reshape(extent, inner)
    z = z_ref[...].reshape(extent, inner)
    logistic = jax.nn.sigmoid(z)
    gate = z * logistic
    y = y_ref[0]
    gated = y * gate
    inv_rms = tok_ref[0, :, 0:1]
    cross = tok_ref[0, :, 1:2]
    part = jnp.sum(grad * gated * inv_rms, axis=0, keepdims=True)

    @pl.when(pl.program_id(0) == 0)
    def _():
        gg_ref[...] = jnp.zeros_like(gg_ref)

    gg_ref[0:1, :] += part
    gated_grad = grad * gain_ref[...] * inv_rms - gated * cross
    gy = gated_grad * gate
    gy_ref[0] = gy
    gz = gated_grad * y * (logistic * (1.0 + z * (1.0 - logistic)))
    gz_ref[...] = gz.astype(bf16).reshape(zs, 1, rows, inner)
    grown = dot_ones(jnp.exp(dl_ref[0, :, LANES:]), head_spread(inner), NN)
    s_ref[0] = dot_split(split_parts(gy * grown), split_parts(rw_ref[0, :, STATE_DIM:]), TN)


def mixer_unmix(gn, y, z, rw, dl, tok, gain):
    zs, slots, rows, inner = z.shape
    extent = zs * rows
    return pl.pallas_call(
        functools.partial(unmix_kernel, inner),
        grid=(slots,),
        in_specs=[
            pl.BlockSpec((zs, 1, rows, inner), lambda s: (0, s, 0, 0)),
            pl.BlockSpec((1, extent, inner), lambda s: (s, 0, 0)),
            pl.BlockSpec((zs, 1, rows, inner), lambda s: (0, s, 0, 0)),
            pl.BlockSpec((1, extent, 2 * STATE_DIM), lambda s: (s, 0, 0)),
            pl.BlockSpec((1, extent, 2 * LANES), lambda s: (s, 0, 0)),
            pl.BlockSpec((1, extent, 2), lambda s: (s, 0, 0)),
            pl.BlockSpec(gain.shape, lambda s: (0, 0)),
        ],
        out_specs=[
            pl.BlockSpec((1, extent, inner), lambda s: (s, 0, 0)),
            pl.BlockSpec((zs, 1, rows, inner), lambda s: (0, s, 0, 0)),
            pl.BlockSpec((1, inner, STATE_DIM), lambda s: (s, 0, 0)),
            pl.BlockSpec((8, inner), lambda s: (0, 0)),
        ],
        out_shape=[
            jax.ShapeDtypeStruct((slots, extent, inner), f32),
            jax.ShapeDtypeStruct((zs, slots, rows, inner), bf16),
            jax.ShapeDtypeStruct((slots, inner, STATE_DIM), f32),
            jax.ShapeDtypeStruct((8, inner), f32),
        ],
        compiler_params=kernel_params(48),
        cost_estimate=taking(9, zs * slots * rows),
        name="mixer_unmix",
    )(gn, y, z, rw, dl, tok, gain)


def pairs_kernel(inner, xs_ref, rw_ref, dl_ref, gy_ref, gx_ref, grw_ref, gdl_ref, cols_buf):
    extent = gy_ref.shape[1]
    write = split_parts(rw_ref[0, :, :STATE_DIM])
    read = split_parts(rw_ref[0, :, STATE_DIM:])
    step = dl_ref[0, :, 0:LANES]
    log_sum = dl_ref[0, :, LANES:]
    log_t = log_sum.T
    gy_parts, xs_parts = split_parts(gy_ref[0]), split_parts(xs_ref[0])
    scores_t = dot_split(write, read, NT)
    later = lax.broadcasted_iota(jnp.int32, (extent, extent), 1) >= lax.broadcasted_iota(
        jnp.int32, (extent, extent), 0
    )
    lane = lax.broadcasted_iota(jnp.int32, (extent, LANES), 1)
    score_grad_t = jnp.zeros((extent, extent), f32)
    step_direct = jnp.zeros((extent, LANES), f32)
    cols_buf[...] = jnp.zeros_like(cols_buf)
    for head in range(inner // HEAD_DIM):
        cols = slice(head * HEAD_DIM, (head + 1) * HEAD_DIM)
        gap_t = log_t[head : head + 1, :] - log_sum[:, head : head + 1]
        decay_t = jnp.exp(jnp.where(later, gap_t, -jnp.inf))
        step_col = step[:, head : head + 1]
        pair_t = dot_split([x[:, cols] for x in xs_parts], [g[:, cols] for g in gy_parts], NT)
        both_t = decay_t * pair_t
        score_grad_t = score_grad_t + both_t * step_col
        weight_t = both_t * scores_t
        step_direct = step_direct + jnp.where(lane == head, jnp.sum(weight_t, axis=1, keepdims=True), 0.0)
        cols_buf[head : head + 1, :] = jnp.sum(weight_t * step_col, axis=0, keepdims=True)
        gx_ref[0, :, cols] = dot((decay_t * scores_t * step_col).astype(bf16), gy_parts[0][:, cols], NN)
    score_parts = split_parts(score_grad_t)
    grw_ref[0, :, :STATE_DIM] = dot_split(score_parts, read, NN)
    grw_ref[0, :, STATE_DIM:] = dot_split(score_parts, write, TN)
    gdl_ref[0, :, 0:LANES] = step_direct
    gdl_ref[0, :, LANES:] = cols_buf[...].T - step * step_direct


def mixer_pairs(xs, rw, dl, gy):
    slots, extent, inner = xs.shape
    wide = pl.BlockSpec((1, extent, inner), lambda s: (s, 0, 0))
    two = pl.BlockSpec((1, extent, 2 * LANES), lambda s: (s, 0, 0))
    return pl.pallas_call(
        functools.partial(pairs_kernel, inner),
        grid=(slots,),
        in_specs=[wide, two, two, wide],
        out_specs=[wide, two, two],
        out_shape=[
            jax.ShapeDtypeStruct((slots, extent, inner), f32),
            jax.ShapeDtypeStruct((slots, extent, 2 * STATE_DIM), f32),
            jax.ShapeDtypeStruct((slots, extent, 2 * LANES), f32),
        ],
        scratch_shapes=[pltpu.VMEM((LANES, extent), f32)],
        compiler_params=kernel_params(48),
        cost_estimate=taking(42, slots * extent),
        name="mixer_pairs",
    )(xs, rw, dl, gy)


def back_kernel(
    inner, v_ref, halo_ref, cw_ref, hp_ref, skip_ref, rw_ref, dl_ref, gy_ref, gx_ref, grw_ref, gdl_ref, h_ref, gh_ref,
    gv_ref, gbc_ref, gp_ref, gc_ref, ghp_ref, padded, gpad,
):
    extent = gy_ref.shape[1]
    zs, _, rows, _ = v_ref.shape
    width = padded.shape[1]
    heads = inner // HEAD_DIM
    first = pl.program_id(0) == 0
    pre = conv_of(v_ref, halo_ref, cw_ref, padded)
    logistic = jax.nn.sigmoid(pre)
    slope = logistic * (1.0 + pre * (1.0 - logistic))
    xs = pre[:, :inner] * logistic[:, :inner]
    write_low = rw_ref[0, :, :STATE_DIM].astype(bf16)
    read_low = rw_ref[0, :, STATE_DIM:].astype(bf16)
    raw, step = step_sizes(v_ref, hp_ref, width, extent)
    rate = jnp.exp(hp_ref[0:1, :])
    log_sum = dl_ref[0, :, LANES:]
    gy = gy_ref[0]
    step_direct = gdl_ref[0, :, 0:LANES]
    sums = head_sums(inner)
    spread = head_spread(inner)
    last = log_sum[extent - 1 : extent, :]
    tail_decay = jnp.exp(last - log_sum)
    tail = dot_ones(tail_decay * step, spread, NN)
    grown = dot_ones(jnp.exp(log_sum), spread, NN)
    gh = gh_ref[0]
    h_in = h_ref[0]
    gh_parts, h_parts = split_parts(gh), split_parts(h_in)
    tail_in = dot(write_low, gh_parts[0], NT)
    tail_direct = tail_decay * dot_ones(xs * tail_in, sums, NN)
    tail_weight = tail_direct * step
    state_part = grown * dot(read_low, h_parts[0], NT)
    state_weight = dot_ones(gy * state_part, sums, NN)
    held = split_parts(gh * h_in)
    row_ones = jnp.ones((8, STATE_DIM), bf16)
    kept = dot_ones(dot(row_ones, held[0], NT) + dot(row_ones, held[1], NT), sums, NN)[0:1, :]
    log_grad = gdl_ref[0, :, LANES:] + state_weight - tail_weight
    end_grad = jnp.sum(tail_weight, axis=0, keepdims=True) + jnp.exp(last) * kept
    rate_arg_grad = dot(lower_ones(extent), log_grad, TN, highest) + end_grad
    step_grad = step_direct + tail_direct - rate * rate_arg_grad
    raw_grad = step_grad * jax.nn.sigmoid(raw)
    xs_grad = gx_ref[0] + tail * tail_in + skip_ref[3:4, :] * gy
    write_grad = grw_ref[0, :, :STATE_DIM] + dot_split(split_parts(tail * xs), gh_parts, NN)
    read_grad = grw_ref[0, :, STATE_DIM:] + dot_split(split_parts(grown * gy), h_parts, NN)
    valid_lane = lax.broadcasted_iota(jnp.int32, (1, LANES), 1) < heads
    rate_grad = jnp.where(valid_lane, jnp.sum(-step * rate * rate_arg_grad, axis=0, keepdims=True), 0.0)
    raw_grad = jnp.where(valid_lane, raw_grad, 0.0)
    skip_grad = jnp.sum(dot_ones(gy * xs, sums, NN), axis=0, keepdims=True)

    @pl.when(first)
    def _():
        gc_ref[...] = jnp.zeros_like(gc_ref)
        ghp_ref[...] = jnp.zeros_like(ghp_ref)

    ghp_ref[0:1, :] += rate_grad
    ghp_ref[1:2, :] += jnp.sum(raw_grad, axis=0, keepdims=True)
    ghp_ref[2:3, :] += skip_grad
    gpad[0:8, :] = jnp.zeros((8, width), f32)
    gpad[extent + 8 :, :] = jnp.zeros((8, width), f32)
    gpad[8 : extent + 8, 0:inner] = xs_grad * slope[:, 0:inner]
    gpad[8 : extent + 8, inner : inner + STATE_DIM] = write_grad * slope[:, inner : inner + STATE_DIM]
    gpad[8 : extent + 8, inner + STATE_DIM :] = read_grad * slope[:, inner + STATE_DIM :]
    back = jnp.zeros((extent, width), f32)
    before = jnp.zeros((8, width), f32)
    pre_grad = gpad[8 : extent + 8, :]
    for tap in range(CONV_WIDTH):
        ahead = CONV_WIDTH - 1 - tap
        weight = cw_ref[tap : tap + 1, :]
        back = back + weight * gpad[8 + ahead : 8 + ahead + extent, :]
        before = before + weight * gpad[ahead : 8 + ahead, :]
        gc_ref[tap : tap + 1, :] += jnp.sum(pre_grad * padded[5 + tap : 5 + tap + extent, :], axis=0, keepdims=True)
    gc_ref[CONV_WIDTH : CONV_WIDTH + 1, :] += jnp.sum(pre_grad, axis=0, keepdims=True)
    gp_ref[0] = before
    gv_ref[:, :, :, 0:inner] = back[:, :inner].astype(bf16).reshape(zs, 1, rows, inner)
    gbc_ref[...] = back[:, inner:].reshape(zs, 1, rows, width - inner)
    gv_ref[:, :, :, inner:] = raw_grad.astype(bf16).reshape(zs, 1, rows, LANES)


def mixer_back(v, halo, cw, hp, skip, rw, dl, gy, gx, grw, gdl, h_in, gh):
    zs, slots, rows, cols = v.shape
    extent = zs * rows
    inner = gy.shape[2]
    width = cw.shape[1]
    wide = pl.BlockSpec((1, extent, inner), lambda s: (s, 0, 0))
    two = pl.BlockSpec((1, extent, 2 * LANES), lambda s: (s, 0, 0))
    state = pl.BlockSpec((1, inner, STATE_DIM), lambda s: (s, 0, 0))
    return pl.pallas_call(
        functools.partial(back_kernel, inner),
        grid=(slots,),
        in_specs=[
            pl.BlockSpec((zs, 1, rows, cols), lambda s: (0, s, 0, 0)),
            pl.BlockSpec((1, 8, width), lambda s: (s, 0, 0)),
            pl.BlockSpec(cw.shape, lambda s: (0, 0)),
            pl.BlockSpec(hp.shape, lambda s: (0, 0)),
            pl.BlockSpec(skip.shape, lambda s: (0, 0)),
            two,
            two,
            wide,
            wide,
            two,
            two,
            state,
            state,
        ],
        out_specs=[
            pl.BlockSpec((zs, 1, rows, inner + LANES), lambda s: (0, s, 0, 0)),
            pl.BlockSpec((zs, 1, rows, 2 * STATE_DIM), lambda s: (0, s, 0, 0)),
            pl.BlockSpec((1, 8, width), lambda s: (s, 0, 0)),
            pl.BlockSpec((8, width), lambda s: (0, 0)),
            pl.BlockSpec((8, LANES), lambda s: (0, 0)),
        ],
        out_shape=[
            jax.ShapeDtypeStruct((zs, slots, rows, inner + LANES), bf16),
            jax.ShapeDtypeStruct((zs, slots, rows, 2 * STATE_DIM), f32),
            jax.ShapeDtypeStruct((slots, 8, width), f32),
            jax.ShapeDtypeStruct((8, width), f32),
            jax.ShapeDtypeStruct((8, LANES), f32),
        ],
        scratch_shapes=[
            pltpu.VMEM((extent + 8, width), f32),
            pltpu.VMEM((extent + 16, width), f32),
        ],
        compiler_params=kernel_params(56),
        cost_estimate=taking(18, zs * slots * rows),
        name="mixer_back",
    )(v, halo, cw, hp, skip, rw, dl, gy, gx, grw, gdl, h_in, gh)


def expert_kernel(
    n_ref, g_ref, mask_ref, router_ref, up_ref, down_ref,
    moe_ref, back_ref, logit_ref, act_ref, hid_ref, moe_sum, back_sum, gates_buf, gate_grad,
):
    pair = pl.program_id(0)
    pairs = pl.num_programs(0)
    tokens = n_ref.shape[0]
    lane = lax.broadcasted_iota(jnp.int32, (tokens, LANES), 1)
    half = up_ref.shape[3] // 2

    @pl.when(pair == 0)
    def _():
        logits = dot(n_ref[...], router_ref[...], NN)
        chosen = mask_ref[...] > 0.0
        logits = jnp.where(chosen, logits, -jnp.inf)
        powers = jnp.exp(logits - jnp.max(logits, axis=1, keepdims=True))
        gates = powers / jnp.sum(powers, axis=1, keepdims=True)
        gates_buf[...] = jnp.where(lane < EXPERTS, gates, 1.0)
        moe_sum[...] = jnp.zeros_like(moe_sum)
        back_sum[...] = jnp.zeros_like(back_sum)
        gate_grad[...] = jnp.zeros_like(gate_grad)

    depth = up_ref.shape[0] * up_ref.shape[2]
    down = down_ref[...].reshape(depth, 2 * half)
    n_val = n_ref[...]
    gates = gates_buf[...]
    act_back = dot(g_ref[...], down, NN)
    ups = [up_ref[:, member].reshape(depth, 2 * half) for member in range(2)]
    for member in range(2):
        hidden = dot(n_val, ups[member], NN)
        gate_part, up_part = hidden[:, :half], hidden[:, half:]
        logistic = jax.nn.sigmoid(gate_part)
        silu = gate_part * logistic
        act = (silu * up_part).astype(bf16).astype(f32)
        own = lane == 2 * pair + member
        gate = jnp.sum(jnp.where(own, gates, 0.0), axis=1, keepdims=True)
        part = act_back[:, member * half : (member + 1) * half]
        gate_grad[...] += jnp.where(own, jnp.sum(act * part, axis=1, keepdims=True), 0.0)
        act_ref[0, :, member * half : (member + 1) * half] = (gate * act).astype(bf16)
        part = part * gate
        first_col = 2 * member * half
        hid_ref[0, :, first_col : first_col + half] = (part * up_part * (logistic * (1.0 + gate_part * (1.0 - logistic)))).astype(bf16)
        hid_ref[0, :, first_col + half : first_col + 2 * half] = (part * silu).astype(bf16)
    moe_sum[...] += dot(act_ref[0], down, NT)
    back_sum[...] += dot(hid_ref[0], jnp.concatenate(ups, axis=1), NT)

    @pl.when(pair == pairs - 1)
    def _():
        gates_in = jnp.where(lane < EXPERTS, gates, 0.0)
        grads = gates_in * gate_grad[...]
        logit_grad = (grads - gates_in * jnp.sum(grads, axis=1, keepdims=True)).astype(bf16)
        logit_ref[...] = logit_grad
        back_ref[...] = (back_sum[...] + dot(logit_grad, router_ref[...], NT)).astype(bf16)
        moe_ref[...] = moe_sum[...].astype(bf16)


def experts(n_two, g_moe, mask, router, weights):
    tokens, width = n_two.shape
    count, blocks, rows, cols = weights.shape
    pairs = blocks // 3
    down_at = 2 * pairs
    return pl.pallas_call(
        expert_kernel,
        grid=(pairs,),
        in_specs=[
            pl.BlockSpec((tokens, width), lambda p: (0, 0)),
            pl.BlockSpec((tokens, width), lambda p: (0, 0)),
            pl.BlockSpec((tokens, LANES), lambda p: (0, 0)),
            pl.BlockSpec((width, LANES), lambda p: (0, 0)),
            pl.BlockSpec((count, 2, rows, cols), lambda p: (0, p, 0, 0)),
            pl.BlockSpec((count, 1, rows, cols), lambda p: (0, down_at + p, 0, 0)),
        ],
        out_specs=[
            pl.BlockSpec((tokens, width), lambda p: (0, 0)),
            pl.BlockSpec((tokens, width), lambda p: (0, 0)),
            pl.BlockSpec((tokens, LANES), lambda p: (0, 0)),
            pl.BlockSpec((1, tokens, cols), lambda p: (p, 0, 0)),
            pl.BlockSpec((1, tokens, 2 * cols), lambda p: (p, 0, 0)),
        ],
        out_shape=[
            jax.ShapeDtypeStruct((tokens, width), bf16),
            jax.ShapeDtypeStruct((tokens, width), bf16),
            jax.ShapeDtypeStruct((tokens, LANES), bf16),
            jax.ShapeDtypeStruct((pairs, tokens, cols), bf16),
            jax.ShapeDtypeStruct((pairs, tokens, 2 * cols), bf16),
        ],
        scratch_shapes=[
            pltpu.VMEM((tokens, width), f32),
            pltpu.VMEM((tokens, width), f32),
            pltpu.VMEM((tokens, LANES), f32),
            pltpu.VMEM((tokens, LANES), f32),
        ],
        compiler_params=kernel_params(60),
        cost_estimate=taking(72, tokens),
        name="experts",
    )(n_two, g_moe, mask, router, weights, weights)


def expert_grad_kernel(up_blocks, chunks, *refs):
    n_refs, g_refs, h_refs, a_refs = (refs[i * chunks : (i + 1) * chunks] for i in range(4))
    out_ref = refs[4 * chunks]
    block = pl.program_id(0)
    count, _, rows, cols = out_ref.shape

    def summed(lefts, rights):
        total = dot(lefts[0][...], rights[0][0], NN)
        for left, right in zip(lefts[1:], rights[1:]):
            total = total + dot(left[...], right[0], NN)
        out_ref[...] = total.astype(bf16).reshape(count, 1, rows, cols)

    @pl.when(block < up_blocks)
    def _():
        summed(n_refs, h_refs)

    @pl.when(block >= up_blocks)
    def _():
        summed(g_refs, a_refs)


def expert_grads(n_list, g_list, hid_list, act_list, count):
    chunks = len(n_list)
    width, tokens = n_list[0].shape
    pairs, _, cols = act_list[0].shape
    ups = 2 * pairs
    blocks = 3 * pairs
    whole = pl.BlockSpec((width, tokens), lambda b: (0, 0))
    hid_at = lambda b: (jnp.minimum(b, ups - 1) // 2, 0, jnp.minimum(b, ups - 1) % 2)
    return pl.pallas_call(
        functools.partial(expert_grad_kernel, ups, chunks),
        grid=(blocks,),
        in_specs=[whole] * (2 * chunks)
        + [pl.BlockSpec((1, tokens, cols), hid_at)] * chunks
        + [pl.BlockSpec((1, tokens, cols), lambda b: (jnp.maximum(b - ups, 0), 0, 0))] * chunks,
        out_specs=pl.BlockSpec((count, 1, width // count, cols), lambda b: (0, b, 0, 0)),
        out_shape=jax.ShapeDtypeStruct((count, blocks, width // count, cols), bf16),
        compiler_params=kernel_params(48),
        cost_estimate=taking(40, chunks * tokens),
        name="expert_grads",
    )(*n_list, *g_list, *hid_list, *act_list)


def body(
    block_input,
    out_grad,
    lengths,
    routes,
    norm1_gain,
    w_zx,
    w_bc,
    w_dt,
    conv_x,
    conv_bc,
    head_params,
    gate_gain,
    w_out,
    norm2_gain,
    w_router,
    w_gu,
    w_dn,
    s_gu,
    s_dn,
):
    zs = lax.axis_size("tensor")
    pieces = lax.axis_size("dp")
    own = lax.axis_index("tensor")
    wide_index = lax.axis_index("dp")
    rows = block_input.shape[0]
    piece_rows = rows * zs
    heads = HEAD_COUNT // zs
    inner = INNER_DIM // zs
    width = inner + 2 * STATE_DIM
    shard = D_MODEL // pieces
    half = w_gu.shape[3]
    rim = CONV_WIDTH - 1
    per = SLOT_COUNT // CHUNKS
    tokens = per * rows
    chunk_ids = range(CHUNKS)

    enter_shard = jnp.concatenate(
        [w_zx[:, 1], w_bc, jnp.pad(w_dt, ((0, 0), (0, LANES - heads)))], axis=1
    )
    side_shard = jnp.concatenate(
        [w_zx[:, 0], w_out.T, jnp.pad(w_router, ((0, 0), (0, LANES - EXPERTS)))], axis=1
    )
    expert_shard = jnp.concatenate(
        [
            w_gu.reshape(EXPERTS, shard, 2 * half),
            s_gu.reshape(shard, 2, 2, half).transpose(2, 0, 1, 3).reshape(2, shard, 2 * half),
            w_dn.reshape(EXPERTS // 2, 2 * half, shard).transpose(0, 2, 1),
            s_dn.T[None],
        ],
        axis=0,
    )

    def by_slot(values):
        return jnp.transpose(values, (1, 0, 2))

    def part(values, c):
        return values[c * per : (c + 1) * per].reshape((tokens,) + values.shape[2:])

    u_slots = by_slot(block_input)
    u_low = [row_major(part(u_slots, c)) for c in chunk_ids]
    u_all = [in_order(line_gather(u_low[c])) for c in chunk_ids]
    full_enter = weight_gather(enter_shard).reshape(D_MODEL, width + LANES)
    gains = jnp.stack([norm1_gain, norm2_gain], axis=1).astype(f32)
    gains = lax.all_gather(gains, "dp", axis=0, tiled=True)
    gain_one, gain_two = gains[:, 0], gains[:, 1]
    full_side = weight_gather(side_shard).reshape(D_MODEL, 2 * inner + LANES)
    full_z, full_out, full_router = full_side[:, :inner], full_side[:, inner : 2 * inner], full_side[:, 2 * inner :]

    positions = wide_index * piece_rows + own * rows + jnp.arange(rows, dtype=jnp.int32)
    valid = (positions[None, :] < lengths[:, None]).astype(f32)[:, :, None]
    grad_slots = by_slot(out_grad).astype(f32) * valid

    conv_w = jnp.pad(jnp.concatenate([conv_x, conv_bc], axis=1), ((0, 8 - CONV_WIDTH - 1), (0, 0)))
    hp = jnp.pad(head_params, ((0, 5), (0, LANES - heads)))
    skip = jnp.pad(jnp.repeat(head_params[2], HEAD_DIM)[None], ((3, 4), (0, 0)))
    gain_row = gate_gain[None]

    hot = jnp.sum(
        (routes[..., None] == jnp.arange(LANES, dtype=jnp.int32)).astype(f32), axis=2
    )
    hot = jnp.transpose(hot.reshape(zs, rows, SLOT_COUNT, LANES), (0, 2, 1, 3))

    hot_at = by_distance(hot)

    def flat(values):
        return values.reshape((zs * tokens,) + values.shape[2:])

    def in_slots(values):
        return values.reshape((zs, per, rows) + values.shape[1:])

    u = [row_major(u_low[c].astype(f32)) for c in chunk_ids]
    valid_c = [part(valid, c) for c in chunk_ids]
    grad_c = [row_major(part(grad_slots, c)) for c in chunk_ids]
    n_one, v, z, halo, entered = [], [], [], [], []
    for c in chunk_ids:
        n_one.append(row_major(rms_scale(flat(u_all[c]).astype(f32), gain_one).astype(bf16)))
        v.append(in_slots(dot(n_one[c], full_enter, NN)))
        rim_rows = in_slots(n_one[c])[zs - 1, :, rows - rim :]
        prior = dot(passed_along(rim_rows, "dp", 1).reshape(per * rim, D_MODEL), full_enter[:, :width], NN)
        halo.append(jnp.pad(prior.reshape(per, rim, width), ((0, 0), (8 - rim, 0), (0, 0))))
    g_blocks = [line_gather(after(grad_c[c].astype(bf16), u_all[CHUNKS - 1])) for c in chunk_ids]
    for c in chunk_ids:
        entered.append(mixer_enter(v[c], halo[c], conv_w, hp, inner))
    resid, mixed_all, y_all, h_all, decay_all, inv_alls, gg_all, n_two = [], [], [], [], [], [], [], []
    for c in chunk_ids:
        xs, rw, dl, s_local = entered[c]
        yi = mixer_inner(xs, rw, dl)
        z.append(in_slots(dot(n_one[c], full_z, NN)))
        s_local = after(s_local, g_blocks[c][1], g_blocks[c][3])
        h_in, decay = states_forward(g_blocks[c][2], s_local, dl[:, piece_rows - 1, LANES : LANES + heads])
        if c == 0:
            full_expert = weight_gather(after(expert_shard, h_in))
        y, gg, squares = mixer_leave(yi, xs, rw, dl, h_in, z[c], skip, gain_row)
        product = dot(flat(gg.reshape(zs, tokens, inner)), full_out, NT).astype(bf16)
        mixed = summed(line_parts(by_distance(product.reshape(zs, tokens, D_MODEL))))
        square_sum = lax.psum(squares[:, :, 0], "tensor")
        inv_all = lax.rsqrt(square_sum / INNER_DIM + norm_eps)
        mixed = mixed * lax.dynamic_slice_in_dim(inv_all, own * rows, rows, 1).reshape(tokens, 1)
        resid.append(row_major(u[c] + mixed))
        mixed_all.append(mixed)
        y_all.append(y)
        h_all.append(h_in)
        decay_all.append(decay)
        inv_alls.append(inv_all)
        gg_all.append(gg)
        n_two.append(jnp.concatenate(line_gather(row_major(rms_scale(resid[c], gain_two).astype(bf16))), axis=0))
    moe_part, back_part, logit_grads, acts, hids = [], [], [], [], []
    g_moe = [jnp.concatenate(g_blocks[c], axis=0) for c in chunk_ids]
    for c in chunk_ids:
        mask = jnp.concatenate([part(hot_at(k), c) for k in range(zs)], axis=0)
        results = experts(n_two[c], g_moe[c], mask, full_router, full_expert)
        moe_part.append(results[0].reshape(zs, tokens, D_MODEL))
        back_part.append(results[1].reshape(zs, tokens, D_MODEL))
        logit_grads.append(results[2])
        acts.append(results[3])
        hids.append(results[4])

    def norm_back(values, gain_vec, grads):
        return jax.vjp(rms_scale, values, gain_vec)[1](grads)

    resid_grad, g_mixed, gain_two_grad = [], [], 0.0
    unmixed, pairs, toks, gate_gain_grad = [], [], [], 0.0
    for c in chunk_ids:
        n_two_grad = summed(line_parts(lambda k: back_part[c][k]))
        from_norm, gain_grad = norm_back(resid[c], gain_two, n_two_grad)
        gain_two_grad = gain_two_grad + gain_grad
        resid_grad.append(row_major(grad_c[c] + from_norm))
        low = resid_grad[c].astype(bf16)
        if c == CHUNKS - 1:
            expert_grad = weight_scatter(
                after(expert_grads([n.T for n in n_two], [g.T for g in g_moe], hids, acts, pieces), low)
            ).astype(f32)
        g_mixed.append(flat(in_order(line_gather(low))))
        grad = in_slots(dot(g_mixed[c], full_out, NN))
        xs, rw, dl, _ = entered[c]
        inv_all = inv_alls[c]
        y_like = jnp.transpose(y_all[c].reshape(per, zs, rows, inner), (1, 0, 2, 3))
        cross = jnp.sum(grad * gain_row * y_like * jax.nn.silu(z[c]), axis=-1)
        cross = lax.psum(jnp.transpose(cross, (1, 0, 2)).reshape(per, piece_rows), "tensor")
        tok = jnp.stack([inv_all, cross * (inv_all * inv_all * inv_all) / INNER_DIM], axis=-1)
        gy, gz, g_local, gg_grad = mixer_unmix(grad, y_all[c], z[c], rw, dl, tok, gain_row)
        toks.append(tok)
        gate_gain_grad = gate_gain_grad + gg_grad[0]
        unmixed.append((gy, gz, g_local))
        pairs.append(mixer_pairs(xs, rw, dl, gy))

    moe = []
    for c in chunk_ids:
        held = after(moe_part[c], *toks)
        moe.append(summed(line_parts(lambda k: held[k])))
    output = [resid[c] + moe[c] for c in chunk_ids]
    stat_terms = sum(
        jnp.stack(
            [
                jnp.sum(valid_c[c] * output[c] * output[c]),
                jnp.sum(valid_c[c] * mixed_all[c] * mixed_all[c]),
                jnp.sum(valid_c[c] * moe[c] * moe[c]),
            ]
        )
        for c in chunk_ids
    )
    router_grad = sum(dot(n_two[c], logit_grads[c], TN)[:, :EXPERTS] for c in chunk_ids)

    def rows_of(values):
        return jnp.concatenate([v.reshape(zs * tokens, -1) for v in values], axis=0)

    inv_rows = [
        jnp.transpose(inv_alls[c].reshape(per, zs, rows), (1, 0, 2)).reshape(zs * tokens, 1) for c in chunk_ids
    ]
    scaled = [(g_mixed[c].astype(f32) * inv_rows[c]).astype(bf16) for c in chunk_ids]
    out_w_grad = dot(rows_of(scaled), rows_of(gg_all), TN).astype(bf16)
    n_rows = rows_of(n_one)
    z_w_grad = dot(n_rows, rows_of([unmixed[c][1] for c in chunk_ids]), TN).astype(bf16)

    ups, downs = EXPERTS + 2, EXPERTS // 2
    expert_outs = (
        expert_grad[:EXPERTS].reshape(EXPERTS, shard, 2, half),
        expert_grad[ups : ups + downs].transpose(0, 2, 1).reshape(EXPERTS, half, shard),
        expert_grad[EXPERTS:ups].reshape(2, shard, 2, half).transpose(1, 2, 0, 3).reshape(shard, 2, 2 * half),
        expert_grad[ups + downs].T,
    )

    v_grads, bc_grads, conv_grad, head_grad = [], [], 0.0, 0.0
    full_x = jnp.concatenate([full_enter[:, :inner], full_enter[:, width:]], axis=1)
    full_bc = full_enter[:, inner:width]
    full_bc = jnp.concatenate([full_bc, full_bc], axis=1)
    for c in chunk_ids:
        gy, gz, g_local = unmixed[c]
        xs, rw, dl, _ = entered[c]
        gh = after(states_backward(g_local, decay_all[c]), moe[c], *expert_outs)
        gv, gbc, g_rim, gc, ghp = mixer_back(
            v[c], halo[c], conv_w, hp, skip, rw, dl, gy, *pairs[c], h_all[c], gh
        )
        conv_grad = conv_grad + gc
        head_grad = head_grad + ghp
        following = passed_along(g_rim[:, 8 - rim :].astype(bf16), "dp", -1).astype(f32)
        edge = gv[zs - 1, :, rows - rim :, :inner].astype(f32) + following[:, :, :inner]
        gv = lax.dynamic_update_slice(gv, edge.astype(bf16)[None], (zs - 1, 0, rows - rim, 0))
        edge = gbc[zs - 1, :, rows - rim :] + following[:, :, inner:]
        gbc = lax.dynamic_update_slice(gbc, edge[None], (zs - 1, 0, rows - rim, 0))
        v_grads.append(gv)
        bc_grads.append(jnp.concatenate(split_parts(gbc), axis=-1))
    n_parts, arrived, gain_one_grad = [], [], 0.0
    for c in chunk_ids:
        n_grad = (
            dot(unmixed[c][1].reshape(zs * tokens, inner), full_z, NT)
            + dot(v_grads[c].reshape(zs * tokens, inner + LANES), full_x, NT)
            + dot(bc_grads[c].reshape(zs * tokens, 4 * STATE_DIM), full_bc, NT)
        )
        every = flat(u_all[c]).astype(f32)
        scale = lax.rsqrt(jnp.mean(every * every, axis=-1, keepdims=True) + norm_eps)
        gain_one_grad = gain_one_grad + jnp.sum(n_grad * (every * scale), axis=0)
        n_parts.append(n_grad.astype(bf16))
        received = line_parts(by_distance(n_parts[c].reshape(zs, tokens, D_MODEL)))
        arrived.append(received)
    enter_w_grad = dot(n_rows, rows_of(v_grads), TN).astype(bf16)
    bc_w_grad = dot(n_rows, rows_of(bc_grads), TN)
    bc_w_grad = bc_w_grad[:, : 2 * STATE_DIM] + bc_w_grad[:, 2 * STATE_DIM :]

    def mixer_scatter(grads):
        return weight_scatter(grads.reshape(pieces, shard, -1)).astype(f32)

    out_part, z_part = mixer_scatter(out_w_grad), mixer_scatter(z_w_grad)
    enter_part = mixer_scatter(enter_w_grad)
    def to_shares(values, dim):
        size = values.shape[dim] // (pieces * zs)
        values = jnp.moveaxis(values, dim, 0).reshape(pieces, zs, size, -1)
        return jnp.moveaxis(values, 3, 2).reshape(pieces, zs, -1)

    column = own * inner
    conv_x_full = lax.dynamic_update_slice(
        jnp.zeros((CONV_WIDTH + 1, INNER_DIM), f32), conv_grad[: CONV_WIDTH + 1, :inner], (jnp.int32(0), column)
    )
    gate_full = lax.dynamic_update_slice(jnp.zeros((INNER_DIM,), f32), gate_gain_grad, (column,))
    small = [
        (gain_one_grad, 0),
        (conv_x_full, 1),
        (conv_grad[: CONV_WIDTH + 1, inner:], 1),
        (gate_full, 0),
        (gain_two_grad, 0),
        (router_grad, 0),
    ]
    shares = [to_shares(values, dim) for values, dim in small]
    sizes = [share.shape[2] for share in shares]
    shares = jnp.concatenate(shares, axis=2)
    length = shares.shape[2]
    shares = jnp.pad(shares, ((0, 0), (0, 0), (0, -length % (8 * LANES))))
    wide_share = bc_w_grad.reshape(pieces, zs, -1, LANES)
    shares = jnp.concatenate([wide_share, shares.reshape(pieces, zs, -1, LANES)], axis=2)
    shares = after(shares, arrived[CHUNKS - 1][2])
    shares = jnp.sum(lax.all_to_all(shares, "dp", 0, 0), axis=0)
    first_sum = shares
    shares = jnp.sum(lax.all_to_all(shares, "tensor", 0, 0), axis=0)
    u_grad = []
    for c in chunk_ids:
        received = arrived[c]
        if c == CHUNKS - 1:
            received[1] = after(received[1], first_sum)
        u_grad.append(resid_grad[c] + norm_back(u[c], gain_one, summed(received))[0])
    bc_lines = wide_share.shape[2]
    bc_grad = shares[:bc_lines].reshape(-1, 2 * STATE_DIM)
    shares = shares[bc_lines:].reshape(-1)
    ends = [sum(sizes[: k + 1]) for k in range(len(sizes))]
    took = []
    for (values, dim), size, end in zip(small, sizes, ends):
        share = shares[end - size : end]
        if values.ndim == 2:
            other = values.shape[1 - dim]
            share = share.reshape(other, size // other)
            share = share if dim == 1 else share.T
        took.append(share)
    tile = jnp.zeros((8, LANES), f32)
    tile = tile.at[:3, :heads].set(head_grad[:3, :heads]).at[3, :3].set(stat_terms)
    tile = jnp.sum(lax.all_gather(tile, "dp"), axis=0)
    tiles = lax.all_gather(tile, "tensor")
    head_sum = jnp.transpose(tiles[:, :3, :heads], (1, 0, 2)).reshape(3, HEAD_COUNT)
    stat_sum = jnp.sum(tiles[:, 3, :3], axis=0)
    stats = jnp.sqrt(stat_sum / (jnp.sum(lengths).astype(f32) * D_MODEL))

    def placed_back(values):
        whole = jnp.concatenate([value.astype(bf16).reshape(per, rows, D_MODEL) for value in values], axis=0)
        return jnp.transpose(whole, (1, 0, 2))

    return (
        placed_back(output),
        placed_back(u_grad),
        took[0],
        jnp.stack([z_part, enter_part[:, :inner]], axis=1),
        bc_grad,
        enter_part[:, inner : inner + heads],
        took[1],
        took[2],
        head_sum,
        took[3],
        out_part.T,
        took[4],
        took[5],
        *expert_outs,
        stats,
    )


def solution(mesh):
    both = ("dp", "tensor")
    placed = (
        P(both, None, None),
        P(both, None, None),
        P(),
        P("dp", None, None),
        P("dp"),
        P("dp", None, "tensor"),
        P("dp", None),
        P("dp", "tensor"),
        P(None, "tensor"),
        P(),
        P(None, "tensor"),
        P("tensor"),
        P("tensor", "dp"),
        P("dp"),
        P("dp", None),
        P(None, "dp", None, "tensor"),
        P(None, "tensor", "dp"),
        P("dp", None, "tensor"),
        P("tensor", "dp"),
    )
    return jax.shard_map(
        body,
        mesh=mesh,
        in_specs=placed,
        out_specs=(
            P(both, None, None),
            P(both, None, None),
            P(both),
            P("dp", None, "tensor"),
            P(both, None),
            P("dp", "tensor"),
            P(None, both),
            P(None, both),
            P(),
            P(both),
            P("tensor", "dp"),
            P(both),
            P(both, None),
            P(None, "dp", None, "tensor"),
            P(None, "tensor", "dp"),
            P("dp", None, "tensor"),
            P("tensor", "dp"),
            P(),
        ),
        check_vma=False,
    )
```

```python
import functools

import jax
import jax.numpy as jnp
from jax import lax
from jax.experimental import pallas as pl
from jax.experimental.layout import Layout, with_layout_constraint
from jax.experimental.pallas import tpu as pltpu
from jax.sharding import PartitionSpec as P

D_MODEL = 1536
HEAD_COUNT = 48
HEAD_DIM = 64
STATE_DIM = 128
CONV_WIDTH = 4
TOP_K = 6
EXPERTS = 16
SLOT_COUNT = 4
INNER_DIM = 3072
LANES = 128
CHUNKS = 1
HALVES = 2

norm_eps = 1e-05
highest = lax.Precision.HIGHEST
f32 = jnp.float32
bf16 = jnp.bfloat16


def passed_along(value, axis, steps):
    count = lax.axis_size(axis)
    first, last = (max(0, -steps), min(count, count - steps))
    return lax.ppermute(value, axis, [(source, source + steps) for source in range(first, last)])


def row_major(value):
    return with_layout_constraint(value, Layout(major_to_minor=tuple(range(value.ndim))))


def line_gather(value):
    size = lax.axis_size("tensor")
    return [value] + [
        row_major(lax.ppermute(row_major(value), "tensor", [(a, (a - step) % size) for a in range(size)]))
        for step in range(1, size)
    ]


def line_parts(block_of):
    size = lax.axis_size("tensor")
    return [block_of(0)] + [
        lax.ppermute(row_major(block_of(step)), "tensor", [(a, (a + step) % size) for a in range(size)])
        for step in range(1, size)
    ]


def summed(parts):
    total = parts[0].astype(f32)
    for part in parts[1:]:
        total = total + part.astype(f32)
    return row_major(total)


def in_order(blocks):
    size = len(blocks)
    own = lax.axis_index("tensor")
    whole = jnp.zeros((size,) + blocks[0].shape, blocks[0].dtype)
    for k in range(size):
        whole = lax.dynamic_update_index_in_dim(whole, blocks[k], (own + k) % size, 0)
    return whole


def by_distance(whole):
    size = whole.shape[0]
    own = lax.axis_index("tensor")
    return lambda k: lax.dynamic_index_in_dim(whole, (own + k) % size, 0, False)


def weight_gather(shard):
    return lax.all_gather(shard, "dp", axis=0, tiled=False)


def weight_scatter(grads):
    return row_major(lax.psum_scatter(grads.astype(bf16), "dp", scatter_dimension=0, tiled=False))


def rms_scale(values, gain_vec):
    return (
        values * lax.rsqrt(jnp.mean(values * values, axis=-1, keepdims=True) + norm_eps) * gain_vec
    )


def silu_slope(values):
    logistic = jax.nn.sigmoid(values)
    return logistic * (1.0 + values * (1.0 - logistic))


def dot(a, b, dims, precision=None):
    return lax.dot_general(a, b, (dims, ((), ())), precision=precision, preferred_element_type=f32)


def split_parts(values):
    upper = values.astype(bf16)
    return upper, (values - upper.astype(f32)).astype(bf16)


def dot_split(a, b, dims):
    return dot(a[0], b[0], dims) + (dot(a[0], b[1], dims) + dot(a[1], b[0], dims))


def dot_ones(values, ones, dims):
    upper, lower = split_parts(values)
    return dot(upper, ones, dims) + dot(lower, ones, dims)


def after(value, *others):
    anywhere = pl.BlockSpec(memory_space=pl.ANY)
    return pl.pallas_call(
        lambda *refs: None,
        in_specs=[anywhere] * (1 + len(others)),
        out_specs=anywhere,
        out_shape=jax.ShapeDtypeStruct(value.shape, value.dtype),
        input_output_aliases={0: 0},
        name="after",
    )(value, *others)


def skipping(kernel, first, count):
    return lambda *refs: kernel(*refs[:first], *refs[first + count :])


ANYWHERE = pl.BlockSpec(memory_space=pl.ANY)
NN = ((1,), (0,))
NT = ((1,), (1,))
TN = ((0,), (0,))


def head_spread(inner):
    row = lax.broadcasted_iota(jnp.int32, (LANES, inner), 0)
    col = lax.broadcasted_iota(jnp.int32, (LANES, inner), 1)
    return (col // HEAD_DIM == row).astype(bf16)


def head_sums(inner):
    row = lax.broadcasted_iota(jnp.int32, (inner, LANES), 0)
    col = lax.broadcasted_iota(jnp.int32, (inner, LANES), 1)
    return (row // HEAD_DIM == col).astype(bf16)


def lower_ones(extent):
    row = lax.broadcasted_iota(jnp.int32, (extent, extent), 0)
    col = lax.broadcasted_iota(jnp.int32, (extent, extent), 1)
    return (row >= col).astype(f32)


def kernel_params(mib):
    return pltpu.CompilerParams(vmem_limit_bytes=mib * 1024 * 1024)


def taking(micros, tokens):
    return pl.CostEstimate(flops=int(micros * tokens * 1.1e6), bytes_accessed=1024, transcendentals=0)


def conv_of(v_ref, halo_ref, cw_ref, padded):
    extent = padded.shape[0] - 8
    width = padded.shape[1]
    padded[0:8, :] = halo_ref[0]
    padded[8:, :] = v_ref[:, 0, :, 0:width].reshape(extent, width)
    summed = cw_ref[CONV_WIDTH : CONV_WIDTH + 1, :]
    for tap in range(CONV_WIDTH):
        summed = summed + cw_ref[tap : tap + 1, :] * padded[5 + tap : 5 + tap + extent, :]
    return summed


def step_sizes(v_ref, hp_ref, conv_width, extent):
    raw = v_ref[:, 0, :, conv_width : conv_width + LANES].reshape(extent, LANES) + hp_ref[1:2, :]
    step = jnp.maximum(raw, 0.0) + jnp.log1p(jnp.exp(-jnp.abs(raw)))
    return raw, step


def enter_kernel(inner, v_ref, halo_ref, cw_ref, hp_ref, xs_ref, rw_ref, dl_ref, s_ref, padded):
    extent = xs_ref.shape[1]
    width = padded.shape[1]
    pre = conv_of(v_ref, halo_ref, cw_ref, padded)
    act = pre * jax.nn.sigmoid(pre)
    xs = act[:, :inner]
    write = act[:, inner : inner + STATE_DIM]
    unused_raw, step = step_sizes(v_ref, hp_ref, width, extent)
    log_sum = dot(lower_ones(extent), -step * jnp.exp(hp_ref[0:1, :]), NN, highest)
    tail = jnp.exp(log_sum[extent - 1 : extent, :] - log_sum) * step
    spread = dot_ones(tail, head_spread(inner), NN)
    xs_ref[0] = xs
    rw_ref[0] = act[:, inner:]
    dl_ref[0, :, 0:LANES] = step
    dl_ref[0, :, LANES:] = log_sum
    s_ref[0] = dot_split(split_parts(xs * spread), split_parts(write), TN)


def mixer_enter(v, halo, cw, hp, inner):
    zs, slots, rows, cols = v.shape
    extent = zs * rows
    width = cw.shape[1]
    heads = inner // HEAD_DIM
    return pl.pallas_call(
        functools.partial(enter_kernel, inner),
        grid=(slots,),
        in_specs=[
            pl.BlockSpec((zs, 1, rows, cols), lambda s: (0, s, 0, 0)),
            pl.BlockSpec((1, 8, width), lambda s: (s, 0, 0)),
            pl.BlockSpec(cw.shape, lambda s: (0, 0)),
            pl.BlockSpec(hp.shape, lambda s: (0, 0)),
        ],
        out_specs=[
            pl.BlockSpec((1, extent, inner), lambda s: (s, 0, 0)),
            pl.BlockSpec((1, extent, 2 * STATE_DIM), lambda s: (s, 0, 0)),
            pl.BlockSpec((1, extent, 2 * LANES), lambda s: (s, 0, 0)),
            pl.BlockSpec((1, inner, STATE_DIM), lambda s: (s, 0, 0)),
        ],
        out_shape=[
            jax.ShapeDtypeStruct((slots, extent, inner), f32),
            jax.ShapeDtypeStruct((slots, extent, 2 * STATE_DIM), f32),
            jax.ShapeDtypeStruct((slots, extent, 2 * LANES), f32),
            jax.ShapeDtypeStruct((slots, inner, STATE_DIM), f32),
        ],
        scratch_shapes=[pltpu.VMEM((extent + 8, width), f32)],
        compiler_params=kernel_params(48),
        cost_estimate=taking(12, zs * slots * rows),
        name="mixer_enter",
    )(v, halo, cw, hp)


def scan_kernel(reverse, got_ref, decay_ref, out_ref):
    count = got_ref.shape[0]
    state = jnp.zeros(got_ref.shape[1:], f32)
    order = range(count - 1, -1, -1) if reverse else range(count)
    for piece in order:
        out_ref[piece] = state
        state = decay_ref[piece] * state + got_ref[piece]


def scan_pieces(got, decay, reverse):
    return pl.pallas_call(
        functools.partial(scan_kernel, reverse),
        out_shape=jax.ShapeDtypeStruct(got.shape, f32),
        compiler_params=kernel_params(32),
        name="scan_pieces",
    )(got, decay)


def exchanged(rows):
    return lax.all_to_all(rows, "dp", 0, 0, tiled=False)


def states_forward(beside, s_local, log_last):
    count = lax.axis_size("dp")
    slots, inner, _ = s_local.shape
    share = slots * inner // count
    per_row = jnp.repeat(jnp.exp(log_last).reshape(-1), HEAD_DIM).reshape(count, share)
    lines = -(-share // (8 * LANES)) * 8
    per_row = jnp.pad(per_row, ((0, 0), (0, lines * LANES - share))).reshape(count, lines, LANES)
    got = exchanged(jnp.concatenate([s_local.reshape(count, share, STATE_DIM), per_row], axis=1))
    decay = got[:, share:].reshape(count, lines * LANES)[:, :share, None]
    entering = exchanged(after(scan_pieces(got[:, :share], decay, False), beside))
    return entering.reshape(slots, inner, STATE_DIM), decay


def states_scanned(g_local, decay):
    count = lax.axis_size("dp")
    slots, inner, _ = g_local.shape
    got = exchanged(g_local.reshape(count, slots * inner // count, STATE_DIM))
    return scan_pieces(got, decay, True)


def inner_kernel(inner, xs_ref, rw_ref, dl_ref, y_ref):
    extent = xs_ref.shape[1]
    write = split_parts(rw_ref[0, :, :STATE_DIM])
    read = split_parts(rw_ref[0, :, STATE_DIM:])
    step_t = dl_ref[0, :, 0:LANES].T
    log_sum = dl_ref[0, :, LANES:]
    log_t = log_sum.T
    scores = dot_split(read, write, NT)
    causal = lax.broadcasted_iota(jnp.int32, (extent, extent), 0) >= lax.broadcasted_iota(
        jnp.int32, (extent, extent), 1
    )
    xs_low = xs_ref[0].astype(bf16)
    for head in range(inner // HEAD_DIM):
        cols = slice(head * HEAD_DIM, (head + 1) * HEAD_DIM)
        gap = log_sum[:, head : head + 1] - log_t[head : head + 1, :]
        mixing = jnp.exp(jnp.where(causal, gap, -jnp.inf)) * scores * step_t[head : head + 1, :]
        y_ref[0, :, cols] = dot(mixing.astype(bf16), xs_low[:, cols], NN)


def mixer_inner(xs, rw, dl):
    slots, extent, inner = xs.shape
    return pl.pallas_call(
        functools.partial(inner_kernel, inner),
        grid=(slots,),
        in_specs=[
            pl.BlockSpec((1, extent, inner), lambda s: (s, 0, 0)),
            pl.BlockSpec((1, extent, 2 * STATE_DIM), lambda s: (s, 0, 0)),
            pl.BlockSpec((1, extent, 2 * LANES), lambda s: (s, 0, 0)),
        ],
        out_specs=pl.BlockSpec((1, extent, inner), lambda s: (s, 0, 0)),
        out_shape=jax.ShapeDtypeStruct((slots, extent, inner), f32),
        compiler_params=kernel_params(40),
        cost_estimate=taking(9, slots * extent),
        name="mixer_inner",
    )(xs, rw, dl)


def leave_kernel(inner, yi_ref, xs_ref, rw_ref, dl_ref, h_ref, z_ref, hp_ref, gain_ref, y_ref, gg_ref, sq_ref):
    extent = xs_ref.shape[1]
    zs, _, rows, _ = z_ref.shape
    read = split_parts(rw_ref[0, :, STATE_DIM:])
    grown = dot_ones(jnp.exp(dl_ref[0, :, LANES:]), head_spread(inner), NN)
    y = yi_ref[0] + grown * dot_split(read, split_parts(h_ref[0]), NT) + hp_ref[3:4, :] * xs_ref[0]
    y_ref[0] = y
    z = z_ref[...].reshape(extent, inner)
    gated = y * (z * jax.nn.sigmoid(z))
    sq_ref[0] = jnp.broadcast_to(jnp.sum(gated * gated, axis=1, keepdims=True), (extent, LANES))
    gg_ref[...] = (gated * gain_ref[...]).astype(bf16).reshape(zs, 1, rows, inner)


def mixer_leave(yi, xs, rw, dl, h_in, z, skip, gain):
    zs, slots, rows, inner = z.shape
    extent = zs * rows
    return pl.pallas_call(
        functools.partial(leave_kernel, inner),
        grid=(slots,),
        in_specs=[
            pl.BlockSpec((1, extent, inner), lambda s: (s, 0, 0)),
            pl.BlockSpec((1, extent, inner), lambda s: (s, 0, 0)),
            pl.BlockSpec((1, extent, 2 * STATE_DIM), lambda s: (s, 0, 0)),
            pl.BlockSpec((1, extent, 2 * LANES), lambda s: (s, 0, 0)),
            pl.BlockSpec((1, inner, STATE_DIM), lambda s: (s, 0, 0)),
            pl.BlockSpec((zs, 1, rows, inner), lambda s: (0, s, 0, 0)),
            pl.BlockSpec(skip.shape, lambda s: (0, 0)),
            pl.BlockSpec(gain.shape, lambda s: (0, 0)),
        ],
        out_specs=[
            pl.BlockSpec((1, extent, inner), lambda s: (s, 0, 0)),
            pl.BlockSpec((zs, 1, rows, inner), lambda s: (0, s, 0, 0)),
            pl.BlockSpec((1, extent, LANES), lambda s: (s, 0, 0)),
        ],
        out_shape=[
            jax.ShapeDtypeStruct((slots, extent, inner), f32),
            jax.ShapeDtypeStruct((zs, slots, rows, inner), bf16),
            jax.ShapeDtypeStruct((slots, extent, LANES), f32),
        ],
        compiler_params=kernel_params(48),
        cost_estimate=taking(7, zs * slots * rows),
        name="mixer_leave",
    )(yi, xs, rw, dl, h_in, z, skip, gain)


def unmix_kernel(inner, gn_ref, y_ref, z_ref, rw_ref, dl_ref, tok_ref, gain_ref, gy_ref, gz_ref, s_ref, gg_ref):
    extent = y_ref.shape[1]
    zs, _, rows, _ = z_ref.shape
    grad = gn_ref[...].reshape(extent, inner)
    z = z_ref[...].reshape(extent, inner)
    logistic = jax.nn.sigmoid(z)
    gate = z * logistic
    y = y_ref[0]
    gated = y * gate
    inv_rms = tok_ref[0, :, 0:1]
    cross = tok_ref[0, :, 1:2]
    part = jnp.sum(grad * gated * inv_rms, axis=0, keepdims=True)

    @pl.when(pl.program_id(0) == 0)
    def _():
        gg_ref[...] = jnp.zeros_like(gg_ref)

    gg_ref[0:1, :] += part
    gated_grad = grad * gain_ref[...] * inv_rms - gated * cross
    gy = gated_grad * gate
    gy_ref[0] = gy
    gz = gated_grad * y * (logistic * (1.0 + z * (1.0 - logistic)))
    gz_ref[...] = gz.astype(bf16).reshape(zs, 1, rows, inner)
    grown = dot_ones(jnp.exp(dl_ref[0, :, LANES:]), head_spread(inner), NN)
    s_ref[0] = dot_split(split_parts(gy * grown), split_parts(rw_ref[0, :, STATE_DIM:]), TN)


def mixer_unmix(gn, y, z, rw, dl, tok, gain):
    zs, slots, rows, inner = z.shape
    extent = zs * rows
    return pl.pallas_call(
        functools.partial(unmix_kernel, inner),
        grid=(slots,),
        in_specs=[
            pl.BlockSpec((zs, 1, rows, inner), lambda s: (0, s, 0, 0)),
            pl.BlockSpec((1, extent, inner), lambda s: (s, 0, 0)),
            pl.BlockSpec((zs, 1, rows, inner), lambda s: (0, s, 0, 0)),
            pl.BlockSpec((1, extent, 2 * STATE_DIM), lambda s: (s, 0, 0)),
            pl.BlockSpec((1, extent, 2 * LANES), lambda s: (s, 0, 0)),
            pl.BlockSpec((1, extent, 2), lambda s: (s, 0, 0)),
            pl.BlockSpec(gain.shape, lambda s: (0, 0)),
        ],
        out_specs=[
            pl.BlockSpec((1, extent, inner), lambda s: (s, 0, 0)),
            pl.BlockSpec((zs, 1, rows, inner), lambda s: (0, s, 0, 0)),
            pl.BlockSpec((1, inner, STATE_DIM), lambda s: (s, 0, 0)),
            pl.BlockSpec((8, inner), lambda s: (0, 0)),
        ],
        out_shape=[
            jax.ShapeDtypeStruct((slots, extent, inner), f32),
            jax.ShapeDtypeStruct((zs, slots, rows, inner), bf16),
            jax.ShapeDtypeStruct((slots, inner, STATE_DIM), f32),
            jax.ShapeDtypeStruct((8, inner), f32),
        ],
        compiler_params=kernel_params(48),
        cost_estimate=taking(9, zs * slots * rows),
        name="mixer_unmix",
    )(gn, y, z, rw, dl, tok, gain)


def pairs_kernel(inner, xs_ref, rw_ref, dl_ref, gy_ref, gx_ref, grw_ref, gdl_ref, cols_buf):
    extent = gy_ref.shape[1]
    write = split_parts(rw_ref[0, :, :STATE_DIM])
    read = split_parts(rw_ref[0, :, STATE_DIM:])
    step = dl_ref[0, :, 0:LANES]
    log_sum = dl_ref[0, :, LANES:]
    log_t = log_sum.T
    gy_parts, xs_parts = split_parts(gy_ref[0]), split_parts(xs_ref[0])
    scores_t = dot_split(write, read, NT)
    later = lax.broadcasted_iota(jnp.int32, (extent, extent), 1) >= lax.broadcasted_iota(
        jnp.int32, (extent, extent), 0
    )
    lane = lax.broadcasted_iota(jnp.int32, (extent, LANES), 1)
    score_grad_t = jnp.zeros((extent, extent), f32)
    step_direct = jnp.zeros((extent, LANES), f32)
    cols_buf[...] = jnp.zeros_like(cols_buf)
    for head in range(inner // HEAD_DIM):
        cols = slice(head * HEAD_DIM, (head + 1) * HEAD_DIM)
        gap_t = log_t[head : head + 1, :] - log_sum[:, head : head + 1]
        decay_t = jnp.exp(jnp.where(later, gap_t, -jnp.inf))
        step_col = step[:, head : head + 1]
        pair_t = dot_split([x[:, cols] for x in xs_parts], [g[:, cols] for g in gy_parts], NT)
        both_t = decay_t * pair_t
        score_grad_t = score_grad_t + both_t * step_col
        weight_t = both_t * scores_t
        step_direct = step_direct + jnp.where(lane == head, jnp.sum(weight_t, axis=1, keepdims=True), 0.0)
        cols_buf[head : head + 1, :] = jnp.sum(weight_t * step_col, axis=0, keepdims=True)
        gx_ref[0, :, cols] = dot((decay_t * scores_t * step_col).astype(bf16), gy_parts[0][:, cols], NN)
    score_parts = split_parts(score_grad_t)
    grw_ref[0, :, :STATE_DIM] = dot_split(score_parts, read, NN)
    grw_ref[0, :, STATE_DIM:] = dot_split(score_parts, write, TN)
    gdl_ref[0, :, 0:LANES] = step_direct
    gdl_ref[0, :, LANES:] = cols_buf[...].T - step * step_direct


def mixer_pairs(xs, rw, dl, gy, *earlier):
    slots, extent, inner = xs.shape
    wide = pl.BlockSpec((1, extent, inner), lambda s: (s, 0, 0))
    two = pl.BlockSpec((1, extent, 2 * LANES), lambda s: (s, 0, 0))
    return pl.pallas_call(
        skipping(functools.partial(pairs_kernel, inner), 4, len(earlier)),
        grid=(slots,),
        in_specs=[wide, two, two, wide] + [ANYWHERE] * len(earlier),
        out_specs=[wide, two, two],
        out_shape=[
            jax.ShapeDtypeStruct((slots, extent, inner), f32),
            jax.ShapeDtypeStruct((slots, extent, 2 * STATE_DIM), f32),
            jax.ShapeDtypeStruct((slots, extent, 2 * LANES), f32),
        ],
        scratch_shapes=[pltpu.VMEM((LANES, extent), f32)],
        compiler_params=kernel_params(48),
        cost_estimate=taking(42, slots * extent),
        name="mixer_pairs",
    )(xs, rw, dl, gy, *earlier)


def back_kernel(
    inner, v_ref, halo_ref, cw_ref, hp_ref, skip_ref, rw_ref, dl_ref, gy_ref, gx_ref, grw_ref, gdl_ref, h_ref, gh_ref,
    gv_ref, gbc_ref, gp_ref, gc_ref, ghp_ref, padded, gpad,
):
    extent = gy_ref.shape[1]
    zs, _, rows, _ = v_ref.shape
    width = padded.shape[1]
    heads = inner // HEAD_DIM
    first = pl.program_id(0) == 0
    pre = conv_of(v_ref, halo_ref, cw_ref, padded)
    logistic = jax.nn.sigmoid(pre)
    slope = logistic * (1.0 + pre * (1.0 - logistic))
    xs = pre[:, :inner] * logistic[:, :inner]
    write_low = rw_ref[0, :, :STATE_DIM].astype(bf16)
    read_low = rw_ref[0, :, STATE_DIM:].astype(bf16)
    raw, step = step_sizes(v_ref, hp_ref, width, extent)
    rate = jnp.exp(hp_ref[0:1, :])
    log_sum = dl_ref[0, :, LANES:]
    gy = gy_ref[0]
    step_direct = gdl_ref[0, :, 0:LANES]
    sums = head_sums(inner)
    spread = head_spread(inner)
    last = log_sum[extent - 1 : extent, :]
    tail_decay = jnp.exp(last - log_sum)
    tail = dot_ones(tail_decay * step, spread, NN)
    grown = dot_ones(jnp.exp(log_sum), spread, NN)
    gh = gh_ref[0]
    h_in = h_ref[0]
    gh_parts, h_parts = split_parts(gh), split_parts(h_in)
    tail_in = dot(write_low, gh_parts[0], NT)
    tail_direct = tail_decay * dot_ones(xs * tail_in, sums, NN)
    tail_weight = tail_direct * step
    state_part = grown * dot(read_low, h_parts[0], NT)
    state_weight = dot_ones(gy * state_part, sums, NN)
    held = split_parts(gh * h_in)
    row_ones = jnp.ones((8, STATE_DIM), bf16)
    kept = dot_ones(dot(row_ones, held[0], NT) + dot(row_ones, held[1], NT), sums, NN)[0:1, :]
    log_grad = gdl_ref[0, :, LANES:] + state_weight - tail_weight
    end_grad = jnp.sum(tail_weight, axis=0, keepdims=True) + jnp.exp(last) * kept
    rate_arg_grad = dot(lower_ones(extent), log_grad, TN, highest) + end_grad
    step_grad = step_direct + tail_direct - rate * rate_arg_grad
    raw_grad = step_grad * jax.nn.sigmoid(raw)
    xs_grad = gx_ref[0] + tail * tail_in + skip_ref[3:4, :] * gy
    write_grad = grw_ref[0, :, :STATE_DIM] + dot_split(split_parts(tail * xs), gh_parts, NN)
    read_grad = grw_ref[0, :, STATE_DIM:] + dot_split(split_parts(grown * gy), h_parts, NN)
    valid_lane = lax.broadcasted_iota(jnp.int32, (1, LANES), 1) < heads
    rate_grad = jnp.where(valid_lane, jnp.sum(-step * rate * rate_arg_grad, axis=0, keepdims=True), 0.0)
    raw_grad = jnp.where(valid_lane, raw_grad, 0.0)
    skip_grad = jnp.sum(dot_ones(gy * xs, sums, NN), axis=0, keepdims=True)

    @pl.when(first)
    def _():
        gc_ref[...] = jnp.zeros_like(gc_ref)
        ghp_ref[...] = jnp.zeros_like(ghp_ref)

    ghp_ref[0:1, :] += rate_grad
    ghp_ref[1:2, :] += jnp.sum(raw_grad, axis=0, keepdims=True)
    ghp_ref[2:3, :] += skip_grad
    gpad[0:8, :] = jnp.zeros((8, width), f32)
    gpad[extent + 8 :, :] = jnp.zeros((8, width), f32)
    gpad[8 : extent + 8, 0:inner] = xs_grad * slope[:, 0:inner]
    gpad[8 : extent + 8, inner : inner + STATE_DIM] = write_grad * slope[:, inner : inner + STATE_DIM]
    gpad[8 : extent + 8, inner + STATE_DIM :] = read_grad * slope[:, inner + STATE_DIM :]
    back = jnp.zeros((extent, width), f32)
    before = jnp.zeros((8, width), f32)
    pre_grad = gpad[8 : extent + 8, :]
    for tap in range(CONV_WIDTH):
        ahead = CONV_WIDTH - 1 - tap
        weight = cw_ref[tap : tap + 1, :]
        back = back + weight * gpad[8 + ahead : 8 + ahead + extent, :]
        before = before + weight * gpad[ahead : 8 + ahead, :]
        gc_ref[tap : tap + 1, :] += jnp.sum(pre_grad * padded[5 + tap : 5 + tap + extent, :], axis=0, keepdims=True)
    gc_ref[CONV_WIDTH : CONV_WIDTH + 1, :] += jnp.sum(pre_grad, axis=0, keepdims=True)
    gp_ref[0] = before
    gv_ref[:, :, :, 0:inner] = back[:, :inner].astype(bf16).reshape(zs, 1, rows, inner)
    gbc_ref[...] = back[:, inner:].reshape(zs, 1, rows, width - inner)
    gv_ref[:, :, :, inner:] = raw_grad.astype(bf16).reshape(zs, 1, rows, LANES)


def mixer_back(v, halo, cw, hp, skip, rw, dl, gy, gx, grw, gdl, h_in, gh):
    zs, slots, rows, cols = v.shape
    extent = zs * rows
    inner = gy.shape[2]
    width = cw.shape[1]
    wide = pl.BlockSpec((1, extent, inner), lambda s: (s, 0, 0))
    two = pl.BlockSpec((1, extent, 2 * LANES), lambda s: (s, 0, 0))
    state = pl.BlockSpec((1, inner, STATE_DIM), lambda s: (s, 0, 0))
    return pl.pallas_call(
        functools.partial(back_kernel, inner),
        grid=(slots,),
        in_specs=[
            pl.BlockSpec((zs, 1, rows, cols), lambda s: (0, s, 0, 0)),
            pl.BlockSpec((1, 8, width), lambda s: (s, 0, 0)),
            pl.BlockSpec(cw.shape, lambda s: (0, 0)),
            pl.BlockSpec(hp.shape, lambda s: (0, 0)),
            pl.BlockSpec(skip.shape, lambda s: (0, 0)),
            two,
            two,
            wide,
            wide,
            two,
            two,
            state,
            state,
        ],
        out_specs=[
            pl.BlockSpec((zs, 1, rows, inner + LANES), lambda s: (0, s, 0, 0)),
            pl.BlockSpec((zs, 1, rows, 2 * STATE_DIM), lambda s: (0, s, 0, 0)),
            pl.BlockSpec((1, 8, width), lambda s: (s, 0, 0)),
            pl.BlockSpec((8, width), lambda s: (0, 0)),
            pl.BlockSpec((8, LANES), lambda s: (0, 0)),
        ],
        out_shape=[
            jax.ShapeDtypeStruct((zs, slots, rows, inner + LANES), bf16),
            jax.ShapeDtypeStruct((zs, slots, rows, 2 * STATE_DIM), f32),
            jax.ShapeDtypeStruct((slots, 8, width), f32),
            jax.ShapeDtypeStruct((8, width), f32),
            jax.ShapeDtypeStruct((8, LANES), f32),
        ],
        scratch_shapes=[
            pltpu.VMEM((extent + 8, width), f32),
            pltpu.VMEM((extent + 16, width), f32),
        ],
        compiler_params=kernel_params(56),
        cost_estimate=taking(18, zs * slots * rows),
        name="mixer_back",
    )(v, halo, cw, hp, skip, rw, dl, gy, gx, grw, gdl, h_in, gh)


def expert_kernel(
    n_ref, g_ref, mask_ref, router_ref, up_ref, down_ref,
    moe_ref, back_ref, logit_ref, act_ref, hid_ref, moe_sum, back_sum, gates_buf, gate_grad,
):
    pair = pl.program_id(0)
    pairs = pl.num_programs(0)
    tokens = n_ref.shape[0]
    lane = lax.broadcasted_iota(jnp.int32, (tokens, LANES), 1)
    half = up_ref.shape[3] // 2

    @pl.when(pair == 0)
    def _():
        logits = dot(n_ref[...], router_ref[...], NN)
        chosen = mask_ref[...] > 0.0
        logits = jnp.where(chosen, logits, -jnp.inf)
        powers = jnp.exp(logits - jnp.max(logits, axis=1, keepdims=True))
        gates = powers / jnp.sum(powers, axis=1, keepdims=True)
        gates_buf[...] = jnp.where(lane < EXPERTS, gates, 1.0)
        moe_sum[...] = jnp.zeros_like(moe_sum)
        back_sum[...] = jnp.zeros_like(back_sum)
        gate_grad[...] = jnp.zeros_like(gate_grad)

    depth = up_ref.shape[0] * up_ref.shape[2]
    down = down_ref[...].reshape(depth, 2 * half)
    n_val = n_ref[...]
    gates = gates_buf[...]
    act_back = dot(g_ref[...], down, NN)
    ups = [up_ref[:, member].reshape(depth, 2 * half) for member in range(2)]
    for member in range(2):
        hidden = dot(n_val, ups[member], NN)
        gate_part, up_part = hidden[:, :half], hidden[:, half:]
        logistic = jax.nn.sigmoid(gate_part)
        silu = gate_part * logistic
        act = (silu * up_part).astype(bf16).astype(f32)
        own = lane == 2 * pair + member
        gate = jnp.sum(jnp.where(own, gates, 0.0), axis=1, keepdims=True)
        part = act_back[:, member * half : (member + 1) * half]
        gate_grad[...] += jnp.where(own, jnp.sum(act * part, axis=1, keepdims=True), 0.0)
        act_ref[0, :, member * half : (member + 1) * half] = (gate * act).astype(bf16)
        part = part * gate
        first_col = 2 * member * half
        hid_ref[0, :, first_col : first_col + half] = (part * up_part * (logistic * (1.0 + gate_part * (1.0 - logistic)))).astype(bf16)
        hid_ref[0, :, first_col + half : first_col + 2 * half] = (part * silu).astype(bf16)
    moe_sum[...] += dot(act_ref[0], down, NT)
    back_sum[...] += dot(hid_ref[0], jnp.concatenate(ups, axis=1), NT)

    @pl.when(pair == pairs - 1)
    def _():
        gates_in = jnp.where(lane < EXPERTS, gates, 0.0)
        grads = gates_in * gate_grad[...]
        logit_grad = (grads - gates_in * jnp.sum(grads, axis=1, keepdims=True)).astype(bf16)
        logit_ref[...] = logit_grad
        back_ref[...] = (back_sum[...] + dot(logit_grad, router_ref[...], NT)).astype(bf16)
        moe_ref[...] = moe_sum[...].astype(bf16)


def experts(n_two, g_moe, mask, router, weights):
    tokens, width = n_two.shape
    count, blocks, rows, cols = weights.shape
    pairs = blocks // 3
    down_at = 2 * pairs
    return pl.pallas_call(
        expert_kernel,
        grid=(pairs,),
        in_specs=[
            pl.BlockSpec((tokens, width), lambda p: (0, 0)),
            pl.BlockSpec((tokens, width), lambda p: (0, 0)),
            pl.BlockSpec((tokens, LANES), lambda p: (0, 0)),
            pl.BlockSpec((width, LANES), lambda p: (0, 0)),
            pl.BlockSpec((count, 2, rows, cols), lambda p: (0, p, 0, 0)),
            pl.BlockSpec((count, 1, rows, cols), lambda p: (0, down_at + p, 0, 0)),
        ],
        out_specs=[
            pl.BlockSpec((tokens, width), lambda p: (0, 0)),
            pl.BlockSpec((tokens, width), lambda p: (0, 0)),
            pl.BlockSpec((tokens, LANES), lambda p: (0, 0)),
            pl.BlockSpec((1, tokens, cols), lambda p: (p, 0, 0)),
            pl.BlockSpec((1, tokens, 2 * cols), lambda p: (p, 0, 0)),
        ],
        out_shape=[
            jax.ShapeDtypeStruct((tokens, width), bf16),
            jax.ShapeDtypeStruct((tokens, width), bf16),
            jax.ShapeDtypeStruct((tokens, LANES), bf16),
            jax.ShapeDtypeStruct((pairs, tokens, cols), bf16),
            jax.ShapeDtypeStruct((pairs, tokens, 2 * cols), bf16),
        ],
        scratch_shapes=[
            pltpu.VMEM((tokens, width), f32),
            pltpu.VMEM((tokens, width), f32),
            pltpu.VMEM((tokens, LANES), f32),
            pltpu.VMEM((tokens, LANES), f32),
        ],
        compiler_params=kernel_params(60),
        cost_estimate=taking(72, tokens),
        name="experts",
    )(n_two, g_moe, mask, router, weights, weights)


def expert_grad_kernel(up_blocks, chunks, *refs):
    n_refs, g_refs, h_refs, a_refs = (refs[i * chunks : (i + 1) * chunks] for i in range(4))
    out_ref, turned = refs[4 * chunks :]
    block = pl.program_id(0)
    count, _, rows, cols = out_ref.shape
    tokens = n_refs[0].shape[0]

    def turn(sources):
        for at, source in enumerate(sources):
            turned[:, at * tokens : (at + 1) * tokens] = source[...].T

    def summed_over(rights):
        total = dot(turned[:, 0:tokens], rights[0][0], NN)
        for at in range(1, chunks):
            total = total + dot(turned[:, at * tokens : (at + 1) * tokens], rights[at][0], NN)
        out_ref[...] = total.astype(bf16).reshape(count, 1, rows, cols)

    @pl.when(block == 0)
    def _():
        turn(n_refs)

    @pl.when(block == up_blocks)
    def _():
        turn(g_refs)

    @pl.when(block < up_blocks)
    def _():
        summed_over(h_refs)

    @pl.when(block >= up_blocks)
    def _():
        summed_over(a_refs)


def expert_grads(n_list, g_list, hid_list, act_list, count, *earlier):
    chunks = len(n_list)
    tokens, width = n_list[0].shape
    cols = 2 * LANES
    hid_wide, act_wide = (values[0].shape[2] // cols for values in (hid_list, act_list))
    ups = hid_list[0].shape[0] * hid_wide
    downs = act_list[0].shape[0] * act_wide
    blocks = ups + downs
    whole = pl.BlockSpec((tokens, width), lambda b: (0, 0))

    def hid_at(b):
        b = jnp.minimum(b, ups - 1)
        return b // hid_wide, 0, b % hid_wide

    def act_at(b):
        b = jnp.maximum(b - ups, 0)
        return b // act_wide, 0, b % act_wide

    return pl.pallas_call(
        skipping(functools.partial(expert_grad_kernel, ups, chunks), 4 * chunks, len(earlier)),
        grid=(blocks,),
        in_specs=[whole] * (2 * chunks)
        + [pl.BlockSpec((1, tokens, cols), hid_at)] * chunks
        + [pl.BlockSpec((1, tokens, cols), act_at)] * chunks
        + [ANYWHERE] * len(earlier),
        out_specs=pl.BlockSpec((count, 1, width // count, cols), lambda b: (0, b, 0, 0)),
        out_shape=jax.ShapeDtypeStruct((count, blocks, width // count, cols), bf16),
        scratch_shapes=[pltpu.VMEM((width, chunks * tokens), bf16)],
        compiler_params=kernel_params(48),
        cost_estimate=taking(4 * blocks / 3, chunks * tokens),
        name="expert_grads",
    )(*n_list, *g_list, *hid_list, *act_list, *earlier)


def body(
    block_input,
    out_grad,
    lengths,
    routes,
    norm1_gain,
    w_zx,
    w_bc,
    w_dt,
    conv_x,
    conv_bc,
    head_params,
    gate_gain,
    w_out,
    norm2_gain,
    w_router,
    w_gu,
    w_dn,
    s_gu,
    s_dn,
):
    zs = lax.axis_size("tensor")
    pieces = lax.axis_size("dp")
    own = lax.axis_index("tensor")
    wide_index = lax.axis_index("dp")
    rows = block_input.shape[0]
    piece_rows = rows * zs
    heads = HEAD_COUNT // zs
    inner = INNER_DIM // zs
    width = inner + 2 * STATE_DIM
    shard = D_MODEL // pieces
    half = w_gu.shape[3]
    rim = CONV_WIDTH - 1
    per = SLOT_COUNT // CHUNKS
    tokens = per * rows
    chunk_ids = range(CHUNKS)

    enter_shard = jnp.concatenate(
        [w_zx[:, 1], w_bc, jnp.pad(w_dt, ((0, 0), (0, LANES - heads)))], axis=1
    )
    side_shard = jnp.concatenate(
        [w_zx[:, 0], w_out.T, jnp.pad(w_router, ((0, 0), (0, LANES - EXPERTS)))], axis=1
    )
    expert_shard = jnp.concatenate(
        [
            w_gu.reshape(EXPERTS, shard, 2 * half),
            s_gu.reshape(shard, 2, 2, half).transpose(2, 0, 1, 3).reshape(2, shard, 2 * half),
            w_dn.reshape(EXPERTS // 2, 2 * half, shard).transpose(0, 2, 1),
            s_dn.T[None],
        ],
        axis=0,
    )

    def by_slot(values):
        return jnp.transpose(values, (1, 0, 2))

    def part(values, c):
        return values[c * per : (c + 1) * per].reshape((tokens,) + values.shape[2:])

    u_slots = by_slot(block_input)
    u_low = [row_major(part(u_slots, c)) for c in chunk_ids]
    u_all = [in_order(line_gather(u_low[c])) for c in chunk_ids]
    full_enter = weight_gather(enter_shard).reshape(D_MODEL, width + LANES)
    gains = jnp.stack([norm1_gain, norm2_gain], axis=1).astype(f32)
    gains = lax.all_gather(gains, "dp", axis=0, tiled=True)
    gain_one, gain_two = gains[:, 0], gains[:, 1]
    full_side = weight_gather(side_shard).reshape(D_MODEL, 2 * inner + LANES)
    full_z, full_out, full_router = full_side[:, :inner], full_side[:, inner : 2 * inner], full_side[:, 2 * inner :]

    positions = wide_index * piece_rows + own * rows + jnp.arange(rows, dtype=jnp.int32)
    valid = (positions[None, :] < lengths[:, None]).astype(f32)[:, :, None]
    grad_slots = by_slot(out_grad).astype(f32) * valid

    conv_w = jnp.pad(jnp.concatenate([conv_x, conv_bc], axis=1), ((0, 8 - CONV_WIDTH - 1), (0, 0)))
    hp = jnp.pad(head_params, ((0, 5), (0, LANES - heads)))
    skip = jnp.pad(jnp.repeat(head_params[2], HEAD_DIM)[None], ((3, 4), (0, 0)))
    gain_row = gate_gain[None]

    hot = jnp.sum(
        (routes[..., None] == jnp.arange(LANES, dtype=jnp.int32)).astype(f32), axis=2
    )
    hot = jnp.transpose(hot.reshape(zs, rows, SLOT_COUNT, LANES), (0, 2, 1, 3))

    hot_at = by_distance(hot)

    def flat(values):
        return values.reshape((zs * tokens,) + values.shape[2:])

    def in_slots(values):
        return values.reshape((zs, per, rows) + values.shape[1:])

    u = [row_major(u_low[c].astype(f32)) for c in chunk_ids]
    valid_c = [part(valid, c) for c in chunk_ids]
    grad_c = [row_major(part(grad_slots, c)) for c in chunk_ids]
    n_one, v, z, halo, entered = [], [], [], [], []
    for c in chunk_ids:
        n_one.append(row_major(rms_scale(flat(u_all[c]).astype(f32), gain_one).astype(bf16)))
        v.append(in_slots(dot(n_one[c], full_enter, NN)))
        rim_rows = in_slots(n_one[c])[zs - 1, :, rows - rim :]
        prior = dot(passed_along(rim_rows, "dp", 1).reshape(per * rim, D_MODEL), full_enter[:, :width], NN)
        halo.append(jnp.pad(prior.reshape(per, rim, width), ((0, 0), (8 - rim, 0), (0, 0))))
    g_blocks = [line_gather(after(grad_c[c].astype(bf16), u_all[CHUNKS - 1])) for c in chunk_ids]
    for c in chunk_ids:
        entered.append(mixer_enter(v[c], halo[c], conv_w, hp, inner))
    resid, mixed_all, y_all, h_all, decay_all, inv_alls, gg_all, n_two = [], [], [], [], [], [], [], []
    for c in chunk_ids:
        xs, rw, dl, s_local = entered[c]
        yi = mixer_inner(xs, rw, dl)
        z.append(in_slots(dot(n_one[c], full_z, NN)))
        s_local = after(s_local, g_blocks[c][1], g_blocks[c][3])
        h_in, decay = states_forward(g_blocks[c][2], s_local, dl[:, piece_rows - 1, LANES : LANES + heads])
        if c == 0:
            full_expert = weight_gather(after(expert_shard, h_in))
        y, gg, squares = mixer_leave(yi, xs, rw, dl, h_in, z[c], skip, gain_row)
        product = dot(flat(gg.reshape(zs, tokens, inner)), full_out, NT).astype(bf16)
        product = product.reshape(zs, tokens, D_MODEL)
        square_sum = lax.psum(squares[:, :, 0], "tensor")
        inv_all = lax.rsqrt(square_sum / INNER_DIM + norm_eps)
        y_all.append(y)
        h_all.append(h_in)
        decay_all.append(decay)
        inv_alls.append(inv_all)
        gg_all.append(gg)

    few = tokens // HALVES
    halves = range(HALVES)

    def half_of(values, m):
        return values[m * few : (m + 1) * few]

    inv_own = lax.dynamic_slice_in_dim(inv_alls[0], own * rows, rows, 1).reshape(tokens, 1)
    mixed_own = summed(line_parts(by_distance(product))) * inv_own
    resid_own = row_major(u[0] + mixed_own)
    normed_two = row_major(rms_scale(resid_own, gain_two).astype(bf16))
    n_two_low, n_two, g_moe, masks = [], [], [], []
    for m in halves:
        low = half_of(normed_two, m)
        if m > 0:
            low = after(low, *n_two_low[m - 1][1:])
        n_two_low.append(line_gather(low))
        g_moe.append(jnp.concatenate([half_of(block, m) for block in g_blocks[0]], axis=0))
        masks.append(jnp.concatenate([half_of(part(hot_at(k), 0), m) for k in range(zs)], axis=0))
    moe_part, back_part, logit_grads, acts, hids = [], [], [], [], []
    for m in halves:
        if m > 0:
            n_two_low[m][1] = after(n_two_low[m][1], back_part[m - 1])
        n_two.append(jnp.concatenate(n_two_low[m], axis=0))
        results = experts(n_two[m], g_moe[m], masks[m], full_router, full_expert)
        moe_part.append(results[0].reshape(zs, few, D_MODEL))
        back_part.append(results[1].reshape(zs, few, D_MODEL))
        logit_grads.append(results[2])
        acts.append(results[3])
        hids.append(results[4])

    def norm_back(values, gain_vec, grads):
        return jax.vjp(rms_scale, values, gain_vec)[1](grads)

    back_blocks = []
    for m in halves:
        sent = back_part[m]
        if m > 0:
            sent = after(sent, *back_blocks[m - 1][1:])
        back_blocks.append(line_parts(lambda k: sent[k]))
    n_two_grad = jnp.concatenate([summed(blocks) for blocks in back_blocks], axis=0)
    from_norm, gain_two_grad = norm_back(resid_own, gain_two, n_two_grad)
    resid_grad = [row_major(grad_c[0] + from_norm)]
    low = resid_grad[0].astype(bf16)
    low_blocks = line_gather(low)
    gathered = in_order(low_blocks)
    expert_grad = weight_scatter(after(expert_grads(n_two, g_moe, hids, acts, pieces), gathered))
    g_mixed = [flat(gathered)]
    unmixed, scanned, pairs, toks, gate_gain_grad = [], [], [], [], 0.0
    for c in chunk_ids:
        grad = in_slots(dot(g_mixed[c], full_out, NN))
        xs, rw, dl, _ = entered[c]
        inv_all = inv_alls[c]
        y_like = jnp.transpose(y_all[c].reshape(per, zs, rows, inner), (1, 0, 2, 3))
        cross = jnp.sum(grad * gain_row * y_like * jax.nn.silu(z[c]), axis=-1)
        cross = lax.psum(jnp.transpose(cross, (1, 0, 2)).reshape(per, piece_rows), "tensor")
        tok = jnp.stack([inv_all, cross * (inv_all * inv_all * inv_all) / INNER_DIM], axis=-1)
        gy, gz, g_local, gg_grad = mixer_unmix(grad, y_all[c], z[c], rw, dl, tok, gain_row)
        toks.append(tok)
        gate_gain_grad = gate_gain_grad + gg_grad[0]
        unmixed.append((gy, gz))
        scanned.append(states_scanned(g_local, decay_all[c]))
        pairs.append(mixer_pairs(xs, rw, dl, gy))

    moe_blocks = []
    for m in halves:
        held = after(moe_part[m], *toks)
        moe_blocks.append(line_parts(lambda k: held[k]))
    sooner = [block for blocks in moe_blocks for block in blocks[1::2]]
    later = [block for blocks in moe_blocks for block in blocks[2::2]]
    moe = [summed(blocks) for blocks in moe_blocks]
    moe_own = jnp.concatenate(moe, axis=0)
    output = [resid_own + moe_own]
    stat_terms = jnp.stack(
        [
            jnp.sum(valid_c[0] * output[0] * output[0]),
            jnp.sum(valid_c[0] * mixed_own * mixed_own),
            jnp.sum(valid_c[0] * moe_own * moe_own),
        ]
    )
    router_grad = sum(dot(n_two[m], logit_grads[m], TN)[:, :EXPERTS] for m in halves)

    def rows_of(values):
        return jnp.concatenate([v.reshape(zs * tokens, -1) for v in values], axis=0)

    inv_rows = [
        jnp.transpose(inv_alls[c].reshape(per, zs, rows), (1, 0, 2)).reshape(zs * tokens, 1) for c in chunk_ids
    ]
    scaled = [(g_mixed[c].astype(f32) * inv_rows[c]).astype(bf16) for c in chunk_ids]
    n_rows = rows_of(n_one)
    gg_row, gz_row = (values.reshape(1, zs * tokens, inner) for values in (gg_all[0], unmixed[0][1]))
    side_products = expert_grads(scaled, [n_rows], [gg_row], [gz_row], pieces)

    v_grads, bc_grads, conv_grad, head_grad = [], [], 0.0, 0.0
    full_x = jnp.concatenate([full_enter[:, :inner], full_enter[:, width:]], axis=1)
    full_bc = full_enter[:, inner:width]
    full_bc = jnp.concatenate([full_bc, full_bc], axis=1)
    for c in chunk_ids:
        gy, gz = unmixed[c]
        xs, rw, dl, _ = entered[c]
        gh = exchanged(after(scanned[c], pairs[c][0], *sooner)).reshape(h_all[c].shape)
        gv, gbc, g_rim, gc, ghp = mixer_back(
            v[c], halo[c], conv_w, hp, skip, rw, dl, gy, *pairs[c], h_all[c], gh
        )
        conv_grad = conv_grad + gc
        head_grad = head_grad + ghp
        following = passed_along(g_rim[:, 8 - rim :].astype(bf16), "dp", -1).astype(f32)
        edge = gv[zs - 1, :, rows - rim :, :inner].astype(f32) + following[:, :, :inner]
        gv = lax.dynamic_update_slice(gv, edge.astype(bf16)[None], (zs - 1, 0, rows - rim, 0))
        edge = gbc[zs - 1, :, rows - rim :] + following[:, :, inner:]
        gbc = lax.dynamic_update_slice(gbc, edge[None], (zs - 1, 0, rows - rim, 0))
        v_grads.append(gv)
        bc_grads.append(after(jnp.concatenate(split_parts(gbc), axis=-1), *later))
    n_parts, arrived, gain_one_grad = [], [], 0.0
    for c in chunk_ids:
        n_grad = (
            dot(unmixed[c][1].reshape(zs * tokens, inner), full_z, NT)
            + dot(v_grads[c].reshape(zs * tokens, inner + LANES), full_x, NT)
            + dot(bc_grads[c].reshape(zs * tokens, 4 * STATE_DIM), full_bc, NT)
        )
        every = flat(u_all[c]).astype(f32)
        scale = lax.rsqrt(jnp.mean(every * every, axis=-1, keepdims=True) + norm_eps)
        gain_one_grad = gain_one_grad + jnp.sum(n_grad * (every * scale), axis=0)
        n_parts.append(n_grad.astype(bf16))
        received = line_parts(by_distance(n_parts[c].reshape(zs, tokens, D_MODEL)))
        arrived.append(received)
    enter_w_grad = dot(n_rows, rows_of(v_grads), TN).astype(bf16)
    bc_w_grad = dot(n_rows, rows_of(bc_grads), TN)
    bc_w_grad = bc_w_grad[:, : 2 * STATE_DIM] + bc_w_grad[:, 2 * STATE_DIM :]
    side_grad = weight_scatter(after(side_products, expert_grad, conv_grad))

    def mixer_scatter(grads):
        return weight_scatter(after(grads.reshape(pieces, shard, -1), side_grad)).astype(f32)

    side = side_grad.astype(f32)
    fold = side.shape[0] // 2
    z_part = jnp.transpose(side[fold:], (1, 0, 2)).reshape(shard, inner)
    out_part = jnp.transpose(side[:fold], (0, 2, 1)).reshape(inner, shard)
    enter_part = mixer_scatter(enter_w_grad)
    expert_grad = expert_grad.astype(f32)
    ups, downs = EXPERTS + 2, EXPERTS // 2
    expert_outs = (
        expert_grad[:EXPERTS].reshape(EXPERTS, shard, 2, half),
        expert_grad[ups : ups + downs].transpose(0, 2, 1).reshape(EXPERTS, half, shard),
        expert_grad[EXPERTS:ups].reshape(2, shard, 2, half).transpose(1, 2, 0, 3).reshape(shard, 2, 2 * half),
        expert_grad[ups + downs].T,
    )

    def to_shares(values, dim):
        size = values.shape[dim] // (pieces * zs)
        values = jnp.moveaxis(values, dim, 0).reshape(pieces, zs, size, -1)
        return jnp.moveaxis(values, 3, 2).reshape(pieces, zs, -1)

    column = own * inner
    conv_x_full = lax.dynamic_update_slice(
        jnp.zeros((CONV_WIDTH + 1, INNER_DIM), f32), conv_grad[: CONV_WIDTH + 1, :inner], (jnp.int32(0), column)
    )
    gate_full = lax.dynamic_update_slice(jnp.zeros((INNER_DIM,), f32), gate_gain_grad, (column,))
    small = [
        (gain_one_grad, 0),
        (conv_x_full, 1),
        (conv_grad[: CONV_WIDTH + 1, inner:], 1),
        (gate_full, 0),
        (gain_two_grad, 0),
        (router_grad, 0),
    ]
    shares = [to_shares(values, dim) for values, dim in small]
    sizes = [share.shape[2] for share in shares]
    shares = jnp.concatenate(shares, axis=2)
    length = shares.shape[2]
    shares = jnp.pad(shares, ((0, 0), (0, 0), (0, -length % (8 * LANES))))
    wide_share = bc_w_grad.reshape(pieces, zs, -1, LANES)
    tile = jnp.zeros((8, LANES), f32)
    tile = tile.at[:3, :heads].set(head_grad[:3, :heads]).at[3, :3].set(stat_terms)
    tile = jnp.broadcast_to(tile, (pieces, zs) + tile.shape)
    shares = jnp.concatenate([wide_share, shares.reshape(pieces, zs, -1, LANES), tile], axis=2)
    shares = after(shares, arrived[CHUNKS - 1][1])
    shares = jnp.sum(lax.all_to_all(shares, "dp", 0, 0), axis=0)
    first_sum = after(shares, arrived[0][2])
    shares = first_sum
    got = lax.all_to_all(shares, "tensor", 0, 0)
    tiles = got[:, -8:]
    shares = jnp.sum(got[:, :-8], axis=0)
    u_grad = []
    for c in chunk_ids:
        received = arrived[c]
        if c == CHUNKS - 1:
            received[3] = after(received[3], first_sum, *expert_outs)
        u_grad.append(resid_grad[c] + norm_back(u[c], gain_one, summed(received))[0])
    bc_lines = wide_share.shape[2]
    bc_grad = shares[:bc_lines].reshape(-1, 2 * STATE_DIM)
    shares = shares[bc_lines:].reshape(-1)
    ends = [sum(sizes[: k + 1]) for k in range(len(sizes))]
    took = []
    for (values, dim), size, end in zip(small, sizes, ends):
        share = shares[end - size : end]
        if values.ndim == 2:
            other = values.shape[1 - dim]
            share = share.reshape(other, size // other)
            share = share if dim == 1 else share.T
        took.append(share)
    head_sum = jnp.transpose(tiles[:, :3, :heads], (1, 0, 2)).reshape(3, HEAD_COUNT)
    stat_sum = jnp.sum(tiles[:, 3, :3], axis=0)
    stats = jnp.sqrt(stat_sum / (jnp.sum(lengths).astype(f32) * D_MODEL))

    def placed_back(values):
        whole = jnp.concatenate([value.astype(bf16).reshape(per, rows, D_MODEL) for value in values], axis=0)
        return jnp.transpose(whole, (1, 0, 2))

    return (
        placed_back(output),
        placed_back(u_grad),
        took[0],
        jnp.stack([z_part, enter_part[:, :inner]], axis=1),
        bc_grad,
        enter_part[:, inner : inner + heads],
        took[1],
        took[2],
        head_sum,
        took[3],
        out_part,
        took[4],
        took[5],
        *expert_outs,
        stats,
    )


def solution(mesh):
    both = ("dp", "tensor")
    placed = (
        P(both, None, None),
        P(both, None, None),
        P(),
        P("dp", None, None),
        P("dp"),
        P("dp", None, "tensor"),
        P("dp", None),
        P("dp", "tensor"),
        P(None, "tensor"),
        P(),
        P(None, "tensor"),
        P("tensor"),
        P("tensor", "dp"),
        P("dp"),
        P("dp", None),
        P(None, "dp", None, "tensor"),
        P(None, "tensor", "dp"),
        P("dp", None, "tensor"),
        P("tensor", "dp"),
    )
    return jax.shard_map(
        body,
        mesh=mesh,
        in_specs=placed,
        out_specs=(
            P(both, None, None),
            P(both, None, None),
            P(both),
            P("dp", None, "tensor"),
            P(both, None),
            P("dp", "tensor"),
            P(None, both),
            P(None, both),
            P(),
            P(both),
            P("tensor", "dp"),
            P(both),
            P(both, None),
            P(None, "dp", None, "tensor"),
            P(None, "tensor", "dp"),
            P("dp", None, "tensor"),
            P("tensor", "dp"),
            P(),
        ),
        check_vma=False,
    )
```

```python
import functools

import jax
import jax.numpy as jnp
from jax import lax
from jax.experimental import pallas as pl
from jax.experimental.layout import Layout, with_layout_constraint
from jax.experimental.pallas import tpu as pltpu
from jax.sharding import PartitionSpec as P

D_MODEL = 1536
HEAD_COUNT = 48
HEAD_DIM = 64
STATE_DIM = 128
CONV_WIDTH = 4
TOP_K = 6
EXPERTS = 16
SLOT_COUNT = 4
INNER_DIM = 3072
LANES = 128
CHUNKS = 1
HALVES = 2

norm_eps = 1e-05
highest = lax.Precision.HIGHEST
f32 = jnp.float32
bf16 = jnp.bfloat16


def passed_along(value, axis, steps):
    count = lax.axis_size(axis)
    first, last = (max(0, -steps), min(count, count - steps))
    return lax.ppermute(value, axis, [(source, source + steps) for source in range(first, last)])


def row_major(value):
    return with_layout_constraint(value, Layout(major_to_minor=tuple(range(value.ndim))))


def line_gather(value):
    size = lax.axis_size("tensor")
    return [value] + [
        row_major(lax.ppermute(row_major(value), "tensor", [(a, (a - step) % size) for a in range(size)]))
        for step in range(1, size)
    ]


def line_parts(block_of):
    size = lax.axis_size("tensor")
    return [block_of(0)] + [
        lax.ppermute(row_major(block_of(step)), "tensor", [(a, (a + step) % size) for a in range(size)])
        for step in range(1, size)
    ]


def summed(parts):
    total = parts[0].astype(f32)
    for part in parts[1:]:
        total = total + part.astype(f32)
    return row_major(total)


def in_order(blocks):
    size = len(blocks)
    own = lax.axis_index("tensor")
    whole = jnp.zeros((size,) + blocks[0].shape, blocks[0].dtype)
    for k in range(size):
        whole = lax.dynamic_update_index_in_dim(whole, blocks[k], (own + k) % size, 0)
    return whole


def by_distance(whole):
    size = whole.shape[0]
    own = lax.axis_index("tensor")
    return lambda k: lax.dynamic_index_in_dim(whole, (own + k) % size, 0, False)


def weight_gather(shard):
    return lax.all_gather(shard, "dp", axis=0, tiled=False)


def weight_scatter(grads):
    return row_major(lax.psum_scatter(grads.astype(bf16), "dp", scatter_dimension=0, tiled=False))


def rms_scale(values, gain_vec):
    return (
        values * lax.rsqrt(jnp.mean(values * values, axis=-1, keepdims=True) + norm_eps) * gain_vec
    )


def silu_slope(values):
    logistic = jax.nn.sigmoid(values)
    return logistic * (1.0 + values * (1.0 - logistic))


def dot(a, b, dims, precision=None):
    return lax.dot_general(a, b, (dims, ((), ())), precision=precision, preferred_element_type=f32)


def split_parts(values):
    upper = values.astype(bf16)
    return upper, (values - upper.astype(f32)).astype(bf16)


def dot_split(a, b, dims):
    return dot(a[0], b[0], dims) + (dot(a[0], b[1], dims) + dot(a[1], b[0], dims))


def dot_ones(values, ones, dims):
    upper, lower = split_parts(values)
    return dot(upper, ones, dims) + dot(lower, ones, dims)


def after(value, *others):
    anywhere = pl.BlockSpec(memory_space=pl.ANY)
    return pl.pallas_call(
        lambda *refs: None,
        in_specs=[anywhere] * (1 + len(others)),
        out_specs=anywhere,
        out_shape=jax.ShapeDtypeStruct(value.shape, value.dtype),
        input_output_aliases={0: 0},
        name="after",
    )(value, *others)


def skipping(kernel, first, count):
    return lambda *refs: kernel(*refs[:first], *refs[first + count :])


ANYWHERE = pl.BlockSpec(memory_space=pl.ANY)
NN = ((1,), (0,))
NT = ((1,), (1,))
TN = ((0,), (0,))


def head_spread(inner):
    row = lax.broadcasted_iota(jnp.int32, (LANES, inner), 0)
    col = lax.broadcasted_iota(jnp.int32, (LANES, inner), 1)
    return (col // HEAD_DIM == row).astype(bf16)


def head_sums(inner):
    row = lax.broadcasted_iota(jnp.int32, (inner, LANES), 0)
    col = lax.broadcasted_iota(jnp.int32, (inner, LANES), 1)
    return (row // HEAD_DIM == col).astype(bf16)


def lower_ones(extent):
    row = lax.broadcasted_iota(jnp.int32, (extent, extent), 0)
    col = lax.broadcasted_iota(jnp.int32, (extent, extent), 1)
    return (row >= col).astype(f32)


def kernel_params(mib):
    return pltpu.CompilerParams(vmem_limit_bytes=mib * 1024 * 1024)


def taking(micros, tokens):
    return pl.CostEstimate(flops=int(micros * tokens * 1.1e6), bytes_accessed=1024, transcendentals=0)


def conv_of(v_ref, halo_ref, cw_ref, padded):
    extent = padded.shape[0] - 8
    width = padded.shape[1]
    padded[0:8, :] = halo_ref[0]
    padded[8:, :] = v_ref[:, 0, :, 0:width].reshape(extent, width)
    summed = cw_ref[CONV_WIDTH : CONV_WIDTH + 1, :]
    for tap in range(CONV_WIDTH):
        summed = summed + cw_ref[tap : tap + 1, :] * padded[5 + tap : 5 + tap + extent, :]
    return summed


def step_sizes(v_ref, hp_ref, conv_width, extent):
    raw = v_ref[:, 0, :, conv_width : conv_width + LANES].reshape(extent, LANES) + hp_ref[1:2, :]
    step = jnp.maximum(raw, 0.0) + jnp.log1p(jnp.exp(-jnp.abs(raw)))
    return raw, step


def enter_kernel(inner, v_ref, halo_ref, cw_ref, hp_ref, xs_ref, rw_ref, dl_ref, s_ref, padded):
    extent = xs_ref.shape[1]
    width = padded.shape[1]
    pre = conv_of(v_ref, halo_ref, cw_ref, padded)
    act = pre * jax.nn.sigmoid(pre)
    xs = act[:, :inner]
    write = act[:, inner : inner + STATE_DIM]
    unused_raw, step = step_sizes(v_ref, hp_ref, width, extent)
    log_sum = dot(lower_ones(extent), -step * jnp.exp(hp_ref[0:1, :]), NN, highest)
    tail = jnp.exp(log_sum[extent - 1 : extent, :] - log_sum) * step
    spread = dot_ones(tail, head_spread(inner), NN)
    xs_ref[0] = xs
    rw_ref[0] = act[:, inner:]
    dl_ref[0, :, 0:LANES] = step
    dl_ref[0, :, LANES:] = log_sum
    s_ref[0] = dot_split(split_parts(xs * spread), split_parts(write), TN)


def mixer_enter(v, halo, cw, hp, inner):
    zs, slots, rows, cols = v.shape
    extent = zs * rows
    width = cw.shape[1]
    heads = inner // HEAD_DIM
    return pl.pallas_call(
        functools.partial(enter_kernel, inner),
        grid=(slots,),
        in_specs=[
            pl.BlockSpec((zs, 1, rows, cols), lambda s: (0, s, 0, 0)),
            pl.BlockSpec((1, 8, width), lambda s: (s, 0, 0)),
            pl.BlockSpec(cw.shape, lambda s: (0, 0)),
            pl.BlockSpec(hp.shape, lambda s: (0, 0)),
        ],
        out_specs=[
            pl.BlockSpec((1, extent, inner), lambda s: (s, 0, 0)),
            pl.BlockSpec((1, extent, 2 * STATE_DIM), lambda s: (s, 0, 0)),
            pl.BlockSpec((1, extent, 2 * LANES), lambda s: (s, 0, 0)),
            pl.BlockSpec((1, inner, STATE_DIM), lambda s: (s, 0, 0)),
        ],
        out_shape=[
            jax.ShapeDtypeStruct((slots, extent, inner), f32),
            jax.ShapeDtypeStruct((slots, extent, 2 * STATE_DIM), f32),
            jax.ShapeDtypeStruct((slots, extent, 2 * LANES), f32),
            jax.ShapeDtypeStruct((slots, inner, STATE_DIM), f32),
        ],
        scratch_shapes=[pltpu.VMEM((extent + 8, width), f32)],
        compiler_params=kernel_params(48),
        cost_estimate=taking(12, zs * slots * rows),
        name="mixer_enter",
    )(v, halo, cw, hp)


def scan_kernel(reverse, got_ref, decay_ref, out_ref):
    count = got_ref.shape[0]
    state = jnp.zeros(got_ref.shape[1:], f32)
    order = range(count - 1, -1, -1) if reverse else range(count)
    for piece in order:
        out_ref[piece] = state
        state = decay_ref[piece] * state + got_ref[piece]


def scan_pieces(got, decay, reverse):
    return pl.pallas_call(
        functools.partial(scan_kernel, reverse),
        out_shape=jax.ShapeDtypeStruct(got.shape, f32),
        compiler_params=kernel_params(32),
        name="scan_pieces",
    )(got, decay)


def exchanged(rows):
    return lax.all_to_all(rows, "dp", 0, 0, tiled=False)


def states_forward(beside, s_local, log_last):
    count = lax.axis_size("dp")
    slots, inner, _ = s_local.shape
    share = slots * inner // count
    per_row = jnp.repeat(jnp.exp(log_last).reshape(-1), HEAD_DIM).reshape(count, share)
    lines = -(-share // (8 * LANES)) * 8
    per_row = jnp.pad(per_row, ((0, 0), (0, lines * LANES - share))).reshape(count, lines, LANES)
    got = exchanged(jnp.concatenate([s_local.reshape(count, share, STATE_DIM), per_row], axis=1))
    decay = got[:, share:].reshape(count, lines * LANES)[:, :share, None]
    entering = exchanged(after(scan_pieces(got[:, :share], decay, False), *beside))
    return entering.reshape(slots, inner, STATE_DIM), decay


def states_scanned(g_local, decay):
    count = lax.axis_size("dp")
    slots, inner, _ = g_local.shape
    got = exchanged(g_local.reshape(count, slots * inner // count, STATE_DIM))
    return scan_pieces(got, decay, True)


def inner_kernel(inner, xs_ref, rw_ref, dl_ref, y_ref):
    extent = xs_ref.shape[1]
    write = split_parts(rw_ref[0, :, :STATE_DIM])
    read = split_parts(rw_ref[0, :, STATE_DIM:])
    step_t = dl_ref[0, :, 0:LANES].T
    log_sum = dl_ref[0, :, LANES:]
    log_t = log_sum.T
    scores = dot_split(read, write, NT)
    causal = lax.broadcasted_iota(jnp.int32, (extent, extent), 0) >= lax.broadcasted_iota(
        jnp.int32, (extent, extent), 1
    )
    xs_low = xs_ref[0].astype(bf16)
    for head in range(inner // HEAD_DIM):
        cols = slice(head * HEAD_DIM, (head + 1) * HEAD_DIM)
        gap = log_sum[:, head : head + 1] - log_t[head : head + 1, :]
        mixing = jnp.exp(jnp.where(causal, gap, -jnp.inf)) * scores * step_t[head : head + 1, :]
        y_ref[0, :, cols] = dot(mixing.astype(bf16), xs_low[:, cols], NN)


def mixer_inner(xs, rw, dl):
    slots, extent, inner = xs.shape
    return pl.pallas_call(
        functools.partial(inner_kernel, inner),
        grid=(slots,),
        in_specs=[
            pl.BlockSpec((1, extent, inner), lambda s: (s, 0, 0)),
            pl.BlockSpec((1, extent, 2 * STATE_DIM), lambda s: (s, 0, 0)),
            pl.BlockSpec((1, extent, 2 * LANES), lambda s: (s, 0, 0)),
        ],
        out_specs=pl.BlockSpec((1, extent, inner), lambda s: (s, 0, 0)),
        out_shape=jax.ShapeDtypeStruct((slots, extent, inner), f32),
        compiler_params=kernel_params(40),
        cost_estimate=taking(9, slots * extent),
        name="mixer_inner",
    )(xs, rw, dl)


def leave_kernel(inner, yi_ref, xs_ref, rw_ref, dl_ref, h_ref, z_ref, hp_ref, gain_ref, y_ref, gg_ref, sq_ref):
    extent = xs_ref.shape[1]
    zs, _, rows, _ = z_ref.shape
    read = split_parts(rw_ref[0, :, STATE_DIM:])
    grown = dot_ones(jnp.exp(dl_ref[0, :, LANES:]), head_spread(inner), NN)
    y = yi_ref[0] + grown * dot_split(read, split_parts(h_ref[0]), NT) + hp_ref[3:4, :] * xs_ref[0]
    y_ref[0] = y
    z = z_ref[...].reshape(extent, inner)
    gated = y * (z * jax.nn.sigmoid(z))
    sq_ref[0] = jnp.broadcast_to(jnp.sum(gated * gated, axis=1, keepdims=True), (extent, LANES))
    gg_ref[...] = (gated * gain_ref[...]).astype(bf16).reshape(zs, 1, rows, inner)


def mixer_leave(yi, xs, rw, dl, h_in, z, skip, gain):
    zs, slots, rows, inner = z.shape
    extent = zs * rows
    return pl.pallas_call(
        functools.partial(leave_kernel, inner),
        grid=(slots,),
        in_specs=[
            pl.BlockSpec((1, extent, inner), lambda s: (s, 0, 0)),
            pl.BlockSpec((1, extent, inner), lambda s: (s, 0, 0)),
            pl.BlockSpec((1, extent, 2 * STATE_DIM), lambda s: (s, 0, 0)),
            pl.BlockSpec((1, extent, 2 * LANES), lambda s: (s, 0, 0)),
            pl.BlockSpec((1, inner, STATE_DIM), lambda s: (s, 0, 0)),
            pl.BlockSpec((zs, 1, rows, inner), lambda s: (0, s, 0, 0)),
            pl.BlockSpec(skip.shape, lambda s: (0, 0)),
            pl.BlockSpec(gain.shape, lambda s: (0, 0)),
        ],
        out_specs=[
            pl.BlockSpec((1, extent, inner), lambda s: (s, 0, 0)),
            pl.BlockSpec((zs, 1, rows, inner), lambda s: (0, s, 0, 0)),
            pl.BlockSpec((1, extent, LANES), lambda s: (s, 0, 0)),
        ],
        out_shape=[
            jax.ShapeDtypeStruct((slots, extent, inner), f32),
            jax.ShapeDtypeStruct((zs, slots, rows, inner), bf16),
            jax.ShapeDtypeStruct((slots, extent, LANES), f32),
        ],
        compiler_params=kernel_params(48),
        cost_estimate=taking(7, zs * slots * rows),
        name="mixer_leave",
    )(yi, xs, rw, dl, h_in, z, skip, gain)


def unmix_kernel(inner, gn_ref, y_ref, z_ref, rw_ref, dl_ref, tok_ref, gain_ref, gy_ref, gz_ref, s_ref, gg_ref):
    extent = y_ref.shape[1]
    zs, _, rows, _ = z_ref.shape
    grad = gn_ref[...].reshape(extent, inner)
    z = z_ref[...].reshape(extent, inner)
    logistic = jax.nn.sigmoid(z)
    gate = z * logistic
    y = y_ref[0]
    gated = y * gate
    inv_rms = tok_ref[0, :, 0:1]
    cross = tok_ref[0, :, 1:2]
    part = jnp.sum(grad * gated * inv_rms, axis=0, keepdims=True)

    @pl.when(pl.program_id(0) == 0)
    def _():
        gg_ref[...] = jnp.zeros_like(gg_ref)

    gg_ref[0:1, :] += part
    gated_grad = grad * gain_ref[...] * inv_rms - gated * cross
    gy = gated_grad * gate
    gy_ref[0] = gy
    gz = gated_grad * y * (logistic * (1.0 + z * (1.0 - logistic)))
    gz_ref[...] = gz.astype(bf16).reshape(zs, 1, rows, inner)
    grown = dot_ones(jnp.exp(dl_ref[0, :, LANES:]), head_spread(inner), NN)
    s_ref[0] = dot_split(split_parts(gy * grown), split_parts(rw_ref[0, :, STATE_DIM:]), TN)


def mixer_unmix(gn, y, z, rw, dl, tok, gain):
    zs, slots, rows, inner = z.shape
    extent = zs * rows
    return pl.pallas_call(
        functools.partial(unmix_kernel, inner),
        grid=(slots,),
        in_specs=[
            pl.BlockSpec((zs, 1, rows, inner), lambda s: (0, s, 0, 0)),
            pl.BlockSpec((1, extent, inner), lambda s: (s, 0, 0)),
            pl.BlockSpec((zs, 1, rows, inner), lambda s: (0, s, 0, 0)),
            pl.BlockSpec((1, extent, 2 * STATE_DIM), lambda s: (s, 0, 0)),
            pl.BlockSpec((1, extent, 2 * LANES), lambda s: (s, 0, 0)),
            pl.BlockSpec((1, extent, 2), lambda s: (s, 0, 0)),
            pl.BlockSpec(gain.shape, lambda s: (0, 0)),
        ],
        out_specs=[
            pl.BlockSpec((1, extent, inner), lambda s: (s, 0, 0)),
            pl.BlockSpec((zs, 1, rows, inner), lambda s: (0, s, 0, 0)),
            pl.BlockSpec((1, inner, STATE_DIM), lambda s: (s, 0, 0)),
            pl.BlockSpec((8, inner), lambda s: (0, 0)),
        ],
        out_shape=[
            jax.ShapeDtypeStruct((slots, extent, inner), f32),
            jax.ShapeDtypeStruct((zs, slots, rows, inner), bf16),
            jax.ShapeDtypeStruct((slots, inner, STATE_DIM), f32),
            jax.ShapeDtypeStruct((8, inner), f32),
        ],
        compiler_params=kernel_params(48),
        cost_estimate=taking(9, zs * slots * rows),
        name="mixer_unmix",
    )(gn, y, z, rw, dl, tok, gain)


def pairs_kernel(inner, xs_ref, rw_ref, dl_ref, gy_ref, gx_ref, grw_ref, gdl_ref, cols_buf):
    extent = gy_ref.shape[1]
    write = split_parts(rw_ref[0, :, :STATE_DIM])
    read = split_parts(rw_ref[0, :, STATE_DIM:])
    step = dl_ref[0, :, 0:LANES]
    log_sum = dl_ref[0, :, LANES:]
    log_t = log_sum.T
    gy_parts, xs_parts = split_parts(gy_ref[0]), split_parts(xs_ref[0])
    scores_t = dot_split(write, read, NT)
    later = lax.broadcasted_iota(jnp.int32, (extent, extent), 1) >= lax.broadcasted_iota(
        jnp.int32, (extent, extent), 0
    )
    lane = lax.broadcasted_iota(jnp.int32, (extent, LANES), 1)
    score_grad_t = jnp.zeros((extent, extent), f32)
    step_direct = jnp.zeros((extent, LANES), f32)
    cols_buf[...] = jnp.zeros_like(cols_buf)
    for head in range(inner // HEAD_DIM):
        cols = slice(head * HEAD_DIM, (head + 1) * HEAD_DIM)
        gap_t = log_t[head : head + 1, :] - log_sum[:, head : head + 1]
        decay_t = jnp.exp(jnp.where(later, gap_t, -jnp.inf))
        step_col = step[:, head : head + 1]
        pair_t = dot_split([x[:, cols] for x in xs_parts], [g[:, cols] for g in gy_parts], NT)
        both_t = decay_t * pair_t
        score_grad_t = score_grad_t + both_t * step_col
        weight_t = both_t * scores_t
        step_direct = step_direct + jnp.where(lane == head, jnp.sum(weight_t, axis=1, keepdims=True), 0.0)
        cols_buf[head : head + 1, :] = jnp.sum(weight_t * step_col, axis=0, keepdims=True)
        gx_ref[0, :, cols] = dot((decay_t * scores_t * step_col).astype(bf16), gy_parts[0][:, cols], NN)
    score_parts = split_parts(score_grad_t)
    grw_ref[0, :, :STATE_DIM] = dot_split(score_parts, read, NN)
    grw_ref[0, :, STATE_DIM:] = dot_split(score_parts, write, TN)
    gdl_ref[0, :, 0:LANES] = step_direct
    gdl_ref[0, :, LANES:] = cols_buf[...].T - step * step_direct


def mixer_pairs(xs, rw, dl, gy, *earlier):
    slots, extent, inner = xs.shape
    wide = pl.BlockSpec((1, extent, inner), lambda s: (s, 0, 0))
    two = pl.BlockSpec((1, extent, 2 * LANES), lambda s: (s, 0, 0))
    return pl.pallas_call(
        skipping(functools.partial(pairs_kernel, inner), 4, len(earlier)),
        grid=(slots,),
        in_specs=[wide, two, two, wide] + [ANYWHERE] * len(earlier),
        out_specs=[wide, two, two],
        out_shape=[
            jax.ShapeDtypeStruct((slots, extent, inner), f32),
            jax.ShapeDtypeStruct((slots, extent, 2 * STATE_DIM), f32),
            jax.ShapeDtypeStruct((slots, extent, 2 * LANES), f32),
        ],
        scratch_shapes=[pltpu.VMEM((LANES, extent), f32)],
        compiler_params=kernel_params(48),
        cost_estimate=taking(42, slots * extent),
        name="mixer_pairs",
    )(xs, rw, dl, gy, *earlier)


def back_kernel(
    inner, v_ref, halo_ref, cw_ref, hp_ref, skip_ref, rw_ref, dl_ref, gy_ref, gx_ref, grw_ref, gdl_ref, h_ref, gh_ref,
    gv_ref, gbc_ref, gp_ref, gc_ref, ghp_ref, padded, gpad,
):
    extent = gy_ref.shape[1]
    zs, _, rows, _ = v_ref.shape
    width = padded.shape[1]
    heads = inner // HEAD_DIM
    first = pl.program_id(0) == 0
    pre = conv_of(v_ref, halo_ref, cw_ref, padded)
    logistic = jax.nn.sigmoid(pre)
    slope = logistic * (1.0 + pre * (1.0 - logistic))
    xs = pre[:, :inner] * logistic[:, :inner]
    write_low = rw_ref[0, :, :STATE_DIM].astype(bf16)
    read_low = rw_ref[0, :, STATE_DIM:].astype(bf16)
    raw, step = step_sizes(v_ref, hp_ref, width, extent)
    rate = jnp.exp(hp_ref[0:1, :])
    log_sum = dl_ref[0, :, LANES:]
    gy = gy_ref[0]
    step_direct = gdl_ref[0, :, 0:LANES]
    sums = head_sums(inner)
    spread = head_spread(inner)
    last = log_sum[extent - 1 : extent, :]
    tail_decay = jnp.exp(last - log_sum)
    tail = dot_ones(tail_decay * step, spread, NN)
    grown = dot_ones(jnp.exp(log_sum), spread, NN)
    gh = gh_ref[0]
    h_in = h_ref[0]
    gh_parts, h_parts = split_parts(gh), split_parts(h_in)
    tail_in = dot(write_low, gh_parts[0], NT)
    tail_direct = tail_decay * dot_ones(xs * tail_in, sums, NN)
    tail_weight = tail_direct * step
    state_part = grown * dot(read_low, h_parts[0], NT)
    state_weight = dot_ones(gy * state_part, sums, NN)
    held = split_parts(gh * h_in)
    row_ones = jnp.ones((8, STATE_DIM), bf16)
    kept = dot_ones(dot(row_ones, held[0], NT) + dot(row_ones, held[1], NT), sums, NN)[0:1, :]
    log_grad = gdl_ref[0, :, LANES:] + state_weight - tail_weight
    end_grad = jnp.sum(tail_weight, axis=0, keepdims=True) + jnp.exp(last) * kept
    rate_arg_grad = dot(lower_ones(extent), log_grad, TN, highest) + end_grad
    step_grad = step_direct + tail_direct - rate * rate_arg_grad
    raw_grad = step_grad * jax.nn.sigmoid(raw)
    xs_grad = gx_ref[0] + tail * tail_in + skip_ref[3:4, :] * gy
    write_grad = grw_ref[0, :, :STATE_DIM] + dot_split(split_parts(tail * xs), gh_parts, NN)
    read_grad = grw_ref[0, :, STATE_DIM:] + dot_split(split_parts(grown * gy), h_parts, NN)
    valid_lane = lax.broadcasted_iota(jnp.int32, (1, LANES), 1) < heads
    rate_grad = jnp.where(valid_lane, jnp.sum(-step * rate * rate_arg_grad, axis=0, keepdims=True), 0.0)
    raw_grad = jnp.where(valid_lane, raw_grad, 0.0)
    skip_grad = jnp.sum(dot_ones(gy * xs, sums, NN), axis=0, keepdims=True)

    @pl.when(first)
    def _():
        gc_ref[...] = jnp.zeros_like(gc_ref)
        ghp_ref[...] = jnp.zeros_like(ghp_ref)

    ghp_ref[0:1, :] += rate_grad
    ghp_ref[1:2, :] += jnp.sum(raw_grad, axis=0, keepdims=True)
    ghp_ref[2:3, :] += skip_grad
    gpad[0:8, :] = jnp.zeros((8, width), f32)
    gpad[extent + 8 :, :] = jnp.zeros((8, width), f32)
    gpad[8 : extent + 8, 0:inner] = xs_grad * slope[:, 0:inner]
    gpad[8 : extent + 8, inner : inner + STATE_DIM] = write_grad * slope[:, inner : inner + STATE_DIM]
    gpad[8 : extent + 8, inner + STATE_DIM :] = read_grad * slope[:, inner + STATE_DIM :]
    back = jnp.zeros((extent, width), f32)
    before = jnp.zeros((8, width), f32)
    pre_grad = gpad[8 : extent + 8, :]
    for tap in range(CONV_WIDTH):
        ahead = CONV_WIDTH - 1 - tap
        weight = cw_ref[tap : tap + 1, :]
        back = back + weight * gpad[8 + ahead : 8 + ahead + extent, :]
        before = before + weight * gpad[ahead : 8 + ahead, :]
        gc_ref[tap : tap + 1, :] += jnp.sum(pre_grad * padded[5 + tap : 5 + tap + extent, :], axis=0, keepdims=True)
    gc_ref[CONV_WIDTH : CONV_WIDTH + 1, :] += jnp.sum(pre_grad, axis=0, keepdims=True)
    gp_ref[0] = before
    gv_ref[:, :, :, 0:inner] = back[:, :inner].astype(bf16).reshape(zs, 1, rows, inner)
    gbc_ref[...] = back[:, inner:].reshape(zs, 1, rows, width - inner)
    gv_ref[:, :, :, inner:] = raw_grad.astype(bf16).reshape(zs, 1, rows, LANES)


def mixer_back(v, halo, cw, hp, skip, rw, dl, gy, gx, grw, gdl, h_in, gh):
    zs, slots, rows, cols = v.shape
    extent = zs * rows
    inner = gy.shape[2]
    width = cw.shape[1]
    wide = pl.BlockSpec((1, extent, inner), lambda s: (s, 0, 0))
    two = pl.BlockSpec((1, extent, 2 * LANES), lambda s: (s, 0, 0))
    state = pl.BlockSpec((1, inner, STATE_DIM), lambda s: (s, 0, 0))
    return pl.pallas_call(
        functools.partial(back_kernel, inner),
        grid=(slots,),
        in_specs=[
            pl.BlockSpec((zs, 1, rows, cols), lambda s: (0, s, 0, 0)),
            pl.BlockSpec((1, 8, width), lambda s: (s, 0, 0)),
            pl.BlockSpec(cw.shape, lambda s: (0, 0)),
            pl.BlockSpec(hp.shape, lambda s: (0, 0)),
            pl.BlockSpec(skip.shape, lambda s: (0, 0)),
            two,
            two,
            wide,
            wide,
            two,
            two,
            state,
            state,
        ],
        out_specs=[
            pl.BlockSpec((zs, 1, rows, inner + LANES), lambda s: (0, s, 0, 0)),
            pl.BlockSpec((zs, 1, rows, 2 * STATE_DIM), lambda s: (0, s, 0, 0)),
            pl.BlockSpec((1, 8, width), lambda s: (s, 0, 0)),
            pl.BlockSpec((8, width), lambda s: (0, 0)),
            pl.BlockSpec((8, LANES), lambda s: (0, 0)),
        ],
        out_shape=[
            jax.ShapeDtypeStruct((zs, slots, rows, inner + LANES), bf16),
            jax.ShapeDtypeStruct((zs, slots, rows, 2 * STATE_DIM), f32),
            jax.ShapeDtypeStruct((slots, 8, width), f32),
            jax.ShapeDtypeStruct((8, width), f32),
            jax.ShapeDtypeStruct((8, LANES), f32),
        ],
        scratch_shapes=[
            pltpu.VMEM((extent + 8, width), f32),
            pltpu.VMEM((extent + 16, width), f32),
        ],
        compiler_params=kernel_params(56),
        cost_estimate=taking(18, zs * slots * rows),
        name="mixer_back",
    )(v, halo, cw, hp, skip, rw, dl, gy, gx, grw, gdl, h_in, gh)


def expert_kernel(
    n_ref, g_ref, mask_ref, router_ref, up_ref, down_ref,
    moe_ref, back_ref, logit_ref, act_ref, hid_ref, moe_sum, back_sum, gates_buf, gate_grad,
):
    pair = pl.program_id(0)
    pairs = pl.num_programs(0)
    tokens = n_ref.shape[0]
    lane = lax.broadcasted_iota(jnp.int32, (tokens, LANES), 1)
    half = up_ref.shape[3] // 2

    @pl.when(pair == 0)
    def _():
        logits = dot(n_ref[...], router_ref[...], NN)
        chosen = mask_ref[...] > 0.0
        logits = jnp.where(chosen, logits, -jnp.inf)
        powers = jnp.exp(logits - jnp.max(logits, axis=1, keepdims=True))
        gates = powers / jnp.sum(powers, axis=1, keepdims=True)
        gates_buf[...] = jnp.where(lane < EXPERTS, gates, 1.0)
        moe_sum[...] = jnp.zeros_like(moe_sum)
        back_sum[...] = jnp.zeros_like(back_sum)
        gate_grad[...] = jnp.zeros_like(gate_grad)

    depth = up_ref.shape[0] * up_ref.shape[2]
    down = down_ref[...].reshape(depth, 2 * half)
    n_val = n_ref[...]
    gates = gates_buf[...]
    act_back = dot(g_ref[...], down, NN)
    ups = [up_ref[:, member].reshape(depth, 2 * half) for member in range(2)]
    for member in range(2):
        hidden = dot(n_val, ups[member], NN)
        gate_part, up_part = hidden[:, :half], hidden[:, half:]
        logistic = jax.nn.sigmoid(gate_part)
        silu = gate_part * logistic
        act = (silu * up_part).astype(bf16).astype(f32)
        own = lane == 2 * pair + member
        gate = jnp.sum(jnp.where(own, gates, 0.0), axis=1, keepdims=True)
        part = act_back[:, member * half : (member + 1) * half]
        gate_grad[...] += jnp.where(own, jnp.sum(act * part, axis=1, keepdims=True), 0.0)
        act_ref[0, :, member * half : (member + 1) * half] = (gate * act).astype(bf16)
        part = part * gate
        first_col = 2 * member * half
        hid_ref[0, :, first_col : first_col + half] = (part * up_part * (logistic * (1.0 + gate_part * (1.0 - logistic)))).astype(bf16)
        hid_ref[0, :, first_col + half : first_col + 2 * half] = (part * silu).astype(bf16)
    moe_sum[...] += dot(act_ref[0], down, NT)
    back_sum[...] += dot(hid_ref[0], jnp.concatenate(ups, axis=1), NT)

    @pl.when(pair == pairs - 1)
    def _():
        gates_in = jnp.where(lane < EXPERTS, gates, 0.0)
        grads = gates_in * gate_grad[...]
        logit_grad = (grads - gates_in * jnp.sum(grads, axis=1, keepdims=True)).astype(bf16)
        logit_ref[...] = logit_grad
        back_ref[...] = (back_sum[...] + dot(logit_grad, router_ref[...], NT)).astype(bf16)
        moe_ref[...] = moe_sum[...].astype(bf16)


def experts(n_two, g_moe, mask, router, weights):
    tokens, width = n_two.shape
    count, blocks, rows, cols = weights.shape
    pairs = blocks // 3
    down_at = 2 * pairs
    return pl.pallas_call(
        expert_kernel,
        grid=(pairs,),
        in_specs=[
            pl.BlockSpec((tokens, width), lambda p: (0, 0)),
            pl.BlockSpec((tokens, width), lambda p: (0, 0)),
            pl.BlockSpec((tokens, LANES), lambda p: (0, 0)),
            pl.BlockSpec((width, LANES), lambda p: (0, 0)),
            pl.BlockSpec((count, 2, rows, cols), lambda p: (0, p, 0, 0)),
            pl.BlockSpec((count, 1, rows, cols), lambda p: (0, down_at + p, 0, 0)),
        ],
        out_specs=[
            pl.BlockSpec((tokens, width), lambda p: (0, 0)),
            pl.BlockSpec((tokens, width), lambda p: (0, 0)),
            pl.BlockSpec((tokens, LANES), lambda p: (0, 0)),
            pl.BlockSpec((1, tokens, cols), lambda p: (p, 0, 0)),
            pl.BlockSpec((1, tokens, 2 * cols), lambda p: (p, 0, 0)),
        ],
        out_shape=[
            jax.ShapeDtypeStruct((tokens, width), bf16),
            jax.ShapeDtypeStruct((tokens, width), bf16),
            jax.ShapeDtypeStruct((tokens, LANES), bf16),
            jax.ShapeDtypeStruct((pairs, tokens, cols), bf16),
            jax.ShapeDtypeStruct((pairs, tokens, 2 * cols), bf16),
        ],
        scratch_shapes=[
            pltpu.VMEM((tokens, width), f32),
            pltpu.VMEM((tokens, width), f32),
            pltpu.VMEM((tokens, LANES), f32),
            pltpu.VMEM((tokens, LANES), f32),
        ],
        compiler_params=kernel_params(60),
        cost_estimate=taking(72, tokens),
        name="experts",
    )(n_two, g_moe, mask, router, weights, weights)


def expert_grad_kernel(up_blocks, chunks, *refs):
    n_refs, g_refs, h_refs, a_refs = (refs[i * chunks : (i + 1) * chunks] for i in range(4))
    out_ref, turned = refs[4 * chunks :]
    block = pl.program_id(0)
    count, _, rows, cols = out_ref.shape
    tokens = n_refs[0].shape[0]

    def turn(sources):
        for at, source in enumerate(sources):
            turned[:, at * tokens : (at + 1) * tokens] = source[...].T

    def summed_over(rights):
        total = dot(turned[:, 0:tokens], rights[0][0], NN)
        for at in range(1, chunks):
            total = total + dot(turned[:, at * tokens : (at + 1) * tokens], rights[at][0], NN)
        out_ref[...] = total.astype(bf16).reshape(count, 1, rows, cols)

    @pl.when(block == 0)
    def _():
        turn(n_refs)

    @pl.when(block == up_blocks)
    def _():
        turn(g_refs)

    @pl.when(block < up_blocks)
    def _():
        summed_over(h_refs)

    @pl.when(block >= up_blocks)
    def _():
        summed_over(a_refs)


def expert_grads(n_list, g_list, hid_list, act_list, count, *earlier):
    chunks = len(n_list)
    tokens, width = n_list[0].shape
    cols = 2 * LANES
    hid_wide, act_wide = (values[0].shape[2] // cols for values in (hid_list, act_list))
    ups = hid_list[0].shape[0] * hid_wide
    downs = act_list[0].shape[0] * act_wide
    blocks = ups + downs
    whole = pl.BlockSpec((tokens, width), lambda b: (0, 0))

    def hid_at(b):
        b = jnp.minimum(b, ups - 1)
        return b // hid_wide, 0, b % hid_wide

    def act_at(b):
        b = jnp.maximum(b - ups, 0)
        return b // act_wide, 0, b % act_wide

    return pl.pallas_call(
        skipping(functools.partial(expert_grad_kernel, ups, chunks), 4 * chunks, len(earlier)),
        grid=(blocks,),
        in_specs=[whole] * (2 * chunks)
        + [pl.BlockSpec((1, tokens, cols), hid_at)] * chunks
        + [pl.BlockSpec((1, tokens, cols), act_at)] * chunks
        + [ANYWHERE] * len(earlier),
        out_specs=pl.BlockSpec((count, 1, width // count, cols), lambda b: (0, b, 0, 0)),
        out_shape=jax.ShapeDtypeStruct((count, blocks, width // count, cols), bf16),
        scratch_shapes=[pltpu.VMEM((width, chunks * tokens), bf16)],
        compiler_params=kernel_params(48),
        cost_estimate=taking(4 * blocks / 3, chunks * tokens),
        name="expert_grads",
    )(*n_list, *g_list, *hid_list, *act_list, *earlier)


def body(
    block_input,
    out_grad,
    lengths,
    routes,
    norm1_gain,
    w_zx,
    w_bc,
    w_dt,
    conv_x,
    conv_bc,
    head_params,
    gate_gain,
    w_out,
    norm2_gain,
    w_router,
    w_gu,
    w_dn,
    s_gu,
    s_dn,
):
    zs = lax.axis_size("tensor")
    pieces = lax.axis_size("dp")
    own = lax.axis_index("tensor")
    wide_index = lax.axis_index("dp")
    rows = block_input.shape[0]
    piece_rows = rows * zs
    heads = HEAD_COUNT // zs
    inner = INNER_DIM // zs
    width = inner + 2 * STATE_DIM
    shard = D_MODEL // pieces
    half = w_gu.shape[3]
    rim = CONV_WIDTH - 1
    per = SLOT_COUNT // CHUNKS
    tokens = per * rows
    chunk_ids = range(CHUNKS)

    enter_shard = jnp.concatenate(
        [w_zx[:, 1], w_bc, jnp.pad(w_dt, ((0, 0), (0, LANES - heads)))], axis=1
    )
    side_shard = jnp.concatenate(
        [w_zx[:, 0], w_out.T, jnp.pad(w_router, ((0, 0), (0, LANES - EXPERTS)))], axis=1
    )
    expert_shard = jnp.concatenate(
        [
            w_gu.reshape(EXPERTS, shard, 2 * half),
            s_gu.reshape(shard, 2, 2, half).transpose(2, 0, 1, 3).reshape(2, shard, 2 * half),
            w_dn.reshape(EXPERTS // 2, 2 * half, shard).transpose(0, 2, 1),
            s_dn.T[None],
        ],
        axis=0,
    )

    def by_slot(values):
        return jnp.transpose(values, (1, 0, 2))

    def part(values, c):
        return values[c * per : (c + 1) * per].reshape((tokens,) + values.shape[2:])

    u_slots = by_slot(block_input)
    u_low = [row_major(part(u_slots, c)) for c in chunk_ids]
    u_all = [in_order(line_gather(u_low[c])) for c in chunk_ids]
    full_enter = weight_gather(enter_shard).reshape(D_MODEL, width + LANES)
    gains = jnp.stack([norm1_gain, norm2_gain], axis=1).astype(f32)
    gains = lax.all_gather(gains, "dp", axis=0, tiled=True)
    gain_one, gain_two = gains[:, 0], gains[:, 1]
    full_side = weight_gather(side_shard).reshape(D_MODEL, 2 * inner + LANES)
    full_z, full_out, full_router = full_side[:, :inner], full_side[:, inner : 2 * inner], full_side[:, 2 * inner :]

    positions = wide_index * piece_rows + own * rows + jnp.arange(rows, dtype=jnp.int32)
    valid = (positions[None, :] < lengths[:, None]).astype(f32)[:, :, None]
    grad_slots = by_slot(out_grad).astype(f32) * valid

    conv_w = jnp.pad(jnp.concatenate([conv_x, conv_bc], axis=1), ((0, 8 - CONV_WIDTH - 1), (0, 0)))
    hp = jnp.pad(head_params, ((0, 5), (0, LANES - heads)))
    skip = jnp.pad(jnp.repeat(head_params[2], HEAD_DIM)[None], ((3, 4), (0, 0)))
    gain_row = gate_gain[None]

    hot = jnp.sum(
        (routes[..., None] == jnp.arange(LANES, dtype=jnp.int32)).astype(f32), axis=2
    )
    hot = jnp.transpose(hot.reshape(zs, rows, SLOT_COUNT, LANES), (0, 2, 1, 3))

    hot_at = by_distance(hot)

    def flat(values):
        return values.reshape((zs * tokens,) + values.shape[2:])

    def in_slots(values):
        return values.reshape((zs, per, rows) + values.shape[1:])

    u = [row_major(u_low[c].astype(f32)) for c in chunk_ids]
    valid_c = [part(valid, c) for c in chunk_ids]
    grad_c = [row_major(part(grad_slots, c)) for c in chunk_ids]
    n_one, v, z, halo, entered = [], [], [], [], []
    for c in chunk_ids:
        n_one.append(row_major(rms_scale(flat(u_all[c]).astype(f32), gain_one).astype(bf16)))
        v.append(in_slots(dot(n_one[c], full_enter, NN)))
        rim_rows = in_slots(n_one[c])[zs - 1, :, rows - rim :]
        prior = dot(passed_along(rim_rows, "dp", 1).reshape(per * rim, D_MODEL), full_enter[:, :width], NN)
        halo.append(jnp.pad(prior.reshape(per, rim, width), ((0, 0), (8 - rim, 0), (0, 0))))
    g_blocks = [line_gather(after(grad_c[c].astype(bf16), u_all[CHUNKS - 1])) for c in chunk_ids]
    for c in chunk_ids:
        entered.append(mixer_enter(v[c], halo[c], conv_w, hp, inner))
    resid, mixed_all, y_all, h_all, decay_all, inv_alls, gg_all, n_two = [], [], [], [], [], [], [], []
    for c in chunk_ids:
        xs, rw, dl, s_local = entered[c]
        yi = mixer_inner(xs, rw, dl)
        z.append(in_slots(dot(n_one[c], full_z, NN)))
        s_local = after(s_local, g_blocks[c][1], g_blocks[c][3])
        h_in, decay = states_forward((g_blocks[c][2], yi, z[c]), s_local, dl[:, piece_rows - 1, LANES : LANES + heads])
        if c == 0:
            full_expert = weight_gather(after(expert_shard, h_in))
        y, gg, squares = mixer_leave(yi, xs, rw, dl, h_in, z[c], skip, gain_row)
        product = dot(flat(gg.reshape(zs, tokens, inner)), full_out, NT).astype(bf16)
        product = product.reshape(zs, tokens, D_MODEL)
        square_sum = lax.psum(squares[:, :, 0], "tensor")
        inv_all = lax.rsqrt(square_sum / INNER_DIM + norm_eps)
        y_all.append(y)
        h_all.append(h_in)
        decay_all.append(decay)
        inv_alls.append(inv_all)
        gg_all.append(gg)

    few = tokens // HALVES
    halves = range(HALVES)

    def half_of(values, m):
        return values[m * few : (m + 1) * few]

    inv_own = lax.dynamic_slice_in_dim(inv_alls[0], own * rows, rows, 1).reshape(tokens, 1)
    mixed_own = summed(line_parts(by_distance(product))) * inv_own
    resid_own = row_major(u[0] + mixed_own)
    normed_two = row_major(rms_scale(resid_own, gain_two).astype(bf16))
    n_two_low, n_two, g_moe, masks = [], [], [], []
    for m in halves:
        low = half_of(normed_two, m)
        if m > 0:
            low = after(low, *n_two_low[m - 1][1:])
        n_two_low.append(line_gather(low))
        g_moe.append(jnp.concatenate([half_of(block, m) for block in g_blocks[0]], axis=0))
        masks.append(jnp.concatenate([half_of(part(hot_at(k), 0), m) for k in range(zs)], axis=0))
    moe_part, back_part, logit_grads, acts, hids = [], [], [], [], []
    for m in halves:
        if m > 0:
            n_two_low[m][1] = after(n_two_low[m][1], back_part[m - 1])
        n_two.append(jnp.concatenate(n_two_low[m], axis=0))
        results = experts(n_two[m], g_moe[m], masks[m], full_router, full_expert)
        moe_part.append(results[0].reshape(zs, few, D_MODEL))
        back_part.append(results[1].reshape(zs, few, D_MODEL))
        logit_grads.append(results[2])
        acts.append(results[3])
        hids.append(results[4])

    def norm_back(values, gain_vec, grads):
        return jax.vjp(rms_scale, values, gain_vec)[1](grads)

    back_blocks = []
    for m in halves:
        sent = back_part[m]
        if m > 0:
            sent = after(sent, *back_blocks[m - 1][1:])
        back_blocks.append(line_parts(lambda k: sent[k]))
    n_two_grad = jnp.concatenate([summed(blocks) for blocks in back_blocks], axis=0)
    from_norm, gain_two_grad = norm_back(resid_own, gain_two, n_two_grad)
    resid_grad = [row_major(grad_c[0] + from_norm)]
    low = resid_grad[0].astype(bf16)
    low_blocks = line_gather(low)
    gathered = in_order(low_blocks)
    expert_grad = weight_scatter(after(expert_grads(n_two, g_moe, hids, acts, pieces), gathered))
    g_mixed = [flat(gathered)]
    unmixed, scanned, pairs, toks, gate_gain_grad = [], [], [], [], 0.0
    for c in chunk_ids:
        grad = in_slots(dot(g_mixed[c], full_out, NN))
        xs, rw, dl, _ = entered[c]
        inv_all = inv_alls[c]
        y_like = jnp.transpose(y_all[c].reshape(per, zs, rows, inner), (1, 0, 2, 3))
        cross = jnp.sum(grad * gain_row * y_like * jax.nn.silu(z[c]), axis=-1)
        cross = lax.psum(jnp.transpose(cross, (1, 0, 2)).reshape(per, piece_rows), "tensor")
        tok = jnp.stack([inv_all, cross * (inv_all * inv_all * inv_all) / INNER_DIM], axis=-1)
        gy, gz, g_local, gg_grad = mixer_unmix(grad, y_all[c], z[c], rw, dl, tok, gain_row)
        toks.append(tok)
        gate_gain_grad = gate_gain_grad + gg_grad[0]
        unmixed.append((gy, gz))
        scanned.append(states_scanned(g_local, decay_all[c]))
        pairs.append(mixer_pairs(xs, rw, dl, gy))

    moe_blocks = []
    for m in halves:
        held = after(moe_part[m], *toks)
        moe_blocks.append(line_parts(lambda k: held[k]))
    sooner = [block for blocks in moe_blocks for block in blocks[1::2]]
    later = [block for blocks in moe_blocks for block in blocks[2::2]]
    router_grad = sum(dot(n_two[m], logit_grads[m], TN)[:, :EXPERTS] for m in halves)

    def rows_of(values):
        return jnp.concatenate([v.reshape(zs * tokens, -1) for v in values], axis=0)

    inv_rows = [
        jnp.transpose(inv_alls[c].reshape(per, zs, rows), (1, 0, 2)).reshape(zs * tokens, 1) for c in chunk_ids
    ]
    scaled = [(g_mixed[c].astype(f32) * inv_rows[c]).astype(bf16) for c in chunk_ids]
    n_rows = rows_of(n_one)
    gg_row, gz_row = (values.reshape(1, zs * tokens, inner) for values in (gg_all[0], unmixed[0][1]))
    side_products = expert_grads(scaled, [n_rows], [gg_row], [gz_row], pieces)

    v_grads, bc_grads, conv_grad, head_grad = [], [], 0.0, 0.0
    full_x = jnp.concatenate([full_enter[:, :inner], full_enter[:, width:]], axis=1)
    full_bc = full_enter[:, inner:width]
    full_bc = jnp.concatenate([full_bc, full_bc], axis=1)
    for c in chunk_ids:
        gy, gz = unmixed[c]
        xs, rw, dl, _ = entered[c]
        gh = exchanged(after(scanned[c], pairs[c][0], *sooner)).reshape(h_all[c].shape)
        gv, gbc, g_rim, gc, ghp = mixer_back(
            v[c], halo[c], conv_w, hp, skip, rw, dl, gy, *pairs[c], h_all[c], gh
        )
        conv_grad = conv_grad + gc
        head_grad = head_grad + ghp
        following = passed_along(g_rim[:, 8 - rim :].astype(bf16), "dp", -1).astype(f32)
        edge = gv[zs - 1, :, rows - rim :, :inner].astype(f32) + following[:, :, :inner]
        gv = lax.dynamic_update_slice(gv, edge.astype(bf16)[None], (zs - 1, 0, rows - rim, 0))
        edge = gbc[zs - 1, :, rows - rim :] + following[:, :, inner:]
        gbc = lax.dynamic_update_slice(gbc, edge[None], (zs - 1, 0, rows - rim, 0))
        v_grads.append(gv)
        bc_grads.append(after(jnp.concatenate(split_parts(gbc), axis=-1), *later))
    n_parts, arrived, gain_one_grad = [], [], 0.0
    for c in chunk_ids:
        n_grad = (
            dot(unmixed[c][1].reshape(zs * tokens, inner), full_z, NT)
            + dot(v_grads[c].reshape(zs * tokens, inner + LANES), full_x, NT)
            + dot(bc_grads[c].reshape(zs * tokens, 4 * STATE_DIM), full_bc, NT)
        )
        every = flat(u_all[c]).astype(f32)
        scale = lax.rsqrt(jnp.mean(every * every, axis=-1, keepdims=True) + norm_eps)
        gain_one_grad = gain_one_grad + jnp.sum(n_grad * (every * scale), axis=0)
        n_parts.append(n_grad.astype(bf16))
        received = line_parts(by_distance(n_parts[c].reshape(zs, tokens, D_MODEL)))
        arrived.append(received)
    for blocks in moe_blocks:
        blocks[1] = after(blocks[1], n_parts[0])
    moe = [summed(blocks) for blocks in moe_blocks]
    moe_own = jnp.concatenate(moe, axis=0)
    output = [resid_own + moe_own]
    stat_terms = jnp.stack(
        [
            jnp.sum(valid_c[0] * output[0] * output[0]),
            jnp.sum(valid_c[0] * mixed_own * mixed_own),
            jnp.sum(valid_c[0] * moe_own * moe_own),
        ]
    )
    enter_w_grad = dot(n_rows, rows_of(v_grads), TN).astype(bf16)
    bc_w_grad = dot(n_rows, rows_of(bc_grads), TN)
    bc_w_grad = bc_w_grad[:, : 2 * STATE_DIM] + bc_w_grad[:, 2 * STATE_DIM :]
    side_grad = weight_scatter(after(side_products, expert_grad, *n_parts))

    def mixer_scatter(grads):
        return weight_scatter(after(grads.reshape(pieces, shard, -1), side_grad)).astype(f32)

    side = side_grad.astype(f32)
    fold = side.shape[0] // 2
    z_part = jnp.transpose(side[fold:], (1, 0, 2)).reshape(shard, inner)
    out_part = jnp.transpose(side[:fold], (0, 2, 1)).reshape(inner, shard)
    enter_part = mixer_scatter(enter_w_grad)
    expert_grad = expert_grad.astype(f32)
    ups, downs = EXPERTS + 2, EXPERTS // 2
    expert_outs = (
        expert_grad[:EXPERTS].reshape(EXPERTS, shard, 2, half),
        expert_grad[ups : ups + downs].transpose(0, 2, 1).reshape(EXPERTS, half, shard),
        expert_grad[EXPERTS:ups].reshape(2, shard, 2, half).transpose(1, 2, 0, 3).reshape(shard, 2, 2 * half),
        expert_grad[ups + downs].T,
    )

    def to_shares(values, dim):
        size = values.shape[dim] // (pieces * zs)
        values = jnp.moveaxis(values, dim, 0).reshape(pieces, zs, size, -1)
        return jnp.moveaxis(values, 3, 2).reshape(pieces, zs, -1)

    column = own * inner
    conv_x_full = lax.dynamic_update_slice(
        jnp.zeros((CONV_WIDTH + 1, INNER_DIM), f32), conv_grad[: CONV_WIDTH + 1, :inner], (jnp.int32(0), column)
    )
    gate_full = lax.dynamic_update_slice(jnp.zeros((INNER_DIM,), f32), gate_gain_grad, (column,))
    small = [
        (gain_one_grad, 0),
        (conv_x_full, 1),
        (conv_grad[: CONV_WIDTH + 1, inner:], 1),
        (gate_full, 0),
        (gain_two_grad, 0),
        (router_grad, 0),
    ]
    shares = [to_shares(values, dim) for values, dim in small]
    sizes = [share.shape[2] for share in shares]
    shares = jnp.concatenate(shares, axis=2)
    length = shares.shape[2]
    shares = jnp.pad(shares, ((0, 0), (0, 0), (0, -length % (8 * LANES))))
    wide_share = bc_w_grad.reshape(pieces, zs, -1, LANES)
    tile = jnp.zeros((8, LANES), f32)
    tile = tile.at[:3, :heads].set(head_grad[:3, :heads]).at[3, :3].set(stat_terms)
    tile = jnp.broadcast_to(tile, (pieces, zs) + tile.shape)
    shares = jnp.concatenate([wide_share, shares.reshape(pieces, zs, -1, LANES), tile], axis=2)
    shares = after(shares, arrived[0][1], arrived[0][2], *expert_outs)
    shares = jnp.sum(lax.all_to_all(shares, "dp", 0, 0), axis=0)
    first_sum = after(shares, arrived[0][3])
    shares = first_sum
    got = lax.all_to_all(shares, "tensor", 0, 0)
    tiles = got[:, -8:]
    shares = jnp.sum(got[:, :-8], axis=0)
    u_grad = []
    for c in chunk_ids:
        received = arrived[c]
        u_grad.append(resid_grad[c] + norm_back(u[c], gain_one, summed(received))[0])
    bc_lines = wide_share.shape[2]
    bc_grad = shares[:bc_lines].reshape(-1, 2 * STATE_DIM)
    shares = shares[bc_lines:].reshape(-1)
    ends = [sum(sizes[: k + 1]) for k in range(len(sizes))]
    took = []
    for (values, dim), size, end in zip(small, sizes, ends):
        share = shares[end - size : end]
        if values.ndim == 2:
            other = values.shape[1 - dim]
            share = share.reshape(other, size // other)
            share = share if dim == 1 else share.T
        took.append(share)
    head_sum = jnp.transpose(tiles[:, :3, :heads], (1, 0, 2)).reshape(3, HEAD_COUNT)
    stat_sum = jnp.sum(tiles[:, 3, :3], axis=0)
    stats = jnp.sqrt(stat_sum / (jnp.sum(lengths).astype(f32) * D_MODEL))

    def placed_back(values):
        whole = jnp.concatenate([value.astype(bf16).reshape(per, rows, D_MODEL) for value in values], axis=0)
        return jnp.transpose(whole, (1, 0, 2))

    return (
        placed_back(output),
        placed_back(u_grad),
        took[0],
        jnp.stack([z_part, enter_part[:, :inner]], axis=1),
        bc_grad,
        enter_part[:, inner : inner + heads],
        took[1],
        took[2],
        head_sum,
        took[3],
        out_part,
        took[4],
        took[5],
        *expert_outs,
        stats,
    )


def solution(mesh):
    both = ("dp", "tensor")
    placed = (
        P(both, None, None),
        P(both, None, None),
        P(),
        P("dp", None, None),
        P("dp"),
        P("dp", None, "tensor"),
        P("dp", None),
        P("dp", "tensor"),
        P(None, "tensor"),
        P(),
        P(None, "tensor"),
        P("tensor"),
        P("tensor", "dp"),
        P("dp"),
        P("dp", None),
        P(None, "dp", None, "tensor"),
        P(None, "tensor", "dp"),
        P("dp", None, "tensor"),
        P("tensor", "dp"),
    )
    return jax.shard_map(
        body,
        mesh=mesh,
        in_specs=placed,
        out_specs=(
            P(both, None, None),
            P(both, None, None),
            P(both),
            P("dp", None, "tensor"),
            P(both, None),
            P("dp", "tensor"),
            P(None, both),
            P(None, both),
            P(),
            P(both),
            P("tensor", "dp"),
            P(both),
            P(both, None),
            P(None, "dp", None, "tensor"),
            P(None, "tensor", "dp"),
            P("dp", None, "tensor"),
            P("tensor", "dp"),
            P(),
        ),
        check_vma=False,
    )
```

```python
import functools

import jax
import jax.numpy as jnp
from jax import lax
from jax.experimental import pallas as pl
from jax.experimental.layout import Layout, with_layout_constraint
from jax.experimental.pallas import tpu as pltpu
from jax.sharding import PartitionSpec as P

D_MODEL = 1536
HEAD_COUNT = 48
HEAD_DIM = 64
STATE_DIM = 128
CONV_WIDTH = 4
TOP_K = 6
EXPERTS = 16
SLOT_COUNT = 4
INNER_DIM = 3072
LANES = 128
CHUNKS = 1
HALVES = 2

norm_eps = 1e-05
highest = lax.Precision.HIGHEST
f32 = jnp.float32
bf16 = jnp.bfloat16


def passed_along(value, axis, steps):
    count = lax.axis_size(axis)
    first, last = (max(0, -steps), min(count, count - steps))
    return lax.ppermute(value, axis, [(source, source + steps) for source in range(first, last)])


def row_major(value):
    return with_layout_constraint(value, Layout(major_to_minor=tuple(range(value.ndim))))


def line_gather(value):
    size = lax.axis_size("tensor")
    return [value] + [
        row_major(lax.ppermute(row_major(value), "tensor", [(a, (a - step) % size) for a in range(size)]))
        for step in range(1, size)
    ]


def line_parts(block_of):
    size = lax.axis_size("tensor")
    return [block_of(0)] + [
        lax.ppermute(row_major(block_of(step)), "tensor", [(a, (a + step) % size) for a in range(size)])
        for step in range(1, size)
    ]


def summed(parts):
    total = parts[0].astype(f32)
    for part in parts[1:]:
        total = total + part.astype(f32)
    return row_major(total)


def in_order(blocks):
    size = len(blocks)
    own = lax.axis_index("tensor")
    whole = jnp.zeros((size,) + blocks[0].shape, blocks[0].dtype)
    for k in range(size):
        whole = lax.dynamic_update_index_in_dim(whole, blocks[k], (own + k) % size, 0)
    return whole


def by_distance(whole):
    size = whole.shape[0]
    own = lax.axis_index("tensor")
    return lambda k: lax.dynamic_index_in_dim(whole, (own + k) % size, 0, False)


def weight_gather(shard):
    return lax.all_gather(shard, "dp", axis=0, tiled=False)


def weight_scatter(grads):
    return row_major(lax.psum_scatter(grads.astype(bf16), "dp", scatter_dimension=0, tiled=False))


def rms_scale(values, gain_vec):
    return (
        values * lax.rsqrt(jnp.mean(values * values, axis=-1, keepdims=True) + norm_eps) * gain_vec
    )


def silu_slope(values):
    logistic = jax.nn.sigmoid(values)
    return logistic * (1.0 + values * (1.0 - logistic))


def dot(a, b, dims, precision=None):
    return lax.dot_general(a, b, (dims, ((), ())), precision=precision, preferred_element_type=f32)


def split_parts(values):
    upper = values.astype(bf16)
    return upper, (values - upper.astype(f32)).astype(bf16)


def dot_split(a, b, dims):
    return dot(a[0], b[0], dims) + (dot(a[0], b[1], dims) + dot(a[1], b[0], dims))


def dot_ones(values, ones, dims):
    upper, lower = split_parts(values)
    return dot(upper, ones, dims) + dot(lower, ones, dims)


def after(value, *others):
    anywhere = pl.BlockSpec(memory_space=pl.ANY)
    return pl.pallas_call(
        lambda *refs: None,
        in_specs=[anywhere] * (1 + len(others)),
        out_specs=anywhere,
        out_shape=jax.ShapeDtypeStruct(value.shape, value.dtype),
        input_output_aliases={0: 0},
        name="after",
    )(value, *others)


def skipping(kernel, first, count):
    return lambda *refs: kernel(*refs[:first], *refs[first + count :])


ANYWHERE = pl.BlockSpec(memory_space=pl.ANY)
NN = ((1,), (0,))
NT = ((1,), (1,))
TN = ((0,), (0,))


def head_spread(inner):
    row = lax.broadcasted_iota(jnp.int32, (LANES, inner), 0)
    col = lax.broadcasted_iota(jnp.int32, (LANES, inner), 1)
    return (col // HEAD_DIM == row).astype(bf16)


def head_sums(inner):
    row = lax.broadcasted_iota(jnp.int32, (inner, LANES), 0)
    col = lax.broadcasted_iota(jnp.int32, (inner, LANES), 1)
    return (row // HEAD_DIM == col).astype(bf16)


def lower_ones(extent):
    row = lax.broadcasted_iota(jnp.int32, (extent, extent), 0)
    col = lax.broadcasted_iota(jnp.int32, (extent, extent), 1)
    return (row >= col).astype(f32)


def kernel_params(mib):
    return pltpu.CompilerParams(vmem_limit_bytes=mib * 1024 * 1024)


def taking(micros, tokens):
    return pl.CostEstimate(flops=int(micros * tokens * 1.1e6), bytes_accessed=1024, transcendentals=0)


def conv_of(v_ref, halo_ref, cw_ref, padded):
    extent = padded.shape[0] - 8
    width = padded.shape[1]
    padded[0:8, :] = halo_ref[0]
    padded[8:, :] = v_ref[:, 0, :, 0:width].reshape(extent, width)
    summed = cw_ref[CONV_WIDTH : CONV_WIDTH + 1, :]
    for tap in range(CONV_WIDTH):
        summed = summed + cw_ref[tap : tap + 1, :] * padded[5 + tap : 5 + tap + extent, :]
    return summed


def step_sizes(v_ref, hp_ref, conv_width, extent):
    raw = v_ref[:, 0, :, conv_width : conv_width + LANES].reshape(extent, LANES) + hp_ref[1:2, :]
    step = jnp.maximum(raw, 0.0) + jnp.log1p(jnp.exp(-jnp.abs(raw)))
    return raw, step


def enter_kernel(inner, v_ref, halo_ref, cw_ref, hp_ref, xs_ref, rw_ref, dl_ref, s_ref, padded):
    extent = xs_ref.shape[1]
    width = padded.shape[1]
    pre = conv_of(v_ref, halo_ref, cw_ref, padded)
    act = pre * jax.nn.sigmoid(pre)
    xs = act[:, :inner]
    write = act[:, inner : inner + STATE_DIM]
    unused_raw, step = step_sizes(v_ref, hp_ref, width, extent)
    log_sum = dot(lower_ones(extent), -step * jnp.exp(hp_ref[0:1, :]), NN, highest)
    tail = jnp.exp(log_sum[extent - 1 : extent, :] - log_sum) * step
    spread = dot_ones(tail, head_spread(inner), NN)
    xs_ref[0] = xs
    rw_ref[0] = act[:, inner:]
    dl_ref[0, :, 0:LANES] = step
    dl_ref[0, :, LANES:] = log_sum
    s_ref[0] = dot_split(split_parts(xs * spread), split_parts(write), TN)


def mixer_enter(v, halo, cw, hp, inner):
    zs, slots, rows, cols = v.shape
    extent = zs * rows
    width = cw.shape[1]
    heads = inner // HEAD_DIM
    return pl.pallas_call(
        functools.partial(enter_kernel, inner),
        grid=(slots,),
        in_specs=[
            pl.BlockSpec((zs, 1, rows, cols), lambda s: (0, s, 0, 0)),
            pl.BlockSpec((1, 8, width), lambda s: (s, 0, 0)),
            pl.BlockSpec(cw.shape, lambda s: (0, 0)),
            pl.BlockSpec(hp.shape, lambda s: (0, 0)),
        ],
        out_specs=[
            pl.BlockSpec((1, extent, inner), lambda s: (s, 0, 0)),
            pl.BlockSpec((1, extent, 2 * STATE_DIM), lambda s: (s, 0, 0)),
            pl.BlockSpec((1, extent, 2 * LANES), lambda s: (s, 0, 0)),
            pl.BlockSpec((1, inner, STATE_DIM), lambda s: (s, 0, 0)),
        ],
        out_shape=[
            jax.ShapeDtypeStruct((slots, extent, inner), f32),
            jax.ShapeDtypeStruct((slots, extent, 2 * STATE_DIM), f32),
            jax.ShapeDtypeStruct((slots, extent, 2 * LANES), f32),
            jax.ShapeDtypeStruct((slots, inner, STATE_DIM), f32),
        ],
        scratch_shapes=[pltpu.VMEM((extent + 8, width), f32)],
        compiler_params=kernel_params(48),
        cost_estimate=taking(12, zs * slots * rows),
        name="mixer_enter",
    )(v, halo, cw, hp)


def scan_kernel(reverse, got_ref, decay_ref, out_ref):
    count = got_ref.shape[0]
    state = jnp.zeros(got_ref.shape[1:], f32)
    order = range(count - 1, -1, -1) if reverse else range(count)
    for piece in order:
        out_ref[piece] = state
        state = decay_ref[piece] * state + got_ref[piece]


def scan_pieces(got, decay, reverse):
    return pl.pallas_call(
        functools.partial(scan_kernel, reverse),
        out_shape=jax.ShapeDtypeStruct(got.shape, f32),
        compiler_params=kernel_params(32),
        name="scan_pieces",
    )(got, decay)


def exchanged(rows):
    return lax.all_to_all(rows, "dp", 0, 0, tiled=False)


def states_forward(beside, s_local, log_last):
    count = lax.axis_size("dp")
    slots, inner, _ = s_local.shape
    share = slots * inner // count
    per_row = jnp.repeat(jnp.exp(log_last).reshape(-1), HEAD_DIM).reshape(count, share)
    lines = -(-share // (8 * LANES)) * 8
    per_row = jnp.pad(per_row, ((0, 0), (0, lines * LANES - share))).reshape(count, lines, LANES)
    got = exchanged(jnp.concatenate([s_local.reshape(count, share, STATE_DIM), per_row], axis=1))
    decay = got[:, share:].reshape(count, lines * LANES)[:, :share, None]
    entering = exchanged(after(scan_pieces(got[:, :share], decay, False), *beside))
    return entering.reshape(slots, inner, STATE_DIM), decay


def states_scanned(g_local, decay):
    count = lax.axis_size("dp")
    slots, inner, _ = g_local.shape
    got = exchanged(g_local.reshape(count, slots * inner // count, STATE_DIM))
    return scan_pieces(got, decay, True)


def inner_kernel(inner, xs_ref, rw_ref, dl_ref, y_ref):
    extent = xs_ref.shape[1]
    write = split_parts(rw_ref[0, :, :STATE_DIM])
    read = split_parts(rw_ref[0, :, STATE_DIM:])
    step_t = dl_ref[0, :, 0:LANES].T
    log_sum = dl_ref[0, :, LANES:]
    log_t = log_sum.T
    scores = dot_split(read, write, NT)
    causal = lax.broadcasted_iota(jnp.int32, (extent, extent), 0) >= lax.broadcasted_iota(
        jnp.int32, (extent, extent), 1
    )
    xs_low = xs_ref[0].astype(bf16)
    for head in range(inner // HEAD_DIM):
        cols = slice(head * HEAD_DIM, (head + 1) * HEAD_DIM)
        gap = log_sum[:, head : head + 1] - log_t[head : head + 1, :]
        mixing = jnp.exp(jnp.where(causal, gap, -jnp.inf)) * scores * step_t[head : head + 1, :]
        y_ref[0, :, cols] = dot(mixing.astype(bf16), xs_low[:, cols], NN)


def mixer_inner(xs, rw, dl):
    slots, extent, inner = xs.shape
    return pl.pallas_call(
        functools.partial(inner_kernel, inner),
        grid=(slots,),
        in_specs=[
            pl.BlockSpec((1, extent, inner), lambda s: (s, 0, 0)),
            pl.BlockSpec((1, extent, 2 * STATE_DIM), lambda s: (s, 0, 0)),
            pl.BlockSpec((1, extent, 2 * LANES), lambda s: (s, 0, 0)),
        ],
        out_specs=pl.BlockSpec((1, extent, inner), lambda s: (s, 0, 0)),
        out_shape=jax.ShapeDtypeStruct((slots, extent, inner), f32),
        compiler_params=kernel_params(40),
        cost_estimate=taking(9, slots * extent),
        name="mixer_inner",
    )(xs, rw, dl)


def leave_kernel(inner, yi_ref, xs_ref, rw_ref, dl_ref, h_ref, z_ref, hp_ref, gain_ref, y_ref, gg_ref, sq_ref):
    extent = xs_ref.shape[1]
    zs, _, rows, _ = z_ref.shape
    read = split_parts(rw_ref[0, :, STATE_DIM:])
    grown = dot_ones(jnp.exp(dl_ref[0, :, LANES:]), head_spread(inner), NN)
    y = yi_ref[0] + grown * dot_split(read, split_parts(h_ref[0]), NT) + hp_ref[3:4, :] * xs_ref[0]
    y_ref[0] = y
    z = z_ref[...].reshape(extent, inner)
    gated = y * (z * jax.nn.sigmoid(z))
    sq_ref[0] = jnp.broadcast_to(jnp.sum(gated * gated, axis=1, keepdims=True), (extent, LANES))
    gg_ref[...] = (gated * gain_ref[...]).astype(bf16).reshape(zs, 1, rows, inner)


def mixer_leave(yi, xs, rw, dl, h_in, z, skip, gain):
    zs, slots, rows, inner = z.shape
    extent = zs * rows
    return pl.pallas_call(
        functools.partial(leave_kernel, inner),
        grid=(slots,),
        in_specs=[
            pl.BlockSpec((1, extent, inner), lambda s: (s, 0, 0)),
            pl.BlockSpec((1, extent, inner), lambda s: (s, 0, 0)),
            pl.BlockSpec((1, extent, 2 * STATE_DIM), lambda s: (s, 0, 0)),
            pl.BlockSpec((1, extent, 2 * LANES), lambda s: (s, 0, 0)),
            pl.BlockSpec((1, inner, STATE_DIM), lambda s: (s, 0, 0)),
            pl.BlockSpec((zs, 1, rows, inner), lambda s: (0, s, 0, 0)),
            pl.BlockSpec(skip.shape, lambda s: (0, 0)),
            pl.BlockSpec(gain.shape, lambda s: (0, 0)),
        ],
        out_specs=[
            pl.BlockSpec((1, extent, inner), lambda s: (s, 0, 0)),
            pl.BlockSpec((zs, 1, rows, inner), lambda s: (0, s, 0, 0)),
            pl.BlockSpec((1, extent, LANES), lambda s: (s, 0, 0)),
        ],
        out_shape=[
            jax.ShapeDtypeStruct((slots, extent, inner), f32),
            jax.ShapeDtypeStruct((zs, slots, rows, inner), bf16),
            jax.ShapeDtypeStruct((slots, extent, LANES), f32),
        ],
        compiler_params=kernel_params(48),
        cost_estimate=taking(7, zs * slots * rows),
        name="mixer_leave",
    )(yi, xs, rw, dl, h_in, z, skip, gain)


def unmix_kernel(inner, gn_ref, y_ref, z_ref, rw_ref, dl_ref, tok_ref, gain_ref, gy_ref, gz_ref, s_ref, gg_ref):
    extent = y_ref.shape[1]
    zs, _, rows, _ = z_ref.shape
    grad = gn_ref[...].reshape(extent, inner)
    z = z_ref[...].reshape(extent, inner)
    logistic = jax.nn.sigmoid(z)
    gate = z * logistic
    y = y_ref[0]
    gated = y * gate
    inv_rms = tok_ref[0, :, 0:1]
    cross = tok_ref[0, :, 1:2]
    part = jnp.sum(grad * gated * inv_rms, axis=0, keepdims=True)

    @pl.when(pl.program_id(0) == 0)
    def _():
        gg_ref[...] = jnp.zeros_like(gg_ref)

    gg_ref[0:1, :] += part
    gated_grad = grad * gain_ref[...] * inv_rms - gated * cross
    gy = gated_grad * gate
    gy_ref[0] = gy
    gz = gated_grad * y * (logistic * (1.0 + z * (1.0 - logistic)))
    gz_ref[...] = gz.astype(bf16).reshape(zs, 1, rows, inner)
    grown = dot_ones(jnp.exp(dl_ref[0, :, LANES:]), head_spread(inner), NN)
    s_ref[0] = dot_split(split_parts(gy * grown), split_parts(rw_ref[0, :, STATE_DIM:]), TN)


def mixer_unmix(gn, y, z, rw, dl, tok, gain):
    zs, slots, rows, inner = z.shape
    extent = zs * rows
    return pl.pallas_call(
        functools.partial(unmix_kernel, inner),
        grid=(slots,),
        in_specs=[
            pl.BlockSpec((zs, 1, rows, inner), lambda s: (0, s, 0, 0)),
            pl.BlockSpec((1, extent, inner), lambda s: (s, 0, 0)),
            pl.BlockSpec((zs, 1, rows, inner), lambda s: (0, s, 0, 0)),
            pl.BlockSpec((1, extent, 2 * STATE_DIM), lambda s: (s, 0, 0)),
            pl.BlockSpec((1, extent, 2 * LANES), lambda s: (s, 0, 0)),
            pl.BlockSpec((1, extent, 2), lambda s: (s, 0, 0)),
            pl.BlockSpec(gain.shape, lambda s: (0, 0)),
        ],
        out_specs=[
            pl.BlockSpec((1, extent, inner), lambda s: (s, 0, 0)),
            pl.BlockSpec((zs, 1, rows, inner), lambda s: (0, s, 0, 0)),
            pl.BlockSpec((1, inner, STATE_DIM), lambda s: (s, 0, 0)),
            pl.BlockSpec((8, inner), lambda s: (0, 0)),
        ],
        out_shape=[
            jax.ShapeDtypeStruct((slots, extent, inner), f32),
            jax.ShapeDtypeStruct((zs, slots, rows, inner), bf16),
            jax.ShapeDtypeStruct((slots, inner, STATE_DIM), f32),
            jax.ShapeDtypeStruct((8, inner), f32),
        ],
        compiler_params=kernel_params(48),
        cost_estimate=taking(9, zs * slots * rows),
        name="mixer_unmix",
    )(gn, y, z, rw, dl, tok, gain)


def pairs_kernel(inner, xs_ref, rw_ref, dl_ref, gy_ref, gx_ref, grw_ref, gdl_ref, cols_buf):
    extent = gy_ref.shape[1]
    write = split_parts(rw_ref[0, :, :STATE_DIM])
    read = split_parts(rw_ref[0, :, STATE_DIM:])
    step = dl_ref[0, :, 0:LANES]
    log_sum = dl_ref[0, :, LANES:]
    log_t = log_sum.T
    gy_parts, xs_parts = split_parts(gy_ref[0]), split_parts(xs_ref[0])
    scores_t = dot_split(write, read, NT)
    later = lax.broadcasted_iota(jnp.int32, (extent, extent), 1) >= lax.broadcasted_iota(
        jnp.int32, (extent, extent), 0
    )
    lane = lax.broadcasted_iota(jnp.int32, (extent, LANES), 1)
    score_grad_t = jnp.zeros((extent, extent), f32)
    step_direct = jnp.zeros((extent, LANES), f32)
    cols_buf[...] = jnp.zeros_like(cols_buf)
    for head in range(inner // HEAD_DIM):
        cols = slice(head * HEAD_DIM, (head + 1) * HEAD_DIM)
        gap_t = log_t[head : head + 1, :] - log_sum[:, head : head + 1]
        decay_t = jnp.exp(jnp.where(later, gap_t, -jnp.inf))
        step_col = step[:, head : head + 1]
        pair_t = dot_split([x[:, cols] for x in xs_parts], [g[:, cols] for g in gy_parts], NT)
        both_t = decay_t * pair_t
        score_grad_t = score_grad_t + both_t * step_col
        weight_t = both_t * scores_t
        step_direct = step_direct + jnp.where(lane == head, jnp.sum(weight_t, axis=1, keepdims=True), 0.0)
        cols_buf[head : head + 1, :] = jnp.sum(weight_t * step_col, axis=0, keepdims=True)
        gx_ref[0, :, cols] = dot((decay_t * scores_t * step_col).astype(bf16), gy_parts[0][:, cols], NN)
    score_parts = split_parts(score_grad_t)
    grw_ref[0, :, :STATE_DIM] = dot_split(score_parts, read, NN)
    grw_ref[0, :, STATE_DIM:] = dot_split(score_parts, write, TN)
    gdl_ref[0, :, 0:LANES] = step_direct
    gdl_ref[0, :, LANES:] = cols_buf[...].T - step * step_direct


def mixer_pairs(xs, rw, dl, gy, *earlier):
    slots, extent, inner = xs.shape
    wide = pl.BlockSpec((1, extent, inner), lambda s: (s, 0, 0))
    two = pl.BlockSpec((1, extent, 2 * LANES), lambda s: (s, 0, 0))
    return pl.pallas_call(
        skipping(functools.partial(pairs_kernel, inner), 4, len(earlier)),
        grid=(slots,),
        in_specs=[wide, two, two, wide] + [ANYWHERE] * len(earlier),
        out_specs=[wide, two, two],
        out_shape=[
            jax.ShapeDtypeStruct((slots, extent, inner), f32),
            jax.ShapeDtypeStruct((slots, extent, 2 * STATE_DIM), f32),
            jax.ShapeDtypeStruct((slots, extent, 2 * LANES), f32),
        ],
        scratch_shapes=[pltpu.VMEM((LANES, extent), f32)],
        compiler_params=kernel_params(48),
        cost_estimate=taking(42, slots * extent),
        name="mixer_pairs",
    )(xs, rw, dl, gy, *earlier)


def back_kernel(
    inner, v_ref, halo_ref, cw_ref, hp_ref, skip_ref, rw_ref, dl_ref, gy_ref, gx_ref, grw_ref, gdl_ref, h_ref, gh_ref,
    gv_ref, gbc_ref, gp_ref, gc_ref, ghp_ref, padded, gpad,
):
    extent = gy_ref.shape[1]
    zs, _, rows, _ = v_ref.shape
    width = padded.shape[1]
    heads = inner // HEAD_DIM
    first = pl.program_id(0) == 0
    pre = conv_of(v_ref, halo_ref, cw_ref, padded)
    logistic = jax.nn.sigmoid(pre)
    slope = logistic * (1.0 + pre * (1.0 - logistic))
    xs = pre[:, :inner] * logistic[:, :inner]
    write_low = rw_ref[0, :, :STATE_DIM].astype(bf16)
    read_low = rw_ref[0, :, STATE_DIM:].astype(bf16)
    raw, step = step_sizes(v_ref, hp_ref, width, extent)
    rate = jnp.exp(hp_ref[0:1, :])
    log_sum = dl_ref[0, :, LANES:]
    gy = gy_ref[0]
    step_direct = gdl_ref[0, :, 0:LANES]
    sums = head_sums(inner)
    spread = head_spread(inner)
    last = log_sum[extent - 1 : extent, :]
    tail_decay = jnp.exp(last - log_sum)
    tail = dot_ones(tail_decay * step, spread, NN)
    grown = dot_ones(jnp.exp(log_sum), spread, NN)
    gh = gh_ref[0]
    h_in = h_ref[0]
    gh_parts, h_parts = split_parts(gh), split_parts(h_in)
    tail_in = dot(write_low, gh_parts[0], NT)
    tail_direct = tail_decay * dot_ones(xs * tail_in, sums, NN)
    tail_weight = tail_direct * step
    state_part = grown * dot(read_low, h_parts[0], NT)
    state_weight = dot_ones(gy * state_part, sums, NN)
    held = split_parts(gh * h_in)
    row_ones = jnp.ones((8, STATE_DIM), bf16)
    kept = dot_ones(dot(row_ones, held[0], NT) + dot(row_ones, held[1], NT), sums, NN)[0:1, :]
    log_grad = gdl_ref[0, :, LANES:] + state_weight - tail_weight
    end_grad = jnp.sum(tail_weight, axis=0, keepdims=True) + jnp.exp(last) * kept
    rate_arg_grad = dot(lower_ones(extent), log_grad, TN, highest) + end_grad
    step_grad = step_direct + tail_direct - rate * rate_arg_grad
    raw_grad = step_grad * jax.nn.sigmoid(raw)
    xs_grad = gx_ref[0] + tail * tail_in + skip_ref[3:4, :] * gy
    write_grad = grw_ref[0, :, :STATE_DIM] + dot_split(split_parts(tail * xs), gh_parts, NN)
    read_grad = grw_ref[0, :, STATE_DIM:] + dot_split(split_parts(grown * gy), h_parts, NN)
    valid_lane = lax.broadcasted_iota(jnp.int32, (1, LANES), 1) < heads
    rate_grad = jnp.where(valid_lane, jnp.sum(-step * rate * rate_arg_grad, axis=0, keepdims=True), 0.0)
    raw_grad = jnp.where(valid_lane, raw_grad, 0.0)
    skip_grad = jnp.sum(dot_ones(gy * xs, sums, NN), axis=0, keepdims=True)

    @pl.when(first)
    def _():
        gc_ref[...] = jnp.zeros_like(gc_ref)
        ghp_ref[...] = jnp.zeros_like(ghp_ref)

    ghp_ref[0:1, :] += rate_grad
    ghp_ref[1:2, :] += jnp.sum(raw_grad, axis=0, keepdims=True)
    ghp_ref[2:3, :] += skip_grad
    gpad[0:8, :] = jnp.zeros((8, width), f32)
    gpad[extent + 8 :, :] = jnp.zeros((8, width), f32)
    gpad[8 : extent + 8, 0:inner] = xs_grad * slope[:, 0:inner]
    gpad[8 : extent + 8, inner : inner + STATE_DIM] = write_grad * slope[:, inner : inner + STATE_DIM]
    gpad[8 : extent + 8, inner + STATE_DIM :] = read_grad * slope[:, inner + STATE_DIM :]
    back = jnp.zeros((extent, width), f32)
    before = jnp.zeros((8, width), f32)
    pre_grad = gpad[8 : extent + 8, :]
    for tap in range(CONV_WIDTH):
        ahead = CONV_WIDTH - 1 - tap
        weight = cw_ref[tap : tap + 1, :]
        back = back + weight * gpad[8 + ahead : 8 + ahead + extent, :]
        before = before + weight * gpad[ahead : 8 + ahead, :]
        gc_ref[tap : tap + 1, :] += jnp.sum(pre_grad * padded[5 + tap : 5 + tap + extent, :], axis=0, keepdims=True)
    gc_ref[CONV_WIDTH : CONV_WIDTH + 1, :] += jnp.sum(pre_grad, axis=0, keepdims=True)
    gp_ref[0] = before
    gv_ref[:, :, :, 0:inner] = back[:, :inner].astype(bf16).reshape(zs, 1, rows, inner)
    gbc_ref[...] = back[:, inner:].reshape(zs, 1, rows, width - inner)
    gv_ref[:, :, :, inner:] = raw_grad.astype(bf16).reshape(zs, 1, rows, LANES)


def mixer_back(v, halo, cw, hp, skip, rw, dl, gy, gx, grw, gdl, h_in, gh):
    zs, slots, rows, cols = v.shape
    extent = zs * rows
    inner = gy.shape[2]
    width = cw.shape[1]
    wide = pl.BlockSpec((1, extent, inner), lambda s: (s, 0, 0))
    two = pl.BlockSpec((1, extent, 2 * LANES), lambda s: (s, 0, 0))
    state = pl.BlockSpec((1, inner, STATE_DIM), lambda s: (s, 0, 0))
    return pl.pallas_call(
        functools.partial(back_kernel, inner),
        grid=(slots,),
        in_specs=[
            pl.BlockSpec((zs, 1, rows, cols), lambda s: (0, s, 0, 0)),
            pl.BlockSpec((1, 8, width), lambda s: (s, 0, 0)),
            pl.BlockSpec(cw.shape, lambda s: (0, 0)),
            pl.BlockSpec(hp.shape, lambda s: (0, 0)),
            pl.BlockSpec(skip.shape, lambda s: (0, 0)),
            two,
            two,
            wide,
            wide,
            two,
            two,
            state,
            state,
        ],
        out_specs=[
            pl.BlockSpec((zs, 1, rows, inner + LANES), lambda s: (0, s, 0, 0)),
            pl.BlockSpec((zs, 1, rows, 2 * STATE_DIM), lambda s: (0, s, 0, 0)),
            pl.BlockSpec((1, 8, width), lambda s: (s, 0, 0)),
            pl.BlockSpec((8, width), lambda s: (0, 0)),
            pl.BlockSpec((8, LANES), lambda s: (0, 0)),
        ],
        out_shape=[
            jax.ShapeDtypeStruct((zs, slots, rows, inner + LANES), bf16),
            jax.ShapeDtypeStruct((zs, slots, rows, 2 * STATE_DIM), f32),
            jax.ShapeDtypeStruct((slots, 8, width), f32),
            jax.ShapeDtypeStruct((8, width), f32),
            jax.ShapeDtypeStruct((8, LANES), f32),
        ],
        scratch_shapes=[
            pltpu.VMEM((extent + 8, width), f32),
            pltpu.VMEM((extent + 16, width), f32),
        ],
        compiler_params=kernel_params(56),
        cost_estimate=taking(18, zs * slots * rows),
        name="mixer_back",
    )(v, halo, cw, hp, skip, rw, dl, gy, gx, grw, gdl, h_in, gh)


def expert_kernel(
    n_ref, g_ref, mask_ref, router_ref, up_ref, down_ref,
    moe_ref, back_ref, logit_ref, act_ref, hid_ref, moe_sum, back_sum, gates_buf, gate_grad,
):
    pair = pl.program_id(0)
    pairs = pl.num_programs(0)
    tokens = n_ref.shape[0]
    lane = lax.broadcasted_iota(jnp.int32, (tokens, LANES), 1)
    half = up_ref.shape[3] // 2

    @pl.when(pair == 0)
    def _():
        logits = dot(n_ref[...], router_ref[...], NN)
        chosen = mask_ref[...] > 0.0
        logits = jnp.where(chosen, logits, -jnp.inf)
        powers = jnp.exp(logits - jnp.max(logits, axis=1, keepdims=True))
        gates = powers / jnp.sum(powers, axis=1, keepdims=True)
        gates_buf[...] = jnp.where(lane < EXPERTS, gates, 1.0)
        moe_sum[...] = jnp.zeros_like(moe_sum)
        back_sum[...] = jnp.zeros_like(back_sum)
        gate_grad[...] = jnp.zeros_like(gate_grad)

    depth = up_ref.shape[0] * up_ref.shape[2]
    down = down_ref[...].reshape(depth, 2 * half)
    n_val = n_ref[...]
    gates = gates_buf[...]
    act_back = dot(g_ref[...], down, NN)
    ups = [up_ref[:, member].reshape(depth, 2 * half) for member in range(2)]
    for member in range(2):
        hidden = dot(n_val, ups[member], NN)
        gate_part, up_part = hidden[:, :half], hidden[:, half:]
        logistic = jax.nn.sigmoid(gate_part)
        silu = gate_part * logistic
        act = (silu * up_part).astype(bf16).astype(f32)
        own = lane == 2 * pair + member
        gate = jnp.sum(jnp.where(own, gates, 0.0), axis=1, keepdims=True)
        part = act_back[:, member * half : (member + 1) * half]
        gate_grad[...] += jnp.where(own, jnp.sum(act * part, axis=1, keepdims=True), 0.0)
        act_ref[0, :, member * half : (member + 1) * half] = (gate * act).astype(bf16)
        part = part * gate
        first_col = 2 * member * half
        hid_ref[0, :, first_col : first_col + half] = (part * up_part * (logistic * (1.0 + gate_part * (1.0 - logistic)))).astype(bf16)
        hid_ref[0, :, first_col + half : first_col + 2 * half] = (part * silu).astype(bf16)
    moe_sum[...] += dot(act_ref[0], down, NT)
    back_sum[...] += dot(hid_ref[0], jnp.concatenate(ups, axis=1), NT)

    @pl.when(pair == pairs - 1)
    def _():
        gates_in = jnp.where(lane < EXPERTS, gates, 0.0)
        grads = gates_in * gate_grad[...]
        logit_grad = (grads - gates_in * jnp.sum(grads, axis=1, keepdims=True)).astype(bf16)
        logit_ref[...] = logit_grad
        back_ref[...] = (back_sum[...] + dot(logit_grad, router_ref[...], NT)).astype(bf16)
        moe_ref[...] = moe_sum[...].astype(bf16)


def experts(n_two, g_moe, mask, router, weights):
    tokens, width = n_two.shape
    count, blocks, rows, cols = weights.shape
    pairs = blocks // 3
    down_at = 2 * pairs
    return pl.pallas_call(
        expert_kernel,
        grid=(pairs,),
        in_specs=[
            pl.BlockSpec((tokens, width), lambda p: (0, 0)),
            pl.BlockSpec((tokens, width), lambda p: (0, 0)),
            pl.BlockSpec((tokens, LANES), lambda p: (0, 0)),
            pl.BlockSpec((width, LANES), lambda p: (0, 0)),
            pl.BlockSpec((count, 2, rows, cols), lambda p: (0, p, 0, 0)),
            pl.BlockSpec((count, 1, rows, cols), lambda p: (0, down_at + p, 0, 0)),
        ],
        out_specs=[
            pl.BlockSpec((tokens, width), lambda p: (0, 0)),
            pl.BlockSpec((tokens, width), lambda p: (0, 0)),
            pl.BlockSpec((tokens, LANES), lambda p: (0, 0)),
            pl.BlockSpec((1, tokens, cols), lambda p: (p, 0, 0)),
            pl.BlockSpec((1, tokens, 2 * cols), lambda p: (p, 0, 0)),
        ],
        out_shape=[
            jax.ShapeDtypeStruct((tokens, width), bf16),
            jax.ShapeDtypeStruct((tokens, width), bf16),
            jax.ShapeDtypeStruct((tokens, LANES), bf16),
            jax.ShapeDtypeStruct((pairs, tokens, cols), bf16),
            jax.ShapeDtypeStruct((pairs, tokens, 2 * cols), bf16),
        ],
        scratch_shapes=[
            pltpu.VMEM((tokens, width), f32),
            pltpu.VMEM((tokens, width), f32),
            pltpu.VMEM((tokens, LANES), f32),
            pltpu.VMEM((tokens, LANES), f32),
        ],
        compiler_params=kernel_params(60),
        cost_estimate=taking(72, tokens),
        name="experts",
    )(n_two, g_moe, mask, router, weights, weights)


def expert_grad_kernel(up_blocks, chunks, *refs):
    n_refs, g_refs, h_refs, a_refs = (refs[i * chunks : (i + 1) * chunks] for i in range(4))
    out_ref, turned = refs[4 * chunks :]
    block = pl.program_id(0)
    count, _, rows, cols = out_ref.shape
    tokens = n_refs[0].shape[0]

    def turn(sources):
        for at, source in enumerate(sources):
            turned[:, at * tokens : (at + 1) * tokens] = source[...].T

    def summed_over(rights):
        total = dot(turned[:, 0:tokens], rights[0][0], NN)
        for at in range(1, chunks):
            total = total + dot(turned[:, at * tokens : (at + 1) * tokens], rights[at][0], NN)
        out_ref[...] = total.astype(bf16).reshape(count, 1, rows, cols)

    @pl.when(block == 0)
    def _():
        turn(n_refs)

    @pl.when(block == up_blocks)
    def _():
        turn(g_refs)

    @pl.when(block < up_blocks)
    def _():
        summed_over(h_refs)

    @pl.when(block >= up_blocks)
    def _():
        summed_over(a_refs)


def expert_grads(n_list, g_list, hid_list, act_list, count, *earlier):
    chunks = len(n_list)
    tokens, width = n_list[0].shape
    cols = 2 * LANES
    hid_wide, act_wide = (values[0].shape[2] // cols for values in (hid_list, act_list))
    ups = hid_list[0].shape[0] * hid_wide
    downs = act_list[0].shape[0] * act_wide
    blocks = ups + downs
    whole = pl.BlockSpec((tokens, width), lambda b: (0, 0))

    def hid_at(b):
        b = jnp.minimum(b, ups - 1)
        return b // hid_wide, 0, b % hid_wide

    def act_at(b):
        b = jnp.maximum(b - ups, 0)
        return b // act_wide, 0, b % act_wide

    return pl.pallas_call(
        skipping(functools.partial(expert_grad_kernel, ups, chunks), 4 * chunks, len(earlier)),
        grid=(blocks,),
        in_specs=[whole] * (2 * chunks)
        + [pl.BlockSpec((1, tokens, cols), hid_at)] * chunks
        + [pl.BlockSpec((1, tokens, cols), act_at)] * chunks
        + [ANYWHERE] * len(earlier),
        out_specs=pl.BlockSpec((count, 1, width // count, cols), lambda b: (0, b, 0, 0)),
        out_shape=jax.ShapeDtypeStruct((count, blocks, width // count, cols), bf16),
        scratch_shapes=[pltpu.VMEM((width, chunks * tokens), bf16)],
        compiler_params=kernel_params(48),
        cost_estimate=taking(4 * blocks / 3, chunks * tokens),
        name="expert_grads",
    )(*n_list, *g_list, *hid_list, *act_list, *earlier)


def body(
    block_input,
    out_grad,
    lengths,
    routes,
    norm1_gain,
    w_zx,
    w_bc,
    w_dt,
    conv_x,
    conv_bc,
    head_params,
    gate_gain,
    w_out,
    norm2_gain,
    w_router,
    w_gu,
    w_dn,
    s_gu,
    s_dn,
):
    zs = lax.axis_size("tensor")
    pieces = lax.axis_size("dp")
    own = lax.axis_index("tensor")
    wide_index = lax.axis_index("dp")
    rows = block_input.shape[0]
    piece_rows = rows * zs
    heads = HEAD_COUNT // zs
    inner = INNER_DIM // zs
    width = inner + 2 * STATE_DIM
    shard = D_MODEL // pieces
    half = w_gu.shape[3]
    rim = CONV_WIDTH - 1
    per = SLOT_COUNT // CHUNKS
    tokens = per * rows
    chunk_ids = range(CHUNKS)

    enter_shard = jnp.concatenate(
        [w_zx[:, 1], w_bc, jnp.pad(w_dt, ((0, 0), (0, LANES - heads)))], axis=1
    )
    side_shard = jnp.concatenate(
        [w_zx[:, 0], w_out.T, jnp.pad(w_router, ((0, 0), (0, LANES - EXPERTS)))], axis=1
    )
    expert_shard = jnp.concatenate(
        [
            w_gu.reshape(EXPERTS, shard, 2 * half),
            s_gu.reshape(shard, 2, 2, half).transpose(2, 0, 1, 3).reshape(2, shard, 2 * half),
            w_dn.reshape(EXPERTS // 2, 2 * half, shard).transpose(0, 2, 1),
            s_dn.T[None],
        ],
        axis=0,
    )

    def by_slot(values):
        return jnp.transpose(values, (1, 0, 2))

    def part(values, c):
        return values[c * per : (c + 1) * per].reshape((tokens,) + values.shape[2:])

    u_slots = by_slot(block_input)
    u_low = [row_major(part(u_slots, c)) for c in chunk_ids]
    u_all = [in_order(line_gather(u_low[c])) for c in chunk_ids]
    full_enter = weight_gather(enter_shard).reshape(D_MODEL, width + LANES)
    gains = jnp.stack([norm1_gain, norm2_gain], axis=1).astype(f32)
    gains = lax.all_gather(gains, "dp", axis=0, tiled=True)
    gain_one, gain_two = gains[:, 0], gains[:, 1]
    full_side = weight_gather(side_shard).reshape(D_MODEL, 2 * inner + LANES)
    full_z, full_out, full_router = full_side[:, :inner], full_side[:, inner : 2 * inner], full_side[:, 2 * inner :]

    positions = wide_index * piece_rows + own * rows + jnp.arange(rows, dtype=jnp.int32)
    valid = (positions[None, :] < lengths[:, None]).astype(f32)[:, :, None]
    grad_slots = by_slot(out_grad).astype(f32) * valid

    conv_w = jnp.pad(jnp.concatenate([conv_x, conv_bc], axis=1), ((0, 8 - CONV_WIDTH - 1), (0, 0)))
    hp = jnp.pad(head_params, ((0, 5), (0, LANES - heads)))
    skip = jnp.pad(jnp.repeat(head_params[2], HEAD_DIM)[None], ((3, 4), (0, 0)))
    gain_row = gate_gain[None]

    hot = jnp.sum(
        (routes[..., None] == jnp.arange(LANES, dtype=jnp.int32)).astype(f32), axis=2
    )
    hot = jnp.transpose(hot.reshape(zs, rows, SLOT_COUNT, LANES), (0, 2, 1, 3))

    hot_at = by_distance(hot)

    def flat(values):
        return values.reshape((zs * tokens,) + values.shape[2:])

    def in_slots(values):
        return values.reshape((zs, per, rows) + values.shape[1:])

    u = [row_major(u_low[c].astype(f32)) for c in chunk_ids]
    valid_c = [part(valid, c) for c in chunk_ids]
    grad_c = [row_major(part(grad_slots, c)) for c in chunk_ids]
    n_one, v, z, halo, entered = [], [], [], [], []
    for c in chunk_ids:
        n_one.append(row_major(rms_scale(flat(u_all[c]).astype(f32), gain_one).astype(bf16)))
        v.append(in_slots(dot(n_one[c], full_enter, NN)))
        rim_rows = in_slots(n_one[c])[zs - 1, :, rows - rim :]
        prior = dot(passed_along(rim_rows, "dp", 1).reshape(per * rim, D_MODEL), full_enter[:, :width], NN)
        halo.append(jnp.pad(prior.reshape(per, rim, width), ((0, 0), (8 - rim, 0), (0, 0))))
    g_blocks = [line_gather(after(grad_c[c].astype(bf16), u_all[CHUNKS - 1])) for c in chunk_ids]
    for c in chunk_ids:
        entered.append(mixer_enter(v[c], halo[c], conv_w, hp, inner))
    resid, mixed_all, y_all, h_all, decay_all, inv_alls, gg_all, n_two = [], [], [], [], [], [], [], []
    for c in chunk_ids:
        xs, rw, dl, s_local = entered[c]
        yi = mixer_inner(xs, rw, dl)
        z.append(in_slots(dot(n_one[c], full_z, NN)))
        s_local = after(s_local, g_blocks[c][1], g_blocks[c][3])
        h_in, decay = states_forward((g_blocks[c][2], yi, z[c]), s_local, dl[:, piece_rows - 1, LANES : LANES + heads])
        if c == 0:
            full_expert = weight_gather(after(expert_shard, h_in))
        y, gg, squares = mixer_leave(yi, xs, rw, dl, h_in, z[c], skip, gain_row)
        product = dot(flat(gg.reshape(zs, tokens, inner)), full_out, NT).astype(bf16)
        product = product.reshape(zs, tokens, D_MODEL)
        square_sum = lax.psum(squares[:, :, 0], "tensor")
        inv_all = lax.rsqrt(square_sum / INNER_DIM + norm_eps)
        y_all.append(y)
        h_all.append(h_in)
        decay_all.append(decay)
        inv_alls.append(inv_all)
        gg_all.append(gg)

    few = tokens // HALVES
    halves = range(HALVES)

    def half_of(values, m):
        return values[m * few : (m + 1) * few]

    inv_own = lax.dynamic_slice_in_dim(inv_alls[0], own * rows, rows, 1).reshape(tokens, 1)
    mixed_own = summed(line_parts(by_distance(product))) * inv_own
    resid_own = row_major(u[0] + mixed_own)
    normed_two = row_major(rms_scale(resid_own, gain_two).astype(bf16))
    n_two_low, n_two, g_moe, masks = [], [], [], []
    for m in halves:
        low = half_of(normed_two, m)
        if m > 0:
            low = after(low, *n_two_low[m - 1][1:])
        n_two_low.append(line_gather(low))
        g_moe.append(jnp.concatenate([half_of(block, m) for block in g_blocks[0]], axis=0))
        masks.append(jnp.concatenate([half_of(part(hot_at(k), 0), m) for k in range(zs)], axis=0))
    moe_part, back_part, logit_grads, acts, hids = [], [], [], [], []
    for m in halves:
        if m > 0:
            n_two_low[m][1] = after(n_two_low[m][1], back_part[m - 1])
        n_two.append(jnp.concatenate(n_two_low[m], axis=0))
        results = experts(n_two[m], g_moe[m], masks[m], full_router, full_expert)
        moe_part.append(results[0].reshape(zs, few, D_MODEL))
        back_part.append(results[1].reshape(zs, few, D_MODEL))
        logit_grads.append(results[2])
        acts.append(results[3])
        hids.append(results[4])

    def norm_back(values, gain_vec, grads):
        return jax.vjp(rms_scale, values, gain_vec)[1](grads)

    back_blocks = []
    for m in halves:
        sent = back_part[m]
        if m > 0:
            sent = after(sent, *back_blocks[m - 1][1:])
        back_blocks.append(line_parts(lambda k: sent[k]))
    n_two_grad = jnp.concatenate([summed(blocks) for blocks in back_blocks], axis=0)
    from_norm, gain_two_grad = norm_back(resid_own, gain_two, n_two_grad)
    resid_grad = [row_major(grad_c[0] + from_norm)]
    low = resid_grad[0].astype(bf16)
    low_blocks = line_gather(low)
    gathered = in_order(low_blocks)
    expert_grad = weight_scatter(after(expert_grads(n_two, g_moe, hids, acts, pieces), gathered))
    g_mixed = [flat(gathered)]
    unmixed, scanned, pairs, toks, gate_gain_grad = [], [], [], [], 0.0
    for c in chunk_ids:
        grad = in_slots(dot(g_mixed[c], full_out, NN))
        xs, rw, dl, _ = entered[c]
        inv_all = inv_alls[c]
        y_like = jnp.transpose(y_all[c].reshape(per, zs, rows, inner), (1, 0, 2, 3))
        cross = jnp.sum(grad * gain_row * y_like * jax.nn.silu(z[c]), axis=-1)
        cross = lax.psum(jnp.transpose(cross, (1, 0, 2)).reshape(per, piece_rows), "tensor")
        tok = jnp.stack([inv_all, cross * (inv_all * inv_all * inv_all) / INNER_DIM], axis=-1)
        gy, gz, g_local, gg_grad = mixer_unmix(grad, y_all[c], z[c], rw, dl, tok, gain_row)
        toks.append(tok)
        gate_gain_grad = gate_gain_grad + gg_grad[0]
        unmixed.append((gy, gz))
        scanned.append(states_scanned(g_local, decay_all[c]))
        pairs.append(mixer_pairs(xs, rw, dl, gy))

    moe_blocks = []
    for m in halves:
        held = after(moe_part[m], *toks)
        moe_blocks.append(line_parts(lambda k: held[k]))
    sooner = [block for blocks in moe_blocks for block in blocks[1::2]]
    later = [block for blocks in moe_blocks for block in blocks[2::2]]
    router_grad = sum(dot(n_two[m], logit_grads[m], TN)[:, :EXPERTS] for m in halves)

    def rows_of(values):
        return jnp.concatenate([v.reshape(zs * tokens, -1) for v in values], axis=0)

    inv_rows = [
        jnp.transpose(inv_alls[c].reshape(per, zs, rows), (1, 0, 2)).reshape(zs * tokens, 1) for c in chunk_ids
    ]
    scaled = [(g_mixed[c].astype(f32) * inv_rows[c]).astype(bf16) for c in chunk_ids]
    n_rows = rows_of(n_one)
    gg_row, gz_row = (values.reshape(1, zs * tokens, inner) for values in (gg_all[0], unmixed[0][1]))
    side_products = expert_grads(scaled, [n_rows], [gg_row], [gz_row], pieces)

    z_backs = []
    v_grads, bc_grads, conv_grad, head_grad = [], [], 0.0, 0.0
    full_x = jnp.concatenate([full_enter[:, :inner], full_enter[:, width:]], axis=1)
    full_bc = full_enter[:, inner:width]
    full_bc = jnp.concatenate([full_bc, full_bc], axis=1)
    for c in chunk_ids:
        gy, gz = unmixed[c]
        xs, rw, dl, _ = entered[c]
        gh = exchanged(after(scanned[c], pairs[c][0], *sooner)).reshape(h_all[c].shape)
        z_backs.append(dot(gz.reshape(zs * tokens, inner), full_z, NT))
        gh = after(gh, z_backs[c], side_products, *later)
        gv, gbc, g_rim, gc, ghp = mixer_back(
            v[c], halo[c], conv_w, hp, skip, rw, dl, gy, *pairs[c], h_all[c], gh
        )
        conv_grad = conv_grad + gc
        head_grad = head_grad + ghp
        following = passed_along(g_rim[:, 8 - rim :].astype(bf16), "dp", -1).astype(f32)
        edge = gv[zs - 1, :, rows - rim :, :inner].astype(f32) + following[:, :, :inner]
        gv = lax.dynamic_update_slice(gv, edge.astype(bf16)[None], (zs - 1, 0, rows - rim, 0))
        edge = gbc[zs - 1, :, rows - rim :] + following[:, :, inner:]
        gbc = lax.dynamic_update_slice(gbc, edge[None], (zs - 1, 0, rows - rim, 0))
        v_grads.append(gv)
        bc_grads.append(jnp.concatenate(split_parts(gbc), axis=-1))
    n_parts, arrived, gain_one_grad = [], [], 0.0
    for c in chunk_ids:
        n_grad = (
            z_backs[c]
            + dot(v_grads[c].reshape(zs * tokens, inner + LANES), full_x, NT)
            + dot(bc_grads[c].reshape(zs * tokens, 4 * STATE_DIM), full_bc, NT)
        )
        every = flat(u_all[c]).astype(f32)
        scale = lax.rsqrt(jnp.mean(every * every, axis=-1, keepdims=True) + norm_eps)
        gain_one_grad = gain_one_grad + jnp.sum(n_grad * (every * scale), axis=0)
        n_parts.append(n_grad.astype(bf16))
        received = line_parts(by_distance(n_parts[c].reshape(zs, tokens, D_MODEL)))
        arrived.append(received)
    for blocks in moe_blocks:
        blocks[1] = after(blocks[1], n_parts[0])
    moe = [summed(blocks) for blocks in moe_blocks]
    moe_own = jnp.concatenate(moe, axis=0)
    output = [resid_own + moe_own]
    stat_terms = jnp.stack(
        [
            jnp.sum(valid_c[0] * output[0] * output[0]),
            jnp.sum(valid_c[0] * mixed_own * mixed_own),
            jnp.sum(valid_c[0] * moe_own * moe_own),
        ]
    )
    enter_w_grad = dot(n_rows, rows_of(v_grads), TN).astype(bf16)
    bc_w_grad = dot(n_rows, rows_of(bc_grads), TN)
    bc_w_grad = bc_w_grad[:, : 2 * STATE_DIM] + bc_w_grad[:, 2 * STATE_DIM :]
    side_grad = weight_scatter(after(side_products, expert_grad, *n_parts))

    def mixer_scatter(grads):
        return weight_scatter(after(grads.reshape(pieces, shard, -1), side_grad)).astype(f32)

    side = side_grad.astype(f32)
    fold = side.shape[0] // 2
    z_part = jnp.transpose(side[fold:], (1, 0, 2)).reshape(shard, inner)
    out_part = jnp.transpose(side[:fold], (0, 2, 1)).reshape(inner, shard)
    enter_part = mixer_scatter(enter_w_grad)
    expert_grad = expert_grad.astype(f32)
    ups, downs = EXPERTS + 2, EXPERTS // 2
    expert_outs = (
        expert_grad[:EXPERTS].reshape(EXPERTS, shard, 2, half),
        expert_grad[ups : ups + downs].transpose(0, 2, 1).reshape(EXPERTS, half, shard),
        expert_grad[EXPERTS:ups].reshape(2, shard, 2, half).transpose(1, 2, 0, 3).reshape(shard, 2, 2 * half),
        expert_grad[ups + downs].T,
    )

    def to_shares(values, dim):
        size = values.shape[dim] // (pieces * zs)
        values = jnp.moveaxis(values, dim, 0).reshape(pieces, zs, size, -1)
        return jnp.moveaxis(values, 3, 2).reshape(pieces, zs, -1)

    column = own * inner
    conv_x_full = lax.dynamic_update_slice(
        jnp.zeros((CONV_WIDTH + 1, INNER_DIM), f32), conv_grad[: CONV_WIDTH + 1, :inner], (jnp.int32(0), column)
    )
    gate_full = lax.dynamic_update_slice(jnp.zeros((INNER_DIM,), f32), gate_gain_grad, (column,))
    small = [
        (gain_one_grad, 0),
        (conv_x_full, 1),
        (conv_grad[: CONV_WIDTH + 1, inner:], 1),
        (gate_full, 0),
        (gain_two_grad, 0),
        (router_grad, 0),
    ]
    shares = [to_shares(values, dim) for values, dim in small]
    sizes = [share.shape[2] for share in shares]
    shares = jnp.concatenate(shares, axis=2)
    length = shares.shape[2]
    shares = jnp.pad(shares, ((0, 0), (0, 0), (0, -length % (8 * LANES))))
    wide_share = bc_w_grad.reshape(pieces, zs, -1, LANES)
    tile = jnp.zeros((8, LANES), f32)
    tile = tile.at[:3, :heads].set(head_grad[:3, :heads]).at[3, :3].set(stat_terms)
    tile = jnp.broadcast_to(tile, (pieces, zs) + tile.shape)
    shares = jnp.concatenate([wide_share, shares.reshape(pieces, zs, -1, LANES), tile], axis=2)
    shares = after(shares, arrived[0][1], arrived[0][2], *expert_outs)
    shares = jnp.sum(lax.all_to_all(shares, "dp", 0, 0), axis=0)
    first_sum = after(shares, arrived[0][3])
    shares = first_sum
    got = lax.all_to_all(shares, "tensor", 0, 0)
    tiles = got[:, -8:]
    shares = jnp.sum(got[:, :-8], axis=0)
    u_grad = []
    for c in chunk_ids:
        received = arrived[c]
        u_grad.append(resid_grad[c] + norm_back(u[c], gain_one, summed(received))[0])
    bc_lines = wide_share.shape[2]
    bc_grad = shares[:bc_lines].reshape(-1, 2 * STATE_DIM)
    shares = shares[bc_lines:].reshape(-1)
    ends = [sum(sizes[: k + 1]) for k in range(len(sizes))]
    took = []
    for (values, dim), size, end in zip(small, sizes, ends):
        share = shares[end - size : end]
        if values.ndim == 2:
            other = values.shape[1 - dim]
            share = share.reshape(other, size // other)
            share = share if dim == 1 else share.T
        took.append(share)
    head_sum = jnp.transpose(tiles[:, :3, :heads], (1, 0, 2)).reshape(3, HEAD_COUNT)
    stat_sum = jnp.sum(tiles[:, 3, :3], axis=0)
    stats = jnp.sqrt(stat_sum / (jnp.sum(lengths).astype(f32) * D_MODEL))

    def placed_back(values):
        whole = jnp.concatenate([value.astype(bf16).reshape(per, rows, D_MODEL) for value in values], axis=0)
        return jnp.transpose(whole, (1, 0, 2))

    return (
        placed_back(output),
        placed_back(u_grad),
        took[0],
        jnp.stack([z_part, enter_part[:, :inner]], axis=1),
        bc_grad,
        enter_part[:, inner : inner + heads],
        took[1],
        took[2],
        head_sum,
        took[3],
        out_part,
        took[4],
        took[5],
        *expert_outs,
        stats,
    )


def solution(mesh):
    both = ("dp", "tensor")
    placed = (
        P(both, None, None),
        P(both, None, None),
        P(),
        P("dp", None, None),
        P("dp"),
        P("dp", None, "tensor"),
        P("dp", None),
        P("dp", "tensor"),
        P(None, "tensor"),
        P(),
        P(None, "tensor"),
        P("tensor"),
        P("tensor", "dp"),
        P("dp"),
        P("dp", None),
        P(None, "dp", None, "tensor"),
        P(None, "tensor", "dp"),
        P("dp", None, "tensor"),
        P("tensor", "dp"),
    )
    return jax.shard_map(
        body,
        mesh=mesh,
        in_specs=placed,
        out_specs=(
            P(both, None, None),
            P(both, None, None),
            P(both),
            P("dp", None, "tensor"),
            P(both, None),
            P("dp", "tensor"),
            P(None, both),
            P(None, both),
            P(),
            P(both),
            P("tensor", "dp"),
            P(both),
            P(both, None),
            P(None, "dp", None, "tensor"),
            P(None, "tensor", "dp"),
            P("dp", None, "tensor"),
            P("tensor", "dp"),
            P(),
        ),
        check_vma=False,
    )
```
